256 devices in a mesh: dp: 32 (over y, z), pipe: 8 (over x, core).
Axes of the slice: x: 4, y: 4, z: 8, core: 2. Of those that a mesh axis runs over, the one named last changes fastest.
Arguments:
- mel_tiles: bfloat16 [1024, 4, 320], P('dp'), may hold values from -6 to 6
- utt_ids: int32 [1024], P('dp'), may hold values from 0 to 2
- tile_lengths: int32 [1024], P('dp'), may hold values from 1 to 4, as said below
- dest_shard: int32 [1024], P('dp'), may hold values from 0 to 31, as said below
- dest_slot: int32 [1024], P('dp'), may hold values from 0 to 31, as said below
- subsample_weight: bfloat16 [320, 1536], replicated, may hold values from -0.3125 to 0.3125
- mixing_weight: bfloat16 [8, 1536, 1536], P('pipe', 'dp'), may hold values from -0.15625 to 0.15625
- gate_weight: bfloat16 [8, 1536, 1536], P('pipe', 'dp'), may hold values from -0.15625 to 0.15625
- conv_taps: float32 [8, 31, 1536], P('pipe'), may hold values from -1 to 1
- norm_gain: float32 [8, 1536], P('pipe'), may hold values from 0.5 to 1.5
- out_cot: bfloat16 [4096, 1536], P('dp'), may hold values from -0.09375 to 0.09375
Outputs:
- weight_grad: float32 [8, 1536, 1536], P('pipe', 'dp')
- gate_grad: float32 [8, 1536, 1536], P('pipe', 'dp')
- taps_grad: float32 [8, 31, 1536], P('pipe')
- gain_grad: float32 [8, 1536], P('pipe')
The draws below stay inside these ranges and needn't reach their ends.
Inputs may be any that keep to these rules, and one draw needn't show every extreme that they name: `tile_lengths`: every loader shard's first tile has 4 live frames. `dest_shard`: each loader shard sends exactly 32 // 32 of its tiles to every data shard. `dest_slot`: the tiles that go to one data shard fill its slots, each slot once.
All inputs are finite; a program needn't handle non-finite values.
Results may differ from the reference program's by a relative error of at most 0.033.
Values may be sent and summed in bfloat16 or wider, within the bound.
A program may use at most 192 MiB of HBM per device.

```python
import jax
import jax.numpy as jnp
from jax import lax

D = 1536
MEL = 80
STACK = 4
TAPS = 31
MB = 2
UTT_IDS = 3
TSUB = 4
SLOTS = 32
SECTIONS = 8
FR_DEV = 128
FR_MB = 64
N_DP = 32


def packing_plan(key):
    key_send = jax.random.fold_in(key, 11)
    key_recv = jax.random.fold_in(key, 23)
    key_length = jax.random.fold_in(key, 37)
    key_label = jax.random.fold_in(key, 41)
    per_peer = SLOTS // N_DP
    shuffle = jax.vmap(lambda subkey: jax.random.permutation(subkey, SLOTS))(jax.random.split(key_send, N_DP))
    senders = jnp.arange(N_DP, dtype=jnp.int32)
    dest_rows = (senders[:, None] + shuffle // per_peer) % N_DP
    arrival = jax.vmap(lambda subkey: jax.random.permutation(subkey, SLOTS))(jax.random.split(key_recv, N_DP))
    slot_rows = arrival[dest_rows, shuffle]
    lowest = max(1, TSUB // 4)
    length_rows = jax.random.randint(key_length, (N_DP, SLOTS), lowest, TSUB + 1).at[:, 0].set(TSUB)
    label_rows = jax.random.randint(key_label, (N_DP, SLOTS), 0, UTT_IDS)
    return (label_rows.reshape(-1).astype(jnp.int32), length_rows.reshape(-1).astype(jnp.int32), dest_rows.reshape(-1).astype(jnp.int32), slot_rows.reshape(-1).astype(jnp.int32))


def draw_utt_ids(key, part):
    return packing_plan(key)[0]


def draw_tile_lengths(key, part):
    return packing_plan(key)[1]


def draw_dest_shard(key, part):
    return packing_plan(key)[2]


def draw_dest_slot(key, part):
    return packing_plan(key)[3]


def steps_of(rng, extent, pieces, low, largest):
    level, own = 1.0, jax.random.fold_in(rng, 6)
    for dim, blocks in pieces:
        heights = jnp.exp(jax.random.uniform(jax.random.fold_in(own, dim), (blocks,), jnp.float32, low / len(pieces), largest / len(pieces)))
        level = level * jnp.repeat(heights, extent[dim] // blocks).reshape([-1 if axis == dim else 1 for axis in range(len(extent))])
    return level


def gaussian(key, extent, deviation, bound, pieces=(), kind=jnp.bfloat16):
    drawn = jax.random.normal(key, extent, jnp.float32) * deviation
    if len(pieces) > 0:
        drawn = steps_of(key, extent, pieces, -0.22, 0.18) * drawn
    return jnp.clip(drawn, min=-bound, max=bound).astype(kind)


def setup_inputs(seed: int = 0) -> dict:
    key_list = jax.random.split(jax.random.key(seed), 12)
    mel_tiles = gaussian(key_list[0], (N_DP * SLOTS, TSUB, STACK * MEL), 1.0, 6.0, ((0, 32),))
    utt_ids = draw_utt_ids(jax.random.fold_in(key_list[11], 71), 0)
    tile_lengths = draw_tile_lengths(jax.random.fold_in(key_list[11], 71), 0)
    dest_shard = draw_dest_shard(jax.random.fold_in(key_list[11], 71), 0)
    dest_slot = draw_dest_slot(jax.random.fold_in(key_list[11], 71), 0)
    subsample_weight = gaussian(key_list[5], (STACK * MEL, D), (STACK * MEL) ** -0.5, 0.3125)
    mixing_weight = gaussian(key_list[6], (SECTIONS, D, D), D ** -0.5, 0.15625, ((0, 8), (1, 32)))
    gate_weight = gaussian(key_list[7], (SECTIONS, D, D), D ** -0.5, 0.15625, ((0, 8), (1, 32)))
    conv_taps = gaussian(key_list[8], (SECTIONS, TAPS, D), TAPS ** -0.5, 1.0, ((0, 8),), jnp.float32)
    norm_gain = jnp.clip(1.0 + 0.1 * jax.random.normal(key_list[9], (SECTIONS, D), jnp.float32), 0.5, 1.5)
    out_cot = gaussian(key_list[10], (N_DP * FR_DEV, D), ((N_DP * FR_DEV) ** -0.5), 0.09375, ((0, 32),))
    return dict(mel_tiles=mel_tiles, utt_ids=utt_ids, tile_lengths=tile_lengths, dest_shard=dest_shard, dest_slot=dest_slot, subsample_weight=subsample_weight, mixing_weight=mixing_weight, gate_weight=gate_weight, conv_taps=conv_taps, norm_gain=norm_gain, out_cot=out_cot)


EPSILON = 1e-05

def normalize(inputs, gain):
    center = lax.optimization_barrier(jnp.mean(inputs, axis=-1, keepdims=True))
    shifted = inputs - center
    spread = lax.optimization_barrier(jnp.mean(shifted * shifted, axis=-1, keepdims=True))
    return shifted * lax.rsqrt(spread + EPSILON) * gain

def mix_time(value, gate, inputs, taps, frame_mask, labels):
    projected = value * jax.nn.sigmoid(gate)
    reach = taps.shape[0] // 2
    length = projected.shape[1]
    masked = projected * frame_mask[..., None]
    padded = jnp.pad(masked, ((0, 0), (reach, reach), (0, 0)))
    padded_labels = jnp.pad(labels, ((0, 0), (reach, reach)), constant_values=-1)
    total = jnp.zeros(projected.shape, jnp.float32)
    for offset in range(taps.shape[0]):
        same = (padded_labels[:, offset:offset + length] == labels).astype(jnp.float32)
        total = total + taps[offset] * padded[:, offset:offset + length] * same[..., None]
    conv_out = total * frame_mask[..., None]
    return inputs + conv_out * jax.nn.sigmoid(conv_out)

def shard_sum(normed, grads):
    width = normed.shape[1]

    def add_shard(index, total):
        start = index * FR_DEV
        rows_normed = lax.dynamic_slice_in_dim(normed, start, FR_DEV, 0)
        rows_grads = lax.dynamic_slice_in_dim(grads, start, FR_DEV, 0)
        partial_sum = lax.dot_general(rows_normed, rows_grads, (((0,), (0,)), ((), ())), preferred_element_type=jnp.float32)
        rounded = lax.optimization_barrier(partial_sum.astype(jnp.bfloat16))
        return total + rounded.astype(jnp.float32)
    return lax.fori_loop(0, N_DP, add_shard, jnp.zeros((width, grads.shape[1]), jnp.float32))

def reference(mel_tiles, utt_ids, tile_lengths, dest_shard, dest_slot, subsample_weight, mixing_weight, gate_weight, conv_taps, norm_gain, out_cot):
    total_slots = N_DP * SLOTS
    batch_rows = N_DP * MB
    target = (dest_shard * SLOTS + dest_slot).astype(jnp.int32)
    placed = jnp.zeros_like(mel_tiles).at[target].set(mel_tiles)
    slot_label = jnp.zeros((total_slots,), jnp.int32).at[target].set(utt_ids)
    slot_length = jnp.zeros((total_slots,), jnp.int32).at[target].set(tile_lengths)
    frame_ids = jnp.arange(TSUB, dtype=jnp.int32)
    frame_mask = (frame_ids[None, :] < slot_length[:, None]).astype(jnp.float32).reshape(batch_rows, FR_MB)
    labels = jnp.broadcast_to(slot_label[:, None], (total_slots, TSUB)).reshape(batch_rows, FR_MB)
    stacked = placed.reshape(total_slots * TSUB, STACK * MEL)
    current = jnp.dot(stacked, subsample_weight, preferred_element_type=jnp.float32).astype(jnp.bfloat16)

    def block_only(value_in, gate_in, input_in, taps_in):
        return mix_time(value_in, gate_in, input_in, taps_in, frame_mask, labels)

    def shaped(array):
        return array.reshape(batch_rows, FR_MB, D)
    saved = []
    for section in range(SECTIONS):
        saved.append(current)
        as_float = current.astype(jnp.float32)
        normed = normalize(as_float, norm_gain[section]).astype(jnp.bfloat16)
        value = jnp.dot(normed, mixing_weight[section], preferred_element_type=jnp.float32)
        gate = jnp.dot(normed, gate_weight[section], preferred_element_type=jnp.float32)
        output = block_only(shaped(value), shaped(gate), shaped(as_float), conv_taps[section])
        current = output.reshape(-1, D).astype(jnp.bfloat16)
    cotangent = out_cot.astype(jnp.float32)
    weight_list, gate_list, taps_list, gain_list = ([], [], [], [])
    for section in reversed(range(SECTIONS)):
        as_float = saved[section].astype(jnp.float32)
        normed = normalize(as_float, norm_gain[section]).astype(jnp.bfloat16)
        value = jnp.dot(normed, mixing_weight[section], preferred_element_type=jnp.float32)
        gate = jnp.dot(normed, gate_weight[section], preferred_element_type=jnp.float32)
        _, block_back = jax.vjp(block_only, shaped(value), shaped(gate), shaped(as_float), conv_taps[section])
        grad_value, grad_gate, grad_res, grad_taps = block_back(shaped(cotangent))
        grad_value = grad_value.reshape(-1, D).astype(jnp.bfloat16)
        grad_gate = grad_gate.reshape(-1, D).astype(jnp.bfloat16)
        both = shard_sum(normed, jnp.concatenate([grad_value, grad_gate], axis=1))
        weight_list.append(both[:, :D])
        gate_list.append(both[:, D:])
        grad_normed = lax.dot_general(grad_value, mixing_weight[section], (((1,), (1,)), ((), ())), preferred_element_type=jnp.float32)
        grad_normed = grad_normed + lax.dot_general(grad_gate, gate_weight[section], (((1,), (1,)), ((), ())), preferred_element_type=jnp.float32)
        _, norm_back = jax.vjp(normalize, as_float, norm_gain[section])
        grad_input, grad_gain = norm_back(grad_normed)
        taps_list.append(grad_taps)
        gain_list.append(grad_gain)
        passed = lax.optimization_barrier((grad_res.reshape(-1, D) + grad_input).astype(jnp.bfloat16))
        cotangent = passed.astype(jnp.float32)
    return (jnp.stack(weight_list[::-1]), jnp.stack(gate_list[::-1]), jnp.stack(taps_list[::-1]), jnp.stack(gain_list[::-1]))
```

```python
import functools

import jax
import jax.numpy as jnp
from jax import lax
from jax.experimental import pallas as pl
from jax.experimental.pallas import tpu as pltpu
from jax.sharding import PartitionSpec as P

PHYS = {32: (4, 8), 8: (2, 4), 4: (2, 2)}
CORES = 2
EPSILON = 1e-05
F32 = jnp.float32
BF16 = jnp.bfloat16
VMEM_LIMIT = 60 * 1024 * 1024


def rcopy(src, dst, send_sem, recv_sem, device):
    return pltpu.make_async_remote_copy(
        src_ref=src,
        dst_ref=dst,
        send_sem=send_sem,
        recv_sem=recv_sem,
        device_id=device,
        device_id_type=pl.DeviceIdType.MESH,
    )


def kernel(
    dims,
    slabs,
    mixing,
    gating,
    tg,
    gain8,
    sub,
    cot,
    o_mix,
    o_gate,
    o_taps,
    W,
    TAPS,
    GAIN,
    T1,
    T2,
    TF,
    EA,
    CP,
    MASK,
    X,
    NT,
    NS,
    GL,
    SP,
    V,
    SG,
    CV,
    GC,
    PF,
    GO,
    GS,
    MS,
    MR,
    G,
    RA,
    RB,
    FS,
    FR,
    TT,
    TS,
    TY,
    TYR,
    TZR,
    TX,
    TXR,
    TO1,
    TO2,
    lw_s,
    xw_s,
    xw_r,
    tg_s,
    tg_r,
    tl_s,
    tl_r,
    ag_s,
    ag_r,
    rs_s,
    rs_r,
    sw_s,
    sw_r,
    st_s,
    st_r,
    xf_s,
    xf_r,
    xb_s,
    xb_r,
    sn_s,
    sn_r,
    sg_s,
    sg_r,
    fin_s,
    fin_r,
    tt_s,
    tt_r,
):
    NX, NY, NZ = dims["X"], dims["Y"], dims["Z"]
    D, R, FRM, TSUB, J, KT = (dims[k] for k in ("D", "R", "F", "TSUB", "J", "TAPS"))
    DX = D // NX
    ND = NY * NZ
    SECT = 2 * NX
    reach = KT // 2
    lanes_x = DX // 128

    dpi = lax.axis_index("dp")
    pipe = lax.axis_index("pipe")
    x, c = pipe // CORES, pipe % CORES
    y, z = dpi // NZ, dpi % NZ

    def dev(yy=None, zz=None, xx=None, cc=None):
        yy = y if yy is None else yy
        zz = z if zz is None else zz
        xx = x if xx is None else xx
        cc = c if cc is None else cc
        return {"dp": yy * NZ + zz, "pipe": xx * CORES + cc}

    sib = dev(cc=1 - c)
    xs_ = [(j, (x + j) % NX) for j in range(1, NX)]
    ys_ = [(j, (y + j) % NY) for j in range(1, NY)]
    zs_ = [(j, (z + j) % NZ) for j in range(1, NZ)]

    def half(h):
        return pl.ds(h * DX, DX)

    def cols(b):
        return pl.ds(pl.multiple_of(b * DX, 128), DX)

    barrier = pltpu.get_barrier_semaphore()
    peers = [sib]
    peers += [dev(xx=xx) for _, xx in xs_]
    peers += [dev(yy=yy) for _, yy in ys_]
    peers += [dev(zz=zz) for _, zz in zs_]
    for peer in peers:
        pl.semaphore_signal(barrier, inc=1, device_id=peer, device_id_type=pl.DeviceIdType.MESH)
    pl.semaphore_wait(barrier, len(peers))

    for j, xx in xs_:
        rcopy(mixing.at[0, :, cols(xx)], W.at[c, x, y, z, :, half(0)], xw_s.at[j], xw_r.at[x], dev(xx=xx)).start()
        rcopy(gating.at[0, :, cols(xx)], W.at[c, x, y, z, :, half(1)], xw_s.at[j], xw_r.at[x], dev(xx=xx)).start()
    own_copies = [
        pltpu.make_async_copy(mixing.at[0, :, cols(x)], W.at[c, x, y, z, :, half(0)], lw_s.at[0]),
        pltpu.make_async_copy(gating.at[0, :, cols(x)], W.at[c, x, y, z, :, half(1)], lw_s.at[1]),
    ]
    for copy in own_copies:
        copy.start()

    for j, yy in ys_:
        rcopy(slabs.at[pl.ds(yy * NZ, NZ)], T1.at[y], tl_s.at[0, j], tl_r.at[0, y], dev(yy=yy)).start()
    T1[y] = slabs[pl.ds(y * NZ, NZ)]

    for j, xx in xs_:
        rcopy(tg.at[:, cols(xx)], TAPS.at[c, x], tg_s.at[0, j], tg_r.at[0, x], dev(xx=xx)).start()
        rcopy(gain8, GAIN.at[c, x], tg_s.at[1, j], tg_r.at[1, x], dev(xx=xx)).start()
    TAPS[c, x] = tg[:, cols(x)]
    GAIN[c, x] = gain8[...]

    for j, yy in ys_:
        rcopy(slabs.at[pl.ds(yy * NZ, NZ)], T1.at[yy], tl_s.at[0, j], tl_r.at[0, yy], dev(yy=yy)).wait()
    for j, zz in zs_:
        rcopy(T1.at[:, zz], T2.at[z], tl_s.at[1, j], tl_r.at[1, z], dev(zz=zz)).start()
    T2[z] = T1[:, z]

    for copy in own_copies:
        copy.wait()
    for j, xx in xs_:
        rcopy(W.at[c, x, y, z], W.at[c, xx, y, z], xw_s.at[j], xw_r.at[xx], dev(xx=xx)).wait()

    def gather(cc):
        n1, n2 = (NY, NZ) if cc == 0 else (NZ, NY)
        me1, me2 = (y, z) if cc == 0 else (z, y)

        def block1(i, j, h):
            return W.at[cc, i, j, z, :, half(h)] if cc == 0 else W.at[cc, i, y, j, :, half(h)]

        def block2(i, j, h):
            return W.at[cc, i, :, j, :, half(h)] if cc == 0 else W.at[cc, i, j, :, :, half(h)]

        def neighbour(phase, me, sgn, n):
            pos = (me + sgn + n) % n
            along_y = (phase == 0) == (cc == 0)
            return dev(yy=pos) if along_y else dev(zz=pos)

        def ring(phase, n, me, block, forward):
            def start(t, i):
                for h, sgn in ((0, 1), (1, -1)):
                    b = (me - sgn * (t - 1) + 2 * n) % n
                    rcopy(
                        block(i, b, h), block(i, b, h), ag_s.at[phase, i, h], ag_r.at[phase, i, h, t - 1],
                        neighbour(phase, me, sgn, n),
                    ).start()
                    if forward:
                        rcopy(block(i, b, h), block(i, b, h), sw_s.at[i], sw_r.at[i], sib).start()

            def arrived(t, i):
                for h, sgn in ((0, 1), (1, -1)):
                    b = (me - sgn * t + 2 * n) % n
                    rcopy(
                        block(i, b, h), block(i, b, h), ag_s.at[phase, i, h], ag_r.at[phase, i, h, t - 1],
                        neighbour(phase, me, sgn, n),
                    ).wait_recv()

            def loop(f):
                lax.fori_loop(0, NX, lambda i, _: (f(i), 0)[1], 0)

            loop(lambda i: start(1, i))

            def step(t, _):
                def one(i):
                    arrived(t, i)
                    start(t + 1, i)

                loop(one)
                return 0

            lax.fori_loop(1, n - 1, step, 0)

            def last(i):
                arrived(n - 1, i)
                if forward:
                    for h, sgn in ((0, 1), (1, -1)):
                        b = (me - sgn * (n - 1) + 2 * n) % n
                        rcopy(block(i, b, h), block(i, b, h), sw_s.at[i], sw_r.at[i], sib).start()

            loop(last)

        ring(0, n1, me1, block1, False)
        ring(1, n2, me2, block2, True)

        def drain(i, _):
            for h in range(2):
                if cc == 0:
                    first, second = W.at[cc, i, 0 : n1 - 1, 0, :, half(h)], W.at[cc, i, :, 0 : n2 - 1, :, half(h)]
                else:
                    first, second = W.at[cc, i, 0, 0 : n1 - 1, :, half(h)], W.at[cc, i, 0 : n2 - 1, :, :, half(h)]
                rcopy(first, first, ag_s.at[0, i, h], ag_r.at[0, i, h, 0], sib).wait_send()
                rcopy(second, second, ag_s.at[1, i, h], ag_r.at[1, i, h, 0], sib).wait_send()
            return 0

        lax.fori_loop(0, NX, drain, 0)

    for cc in range(CORES):
        pl.when(c == cc)(functools.partial(gather, cc))

    for j, xx in xs_:
        rcopy(tg.at[:, cols(xx)], TAPS.at[c, xx], tg_s.at[0, j], tg_r.at[0, xx], dev(xx=xx)).wait()
        rcopy(gain8, GAIN.at[c, xx], tg_s.at[1, j], tg_r.at[1, xx], dev(xx=xx)).wait()
    taps_out = rcopy(TAPS.at[c], TAPS.at[c], st_s.at[0], st_r.at[0], sib)
    gain_out = rcopy(GAIN.at[c], GAIN.at[c], st_s.at[1], st_r.at[1], sib)
    taps_out.start()
    gain_out.start()

    for j, zz in zs_:
        rcopy(T1.at[:, zz], T2.at[zz], tl_s.at[1, j], tl_r.at[1, zz], dev(zz=zz)).wait()
    TF[...] = T2[...].astype(F32).reshape(TF.shape)
    for f in range(TSUB):
        for j in range(J):
            EA[f * ND : (f + 1) * ND, j * 128 : (j + 1) * 128] = TF[:, f * J + j, :]
    embedded = jnp.dot(EA[...].astype(BF16), sub[...], preferred_element_type=F32).astype(BF16)
    detail = TF[:, TSUB * J, :]
    rows = TSUB * ND
    detail_rows = jnp.concatenate([detail] * TSUB, axis=0)
    slot, label, length = (detail_rows[:, k : k + 1] for k in range(3))
    frame_in_tile = (lax.broadcasted_iota(jnp.int32, (rows, 1), 0) // ND).astype(F32)
    time_lane = lax.broadcasted_iota(jnp.int32, (rows, FRM), 1)
    first_slot = (c * (FRM // TSUB)).astype(F32)
    pick = (slot - first_slot == (time_lane // TSUB).astype(F32)) & (
        frame_in_tile == (time_lane % TSUB).astype(F32)
    )
    pick = pick.astype(F32).astype(BF16)
    placed = lax.dot_general(pick, embedded, (((0,), (0,)), ((), ())), preferred_element_type=F32).astype(BF16)
    for b in range(NX):
        X[0, b] = placed[:, b * DX : (b + 1) * DX]
    code_rows = jnp.broadcast_to(jnp.where(frame_in_tile < length, label, -1.0), (rows, 128)).astype(BF16)
    code = lax.dot_general(pick, code_rows, (((0,), (0,)), ((), ())), preferred_element_type=F32)
    CP[...] = jnp.full(CP.shape, -2.0, F32)
    CP[16 : 16 + FRM] = code
    for k in range(KT):
        start = 16 - reach + k
        MASK[k] = jnp.where((CP[start : start + FRM] == code) & (code >= 0.0), 1.0, 0.0)
    edge = jnp.zeros((16, DX), F32)
    SP[0:16] = edge
    SP[16 + FRM :] = edge

    def clear(s, _):
        GL[s, 0:16] = edge
        GL[s, 16 + FRM :] = edge
        return 0

    lax.fori_loop(0, SECT, clear, 0)

    rcopy(TAPS.at[1 - c], TAPS.at[1 - c], st_s.at[0], st_r.at[0], sib).wait_recv()
    rcopy(GAIN.at[1 - c], GAIN.at[1 - c], st_s.at[1], st_r.at[1], sib).wait_recv()

    def statistics(s):
        blocks = [X[s, b].astype(F32) for b in range(NX)]
        mean = sum(jnp.sum(v, axis=1, keepdims=True) for v in blocks) * (1.0 / D)
        shifted = [v - mean for v in blocks]
        spread = sum(jnp.sum(v * v, axis=1, keepdims=True) for v in shifted) * (1.0 / D)
        return mean, shifted, lax.rsqrt(spread + EPSILON)

    def weight(s):
        return W[s % 2, s // 2].reshape(D, 2 * DX)

    def forward(s, _):
        @pl.when(s % 2 != c)
        def _():
            there = W.at[1 - c, s // 2]
            rcopy(there, there, sw_s.at[s // 2], sw_r.at[s // 2], sib).wait_recv()

        @pl.when(s > 0)
        def _():
            for j, xx in xs_:
                rcopy(X.at[s, x], X.at[s, xx], xf_s.at[s, j], xf_r.at[s, xx], dev(xx=xx)).wait()

        _, shifted, inverse = statistics(s)
        for b in range(NX):
            gain = GAIN[s % 2, s // 2, 0:1, b * DX : (b + 1) * DX]
            NT[s, :, b * DX : (b + 1) * DX] = (shifted[b] * inverse * gain).astype(BF16)

        @pl.when(s % 2 != c)
        def _():
            rcopy(NT.at[s], NS.at[s // 2], sn_s.at[s // 2], sn_r.at[s // 2], sib).start()

        both = jnp.dot(NT[s], weight(s), preferred_element_type=F32)
        value, gate = both[:, :DX], both[:, DX:]
        sig = jax.nn.sigmoid(gate)
        V[s] = value
        SG[s] = sig
        GL[s, 16 : 16 + FRM] = value * sig
        for tile in range(lanes_x):
            lane = slice(tile * 128, (tile + 1) * 128)
            total = jnp.zeros((FRM, 128), F32)
            for k in range(KT):
                start = 16 - reach + k
                total = total + GL[s, start : start + FRM, lane] * MASK[k] * TAPS[s % 2, s // 2, k : k + 1, lane]
            CV[s, :, lane] = total
        conv = CV[s]
        result = X[s, x].astype(F32) + conv * jax.nn.sigmoid(conv)

        @pl.when(s < SECT - 1)
        def _():
            X[s + 1, x] = result.astype(BF16)
            for j, xx in xs_:
                rcopy(X.at[s + 1, x], X.at[s + 1, x], xf_s.at[s + 1, j], xf_r.at[s + 1, x], dev(xx=xx)).start()

        return 0

    lax.fori_loop(0, SECT, forward, 0)

    GC[...] = cot[pl.ds(pl.multiple_of(c * FRM, 16), FRM), cols(x)].astype(F32)

    def weight_gradient(s):
        i = s // 2
        rcopy(NT.at[s], NS.at[i], sn_s.at[i], sn_r.at[i], sib).wait_recv()
        rcopy(GO.at[s], GS.at[i], sg_s.at[i], sg_r.at[i], sib).wait_recv()
        grads = jnp.concatenate([GO[s], GS[i]], axis=0)
        width = D // NY
        for part in range(NY):
            lane = slice(part * width, (part + 1) * width)
            normed = jnp.concatenate([NT[s, :, lane], NS[i, :, lane]], axis=0)
            product = lax.dot_general(normed, grads, (((0,), (0,)), ((), ())), preferred_element_type=F32)
            G[i, part] = product.astype(BF16).reshape(NZ, R, 2 * DX)

    def backward(step, _):
        s = SECT - 1 - step
        par, i = s % 2, s // 2
        conv = CV[s]
        sig_conv = jax.nn.sigmoid(conv)
        seed = GC[...]
        SP[16 : 16 + FRM] = seed * (sig_conv * (1.0 + conv * (1.0 - sig_conv)))
        for tile in range(lanes_x):
            lane = slice(tile * 128, (tile + 1) * 128)
            total = jnp.zeros((FRM, 128), F32)
            for k in range(KT):
                start = 16 - reach + k
                total = total + SP[start : start + FRM, lane] * MASK[k] * TAPS[par, i, KT - 1 - k : KT - k, lane]
            grad_value = total * SG[s, :, lane]
            grad_gate = grad_value * V[s, :, lane] * (1.0 - SG[s, :, lane])
            GO[s, :, lane] = grad_value.astype(BF16)
            GO[s, :, DX + tile * 128 : DX + (tile + 1) * 128] = grad_gate.astype(BF16)

        @pl.when(par != c)
        def _():
            rcopy(GO.at[s], GS.at[i], sg_s.at[i], sg_r.at[i], sib).start()

        partial = lax.dot_general(GO[s], weight(s), (((1,), (1,)), ((), ())), preferred_element_type=F32)
        mean, shifted, inverse = statistics(s)
        sum_a = jnp.zeros((FRM, 1), F32)
        sum_b = jnp.zeros((FRM, 1), F32)
        for b in range(NX):
            block = partial[:, b * DX : (b + 1) * DX]
            PF[b] = block
            MS[s, b, :, :DX] = block.astype(BF16)
            scaled = block * GAIN[par, i, 0:1, b * DX : (b + 1) * DX]
            sum_a = sum_a + jnp.sum(scaled, axis=1, keepdims=True)
            sum_b = sum_b + jnp.sum(scaled * (shifted[b] * inverse), axis=1, keepdims=True)
        lane_id = lax.broadcasted_iota(jnp.int32, (FRM, 128), 1)
        high_a, high_b = sum_a.astype(BF16).astype(F32), sum_b.astype(BF16).astype(F32)
        packed = jnp.where(lane_id == 0, high_a, 0.0)
        packed = jnp.where(lane_id == 1, sum_a - high_a, packed)
        packed = jnp.where(lane_id == 2, high_b, packed)
        packed = jnp.where(lane_id == 3, sum_b - high_b, packed).astype(BF16)
        for b in range(NX):
            MS[s, b, :, DX:] = packed
        for j, xx in xs_:
            rcopy(MS.at[s, xx], MR.at[s, x], xb_s.at[s, j], xb_r.at[s, x], dev(xx=xx)).start()

        for tile in range(lanes_x):
            lane = slice(tile * 128, (tile + 1) * 128)
            spread = SP[16 : 16 + FRM, lane]
            for k in range(KT):
                start = 16 - reach + k
                TT[s, k : k + 1, lane] = jnp.sum(
                    spread * GL[s, start : start + FRM, lane] * MASK[k], axis=0, keepdims=True
                )

        @pl.when((par != c) & (step > 0))
        def _():
            weight_gradient(s + 1)

        for j, xx in xs_:
            rcopy(MS.at[s, xx], MR.at[s, xx], xb_s.at[s, j], xb_r.at[s, xx], dev(xx=xx)).wait()
        total = PF[x]
        for j, xx in xs_:
            total = total + MR[s, xx, :, :DX].astype(F32)
            packed = MR[s, xx, :, DX:].astype(F32)
            sum_a = sum_a + packed[:, 0:1] + packed[:, 1:2]
            sum_b = sum_b + packed[:, 2:3] + packed[:, 3:4]
        xhat = (X[s, x].astype(F32) - mean) * inverse
        TT[s, KT : KT + 1, :] = jnp.sum(total * xhat, axis=0, keepdims=True)
        gain = GAIN[par, i, 0:1, cols(x)]
        grad_in = inverse * (total * gain - sum_a * (1.0 / D) - xhat * (sum_b * (1.0 / D)))
        GC[...] = (GC[...] + grad_in).astype(BF16).astype(F32)
        return 0

    lax.fori_loop(0, SECT, backward, 0)

    pl.when(c == 0)(lambda: weight_gradient(0))

    for i in range(NX):
        rcopy(TT.at[2 * i + 1 - c], TS.at[i], tt_s.at[4, i], tt_r.at[4, i], sib).start()

    def scatter(cc):
        n1, n2 = (NY, NZ) if cc == 0 else (NZ, NY)
        me1, me2 = (y, z) if cc == 0 else (z, y)
        dirs = ((0, 1), (1, -1))

        def region(i, j, h):
            return G.at[i, :, j, :, half(h)] if cc == 0 else G.at[i, j, :, :, half(h)]

        def region_value(i, j, h):
            return G[i, :, j, :, half(h)] if cc == 0 else G[i, j, :, :, half(h)]

        def neighbour(phase, sgn):
            me, n = (me2, n2) if phase == 0 else (me1, n1)
            pos = (me + sgn + n) % n
            along_z = (phase == 0) == (cc == 0)
            return dev(zz=pos) if along_z else dev(yy=pos)

        def slot_a(i, h, t):
            return RA.at[i, h, pl.ds((t - 1) * n1, n1)]

        def send_a(i, h, sgn, src, t):
            return rcopy(src, slot_a(i, h, t), rs_s.at[0, i, h], rs_r.at[0, i, h, t - 1], neighbour(0, sgn))

        def loop(f):
            lax.fori_loop(0, NX, lambda i, _: (f(i), 0)[1], 0)

        def first_a(i):
            for h, sgn in dirs:
                send_a(i, h, sgn, region(i, (me2 - sgn + n2) % n2, h), 1).start()

        loop(first_a)

        def add_a(i, h, sgn, t):
            send_a(i, h, sgn, slot_a(i, h, t), t).wait_recv()
            target = (me2 - sgn * (t + 1) + 2 * n2) % n2
            held = pl.ds((t - 1) * n1, n1)
            RA[i, h, held] = (RA[i, h, held].astype(F32) + region_value(i, target, h).astype(F32)).astype(BF16)

        def step_a(t, _):
            def one(i):
                for h, sgn in dirs:
                    add_a(i, h, sgn, t)
                    send_a(i, h, sgn, slot_a(i, h, t), t + 1).start()

            loop(one)
            return 0

        lax.fori_loop(1, n2 - 1, step_a, 0)

        base = (n2 - 2) * n1

        def send_b(i, h, sgn, src, t):
            return rcopy(src, RB.at[i, h, t - 1], rs_s.at[1, i, h], rs_r.at[1, i, h, t - 1], neighbour(1, sgn))

        def last_a(i):
            for h, sgn in dirs:
                add_a(i, h, sgn, n2 - 1)
                send_b(i, h, sgn, RA.at[i, h, base + (me1 - sgn + n1) % n1], 1).start()

        loop(last_a)

        def add_b(i, h, sgn, t):
            send_b(i, h, sgn, RB.at[i, h, t - 1], t).wait_recv()
            target = (me1 - sgn * (t + 1) + 2 * n1) % n1
            return RB[i, h, t - 1].astype(F32) + RA[i, h, base + target].astype(F32)

        def step_b(t, _):
            def one(i):
                for h, sgn in dirs:
                    RB[i, h, t - 1] = add_b(i, h, sgn, t).astype(BF16)
                    send_b(i, h, sgn, RB.at[i, h, t - 1], t + 1).start()

            loop(one)
            return 0

        lax.fori_loop(1, n1 - 1, step_b, 0)

        def last_b(i):
            for h, sgn in dirs:
                FS[i, :, half(h)] = add_b(i, h, sgn, n1 - 1).astype(BF16)

        loop(last_b)

        def drain(i, _):
            for h in range(2):
                sent_a, sent_b = RA.at[i, h, 0 : (n2 - 1) * n1], RB.at[i, h, 0 : n1 - 1]
                rcopy(sent_a, sent_a, rs_s.at[0, i, h], rs_r.at[0, i, h, 0], sib).wait_send()
                rcopy(sent_b, sent_b, rs_s.at[1, i, h], rs_r.at[1, i, h, 0], sib).wait_send()
            return 0

        lax.fori_loop(0, NX, drain, 0)

    for cc in range(CORES):
        pl.when(c == cc)(functools.partial(scatter, cc))

    for j, xx in xs_:
        rcopy(FS.at[xx], FR.at[x], fin_s.at[j], fin_r.at[x], dev(xx=xx)).start()
    FR[x] = FS[x]

    for i in range(NX):
        rcopy(TT.at[2 * i + 1 - c], TS.at[i], tt_s.at[4, i], tt_r.at[4, i], sib).wait()
    TY[...] = jnp.zeros(TY.shape, F32)
    for i in range(NX):
        summed = TT[2 * i + c] + TS[i]
        for r in range(KT + 1):
            TY[r // NZ, r % NZ, i : i + 1, :] = summed[r : r + 1]
    for j, yy in ys_:
        rcopy(TY.at[yy], TYR.at[y], tt_s.at[0, j], tt_r.at[0, y], dev(yy=yy)).start()
    TYR[y] = TY[y]
    for j, yy in ys_:
        rcopy(TY.at[yy], TYR.at[yy], tt_s.at[0, j], tt_r.at[0, yy], dev(yy=yy)).wait()
    TY[y] = sum(TYR[k] for k in range(NY))
    for j, zz in zs_:
        rcopy(TY.at[y, zz], TZR.at[z], tt_s.at[1, j], tt_r.at[1, z], dev(zz=zz)).start()
    TZR[z] = TY[y, z]
    for j, zz in zs_:
        rcopy(TY.at[y, zz], TZR.at[zz], tt_s.at[1, j], tt_r.at[1, zz], dev(zz=zz)).wait()
    TX[...] = sum(TZR[k] for k in range(NZ))
    for j, xx in xs_:
        rcopy(TX, TXR.at[x], tt_s.at[2, j], tt_r.at[2, x], dev(xx=xx)).start()
    TXR[x] = TX[...]
    for j, xx in xs_:
        rcopy(TX, TXR.at[xx], tt_s.at[2, j], tt_r.at[2, xx], dev(xx=xx)).wait()
    TO1[z] = jnp.zeros(TO1.shape[1:], F32)
    mine = lax.broadcasted_iota(jnp.int32, (8, DX), 0) == x
    for b in range(NX):
        row = jnp.sum(jnp.where(mine, TXR[b], 0.0), axis=0, keepdims=True)
        for tile in range(lanes_x):
            k = b * lanes_x + tile
            TO1[z, k : k + 1, :] = row[:, tile * 128 : (tile + 1) * 128]
    for j, zz in zs_:
        rcopy(TO1.at[z], TO1.at[z], tt_s.at[3, j], tt_r.at[3, z], dev(zz=zz)).start()
    for j, zz in zs_:
        rcopy(TO1.at[z], TO1.at[zz], tt_s.at[3, j], tt_r.at[3, zz], dev(zz=zz)).wait()
    for j, yy in ys_:
        rcopy(TO1, TO2.at[y], tt_s.at[5, j], tt_r.at[5, y], dev(yy=yy)).start()
    TO2[y] = TO1[...]
    for j, yy in ys_:
        rcopy(TO1, TO2.at[yy], tt_s.at[5, j], tt_r.at[5, yy], dev(yy=yy)).wait()
    o_taps[...] = TO2[...].reshape(o_taps.shape)

    for j, xx in xs_:
        rcopy(FS.at[xx], FR.at[xx], fin_s.at[j], fin_r.at[xx], dev(xx=xx)).wait()
    for b in range(NX):
        o_mix[0, :, b * DX : (b + 1) * DX] = FR[b, :, :DX].astype(F32)
        o_gate[0, :, b * DX : (b + 1) * DX] = FR[b, :, DX:].astype(F32)

    taps_out.wait_send()
    gain_out.wait_send()

    def drain(i, _):
        there = W.at[c, i]
        rcopy(there, there, sw_s.at[i], sw_r.at[i], sib).wait_send()
        rcopy(NT.at[0], NS.at[i], sn_s.at[i], sn_r.at[i], sib).wait_send()
        rcopy(GO.at[0], GS.at[i], sg_s.at[i], sg_r.at[i], sib).wait_send()
        return 0

    lax.fori_loop(0, NX, drain, 0)


def body(
    mel_tiles,
    utt_ids,
    tile_lengths,
    dest_shard,
    dest_slot,
    subsample_weight,
    mixing_weight,
    gate_weight,
    conv_taps,
    norm_gain,
    out_cot,
):
    ND = lax.axis_size("dp")
    SECT = lax.axis_size("pipe")
    NX = SECT // CORES
    NY, NZ = PHYS[ND]
    tiles, TSUB, feats = mel_tiles.shape
    D = subsample_weight.shape[1]
    KT = conv_taps.shape[1]
    R = mixing_weight.shape[1]
    FRM = tiles * TSUB // 2
    J = -(-feats // 128)
    DX = D // NX
    SR = -(-(TSUB * J + 1) // 16) * 16
    dims = dict(X=NX, Y=NY, Z=NZ, D=D, R=R, F=FRM, TSUB=TSUB, J=J, TAPS=KT)

    details = jnp.stack([dest_slot, utt_ids, tile_lengths], axis=1).astype(BF16)
    flat = jnp.concatenate(
        [
            jnp.pad(mel_tiles, ((0, 0), (0, 0), (0, J * 128 - feats))).reshape(tiles, TSUB * J * 128),
            jnp.pad(details, ((0, 0), (0, 125 + (SR - TSUB * J - 1) * 128))),
        ],
        axis=1,
    )
    order = (dest_shard[None, :] == jnp.arange(ND, dtype=jnp.int32)[:, None]).astype(BF16)
    slabs = jnp.dot(order, flat, preferred_element_type=F32).astype(BF16).reshape(ND, SR, 128)
    tg = jnp.concatenate([conv_taps[0], norm_gain], axis=0)
    gain8 = jnp.broadcast_to(norm_gain, (8, D))
    sub = jnp.pad(subsample_weight, ((0, J * 128 - feats), (0, 0)))
    OR = -(-(D // 128) // 8) * 8
    NR = max(NY, NZ) - 1

    def vm(shape, kind=F32):
        return pltpu.VMEM(shape, kind)

    def sems(*shape):
        return pltpu.SemaphoreType.DMA(shape)

    scratch = [
        vm((2, NX, NY, NZ, R, 2 * DX), BF16),
        vm((2, NX, KT + 1, DX)),
        vm((2, NX, 8, D)),
        vm((NY, NZ, SR, 128), BF16),
        vm((NZ, NY, SR, 128), BF16),
        vm((ND, SR, 128)),
        vm((TSUB * ND, J * 128)),
        vm((FRM + 32, 128)),
        vm((KT, FRM, 128)),
        vm((SECT, NX, FRM, DX), BF16),
        vm((SECT, FRM, D), BF16),
        vm((NX, FRM, D), BF16),
        vm((SECT, FRM + 32, DX)),
        vm((FRM + 32, DX)),
        vm((SECT, FRM, DX)),
        vm((SECT, FRM, DX)),
        vm((SECT, FRM, DX)),
        vm((FRM, DX)),
        vm((NX, FRM, DX)),
        vm((SECT, FRM, 2 * DX), BF16),
        vm((NX, FRM, 2 * DX), BF16),
        vm((SECT, NX, FRM, DX + 128), BF16),
        vm((SECT, NX, FRM, DX + 128), BF16),
        vm((NX, NY, NZ, R, 2 * DX), BF16),
        vm((NX, 2, max((NZ - 1) * NY, (NY - 1) * NZ), R, DX), BF16),
        vm((NX, 2, NR, R, DX), BF16),
        vm((NX, R, 2 * DX), BF16),
        vm((NX, R, 2 * DX), BF16),
        vm((SECT, KT + 1, DX)),
        vm((NX, KT + 1, DX)),
        vm((NY, NZ, 8, DX)),
        vm((NY, NZ, 8, DX)),
        vm((NZ, 8, DX)),
        vm((8, DX)),
        vm((NX, 8, DX)),
        vm((NZ, OR, 128)),
        vm((NY, NZ, OR, 128)),
        sems(2),
        sems(NX),
        sems(NX),
        sems(2, NX),
        sems(2, NX),
        sems(2, max(NY, NZ)),
        sems(2, max(NY, NZ)),
        sems(2, NX, 2),
        sems(2, NX, 2, NR),
        sems(2, NX, 2),
        sems(2, NX, 2, NR),
        sems(NX),
        sems(NX),
        sems(2),
        sems(2),
        sems(SECT, NX),
        sems(SECT, NX),
        sems(SECT, NX),
        sems(SECT, NX),
        sems(NX),
        sems(NX),
        sems(NX),
        sems(NX),
        sems(NX),
        sems(NX),
        sems(6, max(NX, NY, NZ)),
        sems(6, max(NX, NY, NZ)),
    ]
    in_vmem = pl.BlockSpec(memory_space=pltpu.VMEM)
    in_any = pl.BlockSpec(memory_space=pl.ANY)
    mix, gate, taps = pl.pallas_call(
        functools.partial(kernel, dims),
        out_shape=(
            jax.ShapeDtypeStruct((1, R, D), F32),
            jax.ShapeDtypeStruct((1, R, D), F32),
            jax.ShapeDtypeStruct((ND, OR, 128), F32),
        ),
        in_specs=[in_vmem, in_any, in_any, in_vmem, in_vmem, in_vmem, in_vmem],
        out_specs=(in_vmem, in_vmem, in_vmem),
        scratch_shapes=scratch,
        compiler_params=pltpu.CompilerParams(
            collective_id=0, has_side_effects=True, vmem_limit_bytes=VMEM_LIMIT
        ),
    )(slabs, mixing_weight, gate_weight, tg, gain8, sub, out_cot)
    rows = taps[:, : D // 128].reshape(ND, D)
    return mix, gate, rows[None, :KT], rows[KT:]


def solution(mesh):
    in_specs = (
        P("dp", None, None),
        P("dp"),
        P("dp"),
        P("dp"),
        P("dp"),
        P(),
        P("pipe", "dp", None),
        P("pipe", "dp", None),
        P("pipe", None, None),
        P("pipe", None),
        P("dp", None),
    )
    out_specs = (
        P("pipe", "dp", None),
        P("pipe", "dp", None),
        P("pipe", None, None),
        P("pipe", None),
    )
    return jax.shard_map(body, mesh=mesh, in_specs=in_specs, out_specs=out_specs, check_vma=False)
```

```python
import functools

import jax
import jax.numpy as jnp
from jax import lax
from jax.experimental import pallas as pl
from jax.experimental.pallas import tpu as pltpu
from jax.sharding import PartitionSpec as P

PHYS = {32: (4, 8), 8: (2, 4), 4: (2, 2)}
CORES = 2
EPSILON = 1e-05
F32 = jnp.float32
BF16 = jnp.bfloat16
VMEM_LIMIT = 60 * 1024 * 1024


def rcopy(src, dst, send_sem, recv_sem, device):
    return pltpu.make_async_remote_copy(
        src_ref=src,
        dst_ref=dst,
        send_sem=send_sem,
        recv_sem=recv_sem,
        device_id=device,
        device_id_type=pl.DeviceIdType.MESH,
    )


def kernel(
    dims,
    slabs,
    mixing,
    gating,
    tg,
    gain8,
    sub,
    cot,
    o_mix,
    o_gate,
    o_taps,
    W,
    TAPS,
    GAIN,
    T1,
    T2,
    TF,
    EA,
    CP,
    MASK,
    X,
    NT,
    NS,
    GL,
    SP,
    V,
    SG,
    CV,
    GC,
    CT,
    PF,
    XH,
    GO,
    GS,
    MS,
    MR,
    MT,
    G,
    RA,
    RB,
    FS,
    FR,
    TT,
    TS,
    TY,
    TYR,
    TZR,
    TX,
    TXR,
    TO1,
    TO2,
    lw_s,
    xw_s,
    xw_r,
    tg_s,
    tg_r,
    tl_s,
    tl_r,
    p1_s,
    p1_r,
    p2_s,
    p2_r,
    ra_s,
    ra_r,
    rb_s,
    rb_r,
    sw_s,
    sw_r,
    st_s,
    st_r,
    xf_s,
    xf_r,
    xb_s,
    xb_r,
    xt_s,
    xt_r,
    sn_s,
    sn_r,
    sg_s,
    sg_r,
    fin_s,
    fin_r,
    tt_s,
    tt_r,
):
    NX, NY, NZ = dims["X"], dims["Y"], dims["Z"]
    D, R, FRM, TSUB, J, KT = (dims[k] for k in ("D", "R", "F", "TSUB", "J", "TAPS"))
    DX = D // NX
    ND = NY * NZ
    SECT = 2 * NX
    reach = KT // 2
    lanes_x = DX // 128

    dpi = lax.axis_index("dp")
    pipe = lax.axis_index("pipe")
    x, c = pipe // CORES, pipe % CORES
    y, z = dpi // NZ, dpi % NZ

    def dev(yy=None, zz=None, xx=None, cc=None):
        yy = y if yy is None else yy
        zz = z if zz is None else zz
        xx = x if xx is None else xx
        cc = c if cc is None else cc
        return {"dp": yy * NZ + zz, "pipe": xx * CORES + cc}

    sib = dev(cc=1 - c)
    xs_ = [(j, (x + j) % NX) for j in range(1, NX)]
    far_first = sorted(xs_, key=lambda item: -min(item[0], NX - item[0]))
    ys_ = [(j, (y + j) % NY) for j in range(1, NY)]
    zs_ = [(j, (z + j) % NZ) for j in range(1, NZ)]

    def half(h):
        return pl.ds(h * DX, DX)

    def cols(b):
        return pl.ds(pl.multiple_of(b * DX, 128), DX)

    barrier = pltpu.get_barrier_semaphore()
    peers = [sib]
    peers += [dev(xx=xx) for _, xx in xs_]
    peers += [dev(yy=yy) for _, yy in ys_]
    peers += [dev(zz=zz) for _, zz in zs_]
    for peer in peers:
        pl.semaphore_signal(barrier, inc=1, device_id=peer, device_id_type=pl.DeviceIdType.MESH)
    pl.semaphore_wait(barrier, len(peers))

    for j, xx in xs_:
        rcopy(mixing.at[0, :, cols(xx)], W.at[c, x, y, z, :, half(0)], xw_s.at[j], xw_r.at[x], dev(xx=xx)).start()
        rcopy(gating.at[0, :, cols(xx)], W.at[c, x, y, z, :, half(1)], xw_s.at[j], xw_r.at[x], dev(xx=xx)).start()
    own_copies = [
        pltpu.make_async_copy(sub, G.at[0, 0 : NX // 2], lw_s.at[2]),
        pltpu.make_async_copy(cot.at[pl.ds(pl.multiple_of(c * FRM, 16), FRM), cols(x)], CT, lw_s.at[3]),
        pltpu.make_async_copy(mixing.at[0, :, cols(x)], W.at[c, x, y, z, :, half(0)], lw_s.at[0]),
        pltpu.make_async_copy(gating.at[0, :, cols(x)], W.at[c, x, y, z, :, half(1)], lw_s.at[1]),
    ]
    for copy in own_copies:
        copy.start()

    for j, yy in ys_:
        rcopy(slabs.at[pl.ds(yy * NZ, NZ)], T1.at[y], tl_s.at[0, j], tl_r.at[0, y], dev(yy=yy)).start()
    T1[y] = slabs[pl.ds(y * NZ, NZ)]

    for j, xx in xs_:
        rcopy(tg.at[:, cols(xx)], TAPS.at[c, x], tg_s.at[0, j], tg_r.at[0, x], dev(xx=xx)).start()
        rcopy(gain8, GAIN.at[c, x], tg_s.at[1, j], tg_r.at[1, x], dev(xx=xx)).start()
    TAPS[c, x] = tg[:, cols(x)]
    GAIN[c, x] = gain8[...]

    for j, yy in ys_:
        rcopy(slabs.at[pl.ds(yy * NZ, NZ)], T1.at[yy], tl_s.at[0, j], tl_r.at[0, yy], dev(yy=yy)).wait()
    for j, zz in zs_:
        rcopy(T1.at[:, zz], T2.at[z], tl_s.at[1, j], tl_r.at[1, z], dev(zz=zz)).start()
    T2[z] = T1[:, z]

    for copy in own_copies:
        copy.wait()
    for j, xx in xs_:
        rcopy(W.at[c, x, y, z], W.at[c, xx, y, z], xw_s.at[j], xw_r.at[xx], dev(xx=xx)).wait()

    dirs = ((0, 1), (1, -1))

    class Rings:
        def __init__(self, cc):
            self.cc = cc
            self.n1, self.n2 = (NY, NZ) if cc == 0 else (NZ, NY)
            self.me1, self.me2 = (y, z) if cc == 0 else (z, y)
            self.h1, self.h2 = self.n1 // 2, self.n2 // 2
            self.m = self.n1 // 2

        def to(self, ring, sgn):
            me, n = (self.me1, self.n1) if ring == 1 else (self.me2, self.n2)
            pos = (me + sgn + n) % n
            return dev(yy=pos) if (ring == 1) == (self.cc == 0) else dev(zz=pos)

        def near(self, u, d):
            return u == d

    def at(e):
        return 1 + e // 2, e % 2

    class Gather(Rings):
        def block1(self, i, b, u):
            return W.at[0, i, b, z, :, half(u)] if self.cc == 0 else W.at[1, i, y, b, :, half(u)]

        def block2(self, i, b, u):
            part = pl.ds(u * self.m, self.m)
            return W.at[0, i, part, b] if self.cc == 0 else W.at[1, i, b, part]

        def step(self, ring, t, u, i):
            n, me, last, block, send, recv = (
                (self.n1, self.me1, self.h1, self.block1, p1_s, p1_r)
                if ring == 1
                else (self.n2, self.me2, self.h2, self.block2, p2_s, p2_r)
            )
            for d, sgn in dirs:
                held = block(i, (me - sgn * t + 2 * n) % n, u)

                def copy(k):
                    return rcopy(held, held, send.at[i, d, u], recv.at[i, d, u, k], self.to(ring, sgn))

                def arrive():
                    copy(t - 1).wait_recv()
                    if ring == 2:
                        rcopy(held, held, sw_s.at[i], sw_r.at[i], sib).start()

                if isinstance(t, int) and t == 0:
                    if ring == 2 and d == 0:
                        rcopy(held, held, sw_s.at[i], sw_r.at[i], sib).start()
                    if last > 1 or self.near(u, d):
                        copy(0).start()
                    continue
                if self.near(u, d):
                    pl.when(t <= last)(arrive)
                    pl.when(t < last)(lambda: copy(t).start())
                else:
                    pl.when(t < last)(arrive)
                    pl.when(t < last - 1)(lambda: copy(t).start())

        def begin(self, ring, i):
            for u in range(2):
                self.step(ring, 0, u, i)

        def drain(self):
            def one(i, _):
                for u in range(2):
                    for d in range(2):
                        far = 0 if self.near(u, d) else 1
                        k1, k2 = self.h1 - far, self.h2 - far
                        part = pl.ds(0, self.m)
                        if k1 > 0:
                            sent = W.at[0, i, 0:k1, 0, :, half(u)] if self.cc == 0 else W.at[1, i, 0, 0:k1, :, half(u)]
                            rcopy(sent, sent, p1_s.at[i, d, u], p1_r.at[i, d, u, 0], sib).wait_send()
                        if k2 > 0:
                            sent = W.at[0, i, part, 0:k2] if self.cc == 0 else W.at[1, i, 0:k2, part]
                            rcopy(sent, sent, p2_s.at[i, d, u], p2_r.at[i, d, u, 0], sib).wait_send()
                return 0

            lax.fori_loop(0, NX, one, 0)

    gathers = [Gather(cc) for cc in range(CORES)]
    most = max(NY, NZ)

    def each(rings, f):
        for cc in range(CORES):
            pl.when(c == cc)(functools.partial(f, rings[cc]))

    def begin(g):
        g.begin(1, 0)
        for e in range(2 * g.h1):
            g.step(1, *at(e), 0)
        g.begin(2, 0)
        for i in range(1, NX):
            g.begin(1, i)

    def go_on(low, high, g):
        for e in range(low, high):
            if e < 2 * g.h2:
                g.step(2, *at(e), 0)
            if e < 2 * g.h1:
                for i in range(1, NX):
                    g.step(1, *at(e), i)
            if e == 2 * g.h1 - 1 and NX > 1:
                g.begin(2, 1)

    each(gathers, begin)

    for j, xx in xs_:
        rcopy(tg.at[:, cols(xx)], TAPS.at[c, xx], tg_s.at[0, j], tg_r.at[0, xx], dev(xx=xx)).wait()
        rcopy(gain8, GAIN.at[c, xx], tg_s.at[1, j], tg_r.at[1, xx], dev(xx=xx)).wait()
    taps_out = rcopy(TAPS.at[c], TAPS.at[c], st_s.at[0], st_r.at[0], sib)
    gain_out = rcopy(GAIN.at[c], GAIN.at[c], st_s.at[1], st_r.at[1], sib)
    taps_out.start()
    gain_out.start()

    for j, zz in zs_:
        rcopy(T1.at[:, zz], T2.at[zz], tl_s.at[1, j], tl_r.at[1, zz], dev(zz=zz)).wait()
    TF[...] = T2[...].astype(F32).reshape(TF.shape)
    for f in range(TSUB):
        for j in range(J):
            EA[f * ND : (f + 1) * ND, j * 128 : (j + 1) * 128] = TF[:, f * J + j, :]

    each(gathers, functools.partial(go_on, 0, 1))
    stacked = EA[...].astype(BF16)
    embedded = [
        jnp.dot(stacked, G[0, k].reshape(J * 128, 2 * DX), preferred_element_type=F32).astype(BF16)
        for k in range(NX // 2)
    ]
    embedded = jnp.concatenate(embedded, axis=1)
    detail = TF[:, TSUB * J, :]
    rows = TSUB * ND
    detail_rows = jnp.concatenate([detail] * TSUB, axis=0)
    slot, label, length = (detail_rows[:, k : k + 1] for k in range(3))
    frame_in_tile = (lax.broadcasted_iota(jnp.int32, (rows, 1), 0) // ND).astype(F32)
    time_lane = lax.broadcasted_iota(jnp.int32, (rows, FRM), 1)
    first_slot = (c * (FRM // TSUB)).astype(F32)
    pick = (slot - first_slot == (time_lane // TSUB).astype(F32)) & (
        frame_in_tile == (time_lane % TSUB).astype(F32)
    )
    pick = pick.astype(F32).astype(BF16)
    placed = lax.dot_general(pick, embedded, (((0,), (0,)), ((), ())), preferred_element_type=F32).astype(BF16)
    for b in range(NX):
        X[0, b] = placed[:, b * DX : (b + 1) * DX]
    each(gathers, functools.partial(go_on, 1, 3))

    code_rows = jnp.broadcast_to(jnp.where(frame_in_tile < length, label, -1.0), (rows, 128)).astype(BF16)
    code = lax.dot_general(pick, code_rows, (((0,), (0,)), ((), ())), preferred_element_type=F32)
    CP[...] = jnp.full(CP.shape, -2.0, F32)
    CP[16 : 16 + FRM] = code
    for k in range(KT):
        start = 16 - reach + k
        MASK[k] = jnp.where((CP[start : start + FRM] == code) & (code >= 0.0), 1.0, 0.0)
    edge = jnp.zeros((16, DX), F32)
    SP[0:16] = edge
    SP[16 + FRM :] = edge

    def clear(s, _):
        GL[s, 0:16] = edge
        GL[s, 16 + FRM :] = edge
        return 0

    lax.fori_loop(0, SECT, clear, 0)
    each(gathers, functools.partial(go_on, 3, most))

    rcopy(TAPS.at[1 - c], TAPS.at[1 - c], st_s.at[0], st_r.at[0], sib).wait_recv()
    rcopy(GAIN.at[1 - c], GAIN.at[1 - c], st_s.at[1], st_r.at[1], sib).wait_recv()

    def pump(s, q):
        pair = s // 2 + 1

        def one(g):
            if g.cc == 0:
                t, u, e = 1 + (s % 2) * 2 + q // 2, q % 2, (s % 2) * 4 + q
            elif q % 2 == 0:
                t, u, e = 1 + s % 2, q // 2, (s % 2) * 2 + q // 2
            else:
                return
            pl.when((pair < NX) & (t <= g.h2))(lambda: g.step(2, t, u, pair))
            pl.when((pair + 1 < NX) & (e == max(2 * g.h2 - 3, 0)))(lambda: g.begin(2, pair + 1))

        each(gathers, one)

    def statistics(s):
        blocks = [X[s, b].astype(F32) for b in range(NX)]
        mean = sum(jnp.sum(v, axis=1, keepdims=True) for v in blocks) * (1.0 / D)
        shifted = [v - mean for v in blocks]
        spread = sum(jnp.sum(v * v, axis=1, keepdims=True) for v in shifted) * (1.0 / D)
        return mean, shifted, lax.rsqrt(spread + EPSILON)

    def weight(s):
        return W[s % 2, s // 2].reshape(D, 2 * DX)

    def forward(s, _):
        @pl.when(s % 2 != c)
        def _():
            there = W.at[1 - c, s // 2]
            rcopy(there, there, sw_s.at[s // 2], sw_r.at[s // 2], sib).wait_recv()

        @pl.when(s > 0)
        def _():
            for j, xx in xs_:
                rcopy(X.at[s, x], X.at[s, xx], xf_s.at[s, j], xf_r.at[s, xx], dev(xx=xx)).wait()

        _, shifted, inverse = statistics(s)
        for b in range(NX):
            gain = GAIN[s % 2, s // 2, 0:1, b * DX : (b + 1) * DX]
            NT[s, :, b * DX : (b + 1) * DX] = (shifted[b] * inverse * gain).astype(BF16)

        @pl.when(s % 2 != c)
        def _():
            rcopy(NT.at[s], NS.at[s // 2], sn_s.at[s // 2], sn_r.at[s // 2], sib).start()

        pump(s, 0)
        both = jnp.dot(NT[s], weight(s), preferred_element_type=F32)
        value, gate = both[:, :DX], both[:, DX:]
        sig = jax.nn.sigmoid(gate)
        V[s] = value
        SG[s] = sig
        GL[s, 16 : 16 + FRM] = value * sig
        pump(s, 1)
        for tile in range(lanes_x):
            if tile == lanes_x // 2:
                pump(s, 2)
            lane = slice(tile * 128, (tile + 1) * 128)
            conv = jnp.zeros((FRM, 128), F32)
            for k in range(KT):
                start = 16 - reach + k
                conv = conv + GL[s, start : start + FRM, lane] * MASK[k] * TAPS[s % 2, s // 2, k : k + 1, lane]
            CV[s, :, lane] = conv

            @pl.when(s < SECT - 1)
            def _():
                result = X[s, x, :, lane].astype(F32) + conv * jax.nn.sigmoid(conv)
                X[s + 1, x, :, lane] = result.astype(BF16)
                piece = X.at[s + 1, x, :, lane]
                for j, xx in far_first:
                    rcopy(piece, piece, xf_s.at[s + 1, j], xf_r.at[s + 1, x], dev(xx=xx)).start()

        pump(s, 3)
        return 0

    lax.fori_loop(0, SECT, forward, 0)

    GC[...] = CT[...].astype(F32)

    def weight_gradient(s):
        i = s // 2
        rcopy(NT.at[s], NS.at[i], sn_s.at[i], sn_r.at[i], sib).wait_recv()
        rcopy(GO.at[s], GS.at[i], sg_s.at[i], sg_r.at[i], sib).wait_recv()
        grads = jnp.concatenate([GO[s], GS[i]], axis=0)
        width = D // NY
        for part in range(NY):
            lane = slice(part * width, (part + 1) * width)
            normed = jnp.concatenate([NT[s, :, lane], NS[i, :, lane]], axis=0)
            product = lax.dot_general(normed, grads, (((0,), (0,)), ((), ())), preferred_element_type=F32)
            G[i, part] = product.astype(BF16).reshape(NZ, R, 2 * DX)

    class Scatter(Rings):
        def own2(self, i, b, u):
            part = pl.ds(u * self.m, self.m)
            return G.at[i, part, b] if self.cc == 0 else G.at[i, b, part]

        def own1(self, i, b, u):
            return RA.at[i, 0, (self.h2 - 1) * self.n1 + b, :, half(u)]

        def held2(self, i, d, t, u):
            return RA.at[i, d, pl.ds((t - 1) * self.n1 + u * self.m, self.m)]

        def held1(self, i, d, t, u):
            return RB.at[i, d, t - 1, :, half(u)]

        def step(self, ring, t, u, i):
            n, me, last, own, held, send, recv = (
                (self.n1, self.me1, self.h1, self.own1, self.held1, rb_s, rb_r)
                if ring == 1
                else (self.n2, self.me2, self.h2, self.own2, self.held2, ra_s, ra_r)
            )
            for d, sgn in dirs:
                mine = own(i, (me + sgn * (last - t) + 2 * n) % n, u)
                near = self.near(u, d)

                def onward(src):
                    return rcopy(src, held(i, d, t + 1, u), send.at[i, d, u], recv.at[i, d, u, t], self.to(ring, sgn))

                if isinstance(t, int) and t == 0:
                    if near:
                        onward(mine).start()
                    continue

                def arrive():
                    there = held(i, d, t, u)
                    rcopy(there, there, send.at[i, d, u], recv.at[i, d, u, t - 1], self.to(ring, sgn)).wait_recv()

                    @pl.when(t < last)
                    def _():
                        there[...] = (there[...].astype(F32) + mine[...].astype(F32)).astype(BF16)
                        onward(there).start()

                if near:
                    arrive()
                else:
                    pl.when((t == 1) & (t < last))(lambda: onward(mine).start())
                    pl.when(t > 1)(arrive)

            @pl.when(t == last)
            def _():
                total = own(i, me, u)[...].astype(F32)
                for d in range(2):
                    if last > 1 or self.near(u, d):
                        total = total + held(i, d, last, u)[...].astype(F32)
                if ring == 1:
                    FS[i, :, half(u)] = total.astype(BF16)
                else:
                    held(i, 0, last, u)[...] = total.astype(BF16)

        def begin(self, ring, i):
            for u in range(2):
                self.step(ring, 0, u, i)

        def drain(self):
            def one(i, _):
                for u in range(2):
                    for d in range(2):
                        far = 0 if self.near(u, d) else 1
                        k1, k2 = self.h1 - far, self.h2 - far
                        if k1 > 0:
                            sent = RB.at[i, d, 0:k1, :, half(u)]
                            rcopy(sent, sent, rb_s.at[i, d, u], rb_r.at[i, d, u, 0], sib).wait_send()
                        if k2 > 0:
                            sent = RA.at[i, d, 0 : k2 * self.m]
                            rcopy(sent, sent, ra_s.at[i, d, u], ra_r.at[i, d, u, 0], sib).wait_send()
                return 0

            lax.fori_loop(0, NX, one, 0)

    scatters = [Scatter(cc) for cc in range(CORES)]

    def pump_back(s, q):
        k = s // 2

        def one(g):
            if g.cc == 0:
                odd = {0: (5, 2), 1: (6, 2), 2: (7, 2), 3: (0, 1)}[q]
                even = (1 + q, 1)
            else:
                odd = {0: (0, 1), 2: (1, 1)}.get(q)
                even = {0: (2, 1), 2: (3, 1)}.get(q)
            for parity, what in ((1, odd), (0, even)):
                if what is not None and what[0] < 2 * g.h2:
                    e, ahead = what
                    pl.when((s % 2 == parity) & (k + ahead < NX))(lambda: g.step(2, *at(e), k + ahead))

        each(scatters, one)

    def backward(step, _):
        s = SECT - 1 - step
        par, i = s % 2, s // 2
        conv = CV[s]
        sig_conv = jax.nn.sigmoid(conv)
        seed = GC[...]
        SP[16 : 16 + FRM] = seed * (sig_conv * (1.0 + conv * (1.0 - sig_conv)))
        for tile in range(lanes_x):
            lane = slice(tile * 128, (tile + 1) * 128)
            total = jnp.zeros((FRM, 128), F32)
            for k in range(KT):
                start = 16 - reach + k
                total = total + SP[start : start + FRM, lane] * MASK[k] * TAPS[par, i, KT - 1 - k : KT - k, lane]
            grad_value = total * SG[s, :, lane]
            grad_gate = grad_value * V[s, :, lane] * (1.0 - SG[s, :, lane])
            GO[s, :, lane] = grad_value.astype(BF16)
            GO[s, :, DX + tile * 128 : DX + (tile + 1) * 128] = grad_gate.astype(BF16)

        @pl.when(par != c)
        def _():
            rcopy(GO.at[s], GS.at[i], sg_s.at[i], sg_r.at[i], sib).start()

        pump_back(s, 0)
        mean, shifted, inverse = statistics(s)
        for b in range(NX):
            XH[b] = shifted[b] * inverse
        sum_a = jnp.zeros((FRM, 1), F32)
        sum_b = jnp.zeros((FRM, 1), F32)
        per = NY // NX
        for j, xx in far_first + [(0, x)]:
            rows_w = W[par, i, pl.ds(xx * per, per)].reshape(DX, 2 * DX)
            block = lax.dot_general(GO[s], rows_w, (((1,), (1,)), ((), ())), preferred_element_type=F32)
            if j == 0:
                PF[...] = block
            else:
                MS[xx] = block.astype(BF16)
                rcopy(MS.at[xx], MR.at[par, x], xb_s.at[s, j], xb_r.at[s, x], dev(xx=xx)).start()
            scaled = block * GAIN[par, i, 0:1, cols(xx)]
            sum_a = sum_a + jnp.sum(scaled, axis=1, keepdims=True)
            sum_b = sum_b + jnp.sum(scaled * XH[xx], axis=1, keepdims=True)
        lane_id = lax.broadcasted_iota(jnp.int32, (FRM, 128), 1)
        high_a, high_b = sum_a.astype(BF16).astype(F32), sum_b.astype(BF16).astype(F32)
        packed = jnp.where(lane_id == 0, high_a, 0.0)
        packed = jnp.where(lane_id == 1, sum_a - high_a, packed)
        packed = jnp.where(lane_id == 2, high_b, packed)
        MT[par, x] = jnp.where(lane_id == 3, sum_b - high_b, packed).astype(BF16)
        for j, xx in far_first:
            rcopy(MT.at[par, x], MT.at[par, x], xt_s.at[s, j], xt_r.at[s, x], dev(xx=xx)).start()

        pump_back(s, 1)
        for tile in range(lanes_x):
            lane = slice(tile * 128, (tile + 1) * 128)
            spread = SP[16 : 16 + FRM, lane]
            for k in range(KT):
                start = 16 - reach + k
                TT[s, k : k + 1, lane] = jnp.sum(
                    spread * GL[s, start : start + FRM, lane] * MASK[k], axis=0, keepdims=True
                )

        @pl.when(((par != c) & (step > 0)) | ((s == 0) & (c == 0)))
        def _():
            ready = jnp.where(par != c, s + 1, 0)
            weight_gradient(ready)
            each(scatters, lambda g: g.begin(2, ready // 2))

        pump_back(s, 2)
        for j, xx in xs_:
            rcopy(MS.at[xx], MR.at[par, xx], xb_s.at[s, j], xb_r.at[s, xx], dev(xx=xx)).wait()
            rcopy(MT.at[par, xx], MT.at[par, xx], xt_s.at[s, j], xt_r.at[s, xx], dev(xx=xx)).wait()
        total = PF[...]
        for j, xx in xs_:
            total = total + MR[par, xx].astype(F32)
            packed = MT[par, xx].astype(F32)
            sum_a = sum_a + packed[:, 0:1] + packed[:, 1:2]
            sum_b = sum_b + packed[:, 2:3] + packed[:, 3:4]
        xhat = XH[x]
        TT[s, KT : KT + 1, :] = jnp.sum(total * xhat, axis=0, keepdims=True)
        gain = GAIN[par, i, 0:1, cols(x)]
        grad_in = inverse * (total * gain - sum_a * (1.0 / D) - xhat * (sum_b * (1.0 / D)))
        GC[...] = (GC[...] + grad_in).astype(BF16).astype(F32)
        pump_back(s, 3)
        return 0

    lax.fori_loop(0, SECT, backward, 0)

    for i in range(NX):
        rcopy(TT.at[2 * i + 1 - c], TS.at[i], tt_s.at[4, i], tt_r.at[4, i], sib).start()

    def rest(g):
        if g.cc == 0 and NX > 1:
            for e in range(5, 2 * g.h2):
                g.step(2, *at(e), 1)
        for i in range(1, NX):
            g.begin(1, i)

    def tail(low, high, g):
        for e in range(low, high):
            if e < 2 * g.h2:
                g.step(2, *at(e), 0)
            if e < 2 * g.h1:
                for i in range(1, NX):
                    g.step(1, *at(e), i)
            if e == 2 * g.h2 - 1:
                g.begin(1, 0)
            if 0 <= e - 2 * g.h2 < 2 * g.h1:
                g.step(1, *at(e - 2 * g.h2), 0)

    each(scatters, rest)
    each(scatters, functools.partial(tail, 0, 2))

    for i in range(NX):
        rcopy(TT.at[2 * i + 1 - c], TS.at[i], tt_s.at[4, i], tt_r.at[4, i], sib).wait()
    TY[...] = jnp.zeros(TY.shape, F32)
    for i in range(NX):
        summed = TT[2 * i + c] + TS[i]
        for r in range(KT + 1):
            TY[r // NZ, r % NZ, i : i + 1, :] = summed[r : r + 1]
    for j, yy in ys_:
        rcopy(TY.at[yy], TYR.at[y], tt_s.at[0, j], tt_r.at[0, y], dev(yy=yy)).start()
    TYR[y] = TY[y]
    each(scatters, functools.partial(tail, 2, 4))
    for j, yy in ys_:
        rcopy(TY.at[yy], TYR.at[yy], tt_s.at[0, j], tt_r.at[0, yy], dev(yy=yy)).wait()
    TY[y] = sum(TYR[k] for k in range(NY))
    for j, zz in zs_:
        rcopy(TY.at[y, zz], TZR.at[z], tt_s.at[1, j], tt_r.at[1, z], dev(zz=zz)).start()
    TZR[z] = TY[y, z]
    each(scatters, functools.partial(tail, 4, 6))
    for j, zz in zs_:
        rcopy(TY.at[y, zz], TZR.at[zz], tt_s.at[1, j], tt_r.at[1, zz], dev(zz=zz)).wait()
    TX[...] = sum(TZR[k] for k in range(NZ))
    for j, xx in xs_:
        rcopy(TX, TXR.at[x], tt_s.at[2, j], tt_r.at[2, x], dev(xx=xx)).start()
    TXR[x] = TX[...]
    each(scatters, functools.partial(tail, 6, 8))
    for j, xx in xs_:
        rcopy(TX, TXR.at[xx], tt_s.at[2, j], tt_r.at[2, xx], dev(xx=xx)).wait()
    TO1[z] = jnp.zeros(TO1.shape[1:], F32)
    mine = lax.broadcasted_iota(jnp.int32, (8, DX), 0) == x
    for b in range(NX):
        row = jnp.sum(jnp.where(mine, TXR[b], 0.0), axis=0, keepdims=True)
        for tile in range(lanes_x):
            k = b * lanes_x + tile
            TO1[z, k : k + 1, :] = row[:, tile * 128 : (tile + 1) * 128]
    for j, zz in zs_:
        rcopy(TO1.at[z], TO1.at[z], tt_s.at[3, j], tt_r.at[3, z], dev(zz=zz)).start()
    each(scatters, functools.partial(tail, 8, 10))
    for j, zz in zs_:
        rcopy(TO1.at[z], TO1.at[zz], tt_s.at[3, j], tt_r.at[3, zz], dev(zz=zz)).wait()
    for j, yy in ys_:
        rcopy(TO1, TO2.at[y], tt_s.at[5, j], tt_r.at[5, y], dev(yy=yy)).start()
    TO2[y] = TO1[...]
    each(scatters, functools.partial(tail, 10, 12))
    for j, xx in xs_:
        rcopy(FS.at[xx], FR.at[x], fin_s.at[j], fin_r.at[x], dev(xx=xx)).start()
    FR[x] = FS[x]
    for j, yy in ys_:
        rcopy(TO1, TO2.at[yy], tt_s.at[5, j], tt_r.at[5, yy], dev(yy=yy)).wait()
    o_taps[...] = TO2[...].reshape(o_taps.shape)

    for j, xx in xs_:
        rcopy(FS.at[xx], FR.at[xx], fin_s.at[j], fin_r.at[xx], dev(xx=xx)).wait()
    for b in range(NX):
        o_mix[0, :, b * DX : (b + 1) * DX] = FR[b, :, :DX].astype(F32)
        o_gate[0, :, b * DX : (b + 1) * DX] = FR[b, :, DX:].astype(F32)

    taps_out.wait_send()
    gain_out.wait_send()

    def drain(i, _):
        there = W.at[c, i]
        rcopy(there, there, sw_s.at[i], sw_r.at[i], sib).wait_send()
        rcopy(NT.at[0], NS.at[i], sn_s.at[i], sn_r.at[i], sib).wait_send()
        rcopy(GO.at[0], GS.at[i], sg_s.at[i], sg_r.at[i], sib).wait_send()
        return 0

    lax.fori_loop(0, NX, drain, 0)
    each(gathers, lambda g: g.drain())
    each(scatters, lambda g: g.drain())


def body(
    mel_tiles,
    utt_ids,
    tile_lengths,
    dest_shard,
    dest_slot,
    subsample_weight,
    mixing_weight,
    gate_weight,
    conv_taps,
    norm_gain,
    out_cot,
):
    ND = lax.axis_size("dp")
    SECT = lax.axis_size("pipe")
    NX = SECT // CORES
    NY, NZ = PHYS[ND]
    tiles, TSUB, feats = mel_tiles.shape
    D = subsample_weight.shape[1]
    KT = conv_taps.shape[1]
    R = mixing_weight.shape[1]
    FRM = tiles * TSUB // 2
    J = -(-feats // 128)
    DX = D // NX
    SR = -(-(TSUB * J + 1) // 16) * 16
    dims = dict(X=NX, Y=NY, Z=NZ, D=D, R=R, F=FRM, TSUB=TSUB, J=J, TAPS=KT)

    details = jnp.stack([dest_slot, utt_ids, tile_lengths], axis=1).astype(BF16)
    flat = jnp.concatenate(
        [
            jnp.pad(mel_tiles, ((0, 0), (0, 0), (0, J * 128 - feats))).reshape(tiles, TSUB * J * 128),
            jnp.pad(details, ((0, 0), (0, 125 + (SR - TSUB * J - 1) * 128))),
        ],
        axis=1,
    )
    order = (dest_shard[None, :] == jnp.arange(ND, dtype=jnp.int32)[:, None]).astype(BF16)
    slabs = jnp.dot(order, flat, preferred_element_type=F32).astype(BF16).reshape(ND, SR, 128)
    tg = jnp.concatenate([conv_taps[0], norm_gain], axis=0)
    gain8 = jnp.broadcast_to(norm_gain, (8, D))
    sub = jnp.pad(subsample_weight, ((0, J * 128 - feats), (0, 0)))
    sub = sub.reshape(J * 128, NX // 2, 2 * DX).transpose(1, 0, 2).reshape(NX // 2, NZ, R, 2 * DX)
    OR = -(-(D // 128) // 8) * 8
    NR = max(NY, NZ) // 2

    def vm(shape, kind=F32):
        return pltpu.VMEM(shape, kind)

    def sems(*shape):
        return pltpu.SemaphoreType.DMA(shape)

    scratch = [
        vm((2, NX, NY, NZ, R, 2 * DX), BF16),
        vm((2, NX, KT + 1, DX)),
        vm((2, NX, 8, D)),
        vm((NY, NZ, SR, 128), BF16),
        vm((NZ, NY, SR, 128), BF16),
        vm((ND, SR, 128)),
        vm((TSUB * ND, J * 128)),
        vm((FRM + 32, 128)),
        vm((KT, FRM, 128)),
        vm((SECT, NX, FRM, DX), BF16),
        vm((SECT, FRM, D), BF16),
        vm((NX, FRM, D), BF16),
        vm((SECT, FRM + 32, DX)),
        vm((FRM + 32, DX)),
        vm((SECT, FRM, DX)),
        vm((SECT, FRM, DX)),
        vm((SECT, FRM, DX)),
        vm((FRM, DX)),
        vm((FRM, DX), BF16),
        vm((FRM, DX)),
        vm((NX, FRM, DX)),
        vm((SECT, FRM, 2 * DX), BF16),
        vm((NX, FRM, 2 * DX), BF16),
        vm((NX, FRM, DX), BF16),
        vm((2, NX, FRM, DX), BF16),
        vm((2, NX, FRM, 128), BF16),
        vm((NX, NY, NZ, R, 2 * DX), BF16),
        vm((NX, 2, ND // 2, R, 2 * DX), BF16),
        vm((NX, 2, NR, R, 2 * DX), BF16),
        vm((NX, R, 2 * DX), BF16),
        vm((NX, R, 2 * DX), BF16),
        vm((SECT, KT + 1, DX)),
        vm((NX, KT + 1, DX)),
        vm((NY, NZ, 8, DX)),
        vm((NY, NZ, 8, DX)),
        vm((NZ, 8, DX)),
        vm((8, DX)),
        vm((NX, 8, DX)),
        vm((NZ, OR, 128)),
        vm((NY, NZ, OR, 128)),
        sems(4),
        sems(NX),
        sems(NX),
        sems(2, NX),
        sems(2, NX),
        sems(2, max(NY, NZ)),
        sems(2, max(NY, NZ)),
        sems(NX, 2, 2),
        sems(NX, 2, 2, NR),
        sems(NX, 2, 2),
        sems(NX, 2, 2, NR),
        sems(NX, 2, 2),
        sems(NX, 2, 2, NR),
        sems(NX, 2, 2),
        sems(NX, 2, 2, NR),
        sems(NX),
        sems(NX),
        sems(2),
        sems(2),
        sems(SECT, NX),
        sems(SECT, NX),
        sems(SECT, NX),
        sems(SECT, NX),
        sems(SECT, NX),
        sems(SECT, NX),
        sems(NX),
        sems(NX),
        sems(NX),
        sems(NX),
        sems(NX),
        sems(NX),
        sems(6, max(NX, NY, NZ)),
        sems(6, max(NX, NY, NZ)),
    ]
    in_vmem = pl.BlockSpec(memory_space=pltpu.VMEM)
    in_any = pl.BlockSpec(memory_space=pl.ANY)
    mix, gate, taps = pl.pallas_call(
        functools.partial(kernel, dims),
        out_shape=(
            jax.ShapeDtypeStruct((1, R, D), F32),
            jax.ShapeDtypeStruct((1, R, D), F32),
            jax.ShapeDtypeStruct((ND, OR, 128), F32),
        ),
        in_specs=[in_vmem, in_any, in_any, in_vmem, in_vmem, in_any, in_any],
        out_specs=(in_vmem, in_vmem, in_vmem),
        scratch_shapes=scratch,
        compiler_params=pltpu.CompilerParams(
            collective_id=0, has_side_effects=True, vmem_limit_bytes=VMEM_LIMIT
        ),
    )(slabs, mixing_weight, gate_weight, tg, gain8, sub, out_cot)
    rows = taps[:, : D // 128].reshape(ND, D)
    return mix, gate, rows[None, :KT], rows[KT:]


def solution(mesh):
    in_specs = (
        P("dp", None, None),
        P("dp"),
        P("dp"),
        P("dp"),
        P("dp"),
        P(),
        P("pipe", "dp", None),
        P("pipe", "dp", None),
        P("pipe", None, None),
        P("pipe", None),
        P("dp", None),
    )
    out_specs = (
        P("pipe", "dp", None),
        P("pipe", "dp", None),
        P("pipe", None, None),
        P("pipe", None),
    )
    return jax.shard_map(body, mesh=mesh, in_specs=in_specs, out_specs=out_specs, check_vma=False)
```

```python
import functools

import jax
import jax.numpy as jnp
from jax import lax
from jax.experimental import pallas as pl
from jax.experimental.pallas import tpu as pltpu
from jax.sharding import PartitionSpec as P

PHYS = {32: (4, 8), 8: (2, 4), 4: (2, 2)}
CORES = 2
EPSILON = 1e-05
F32 = jnp.float32
BF16 = jnp.bfloat16
VMEM_LIMIT = 60 * 1024 * 1024


def rcopy(src, dst, send_sem, recv_sem, device):
    return pltpu.make_async_remote_copy(
        src_ref=src,
        dst_ref=dst,
        send_sem=send_sem,
        recv_sem=recv_sem,
        device_id=device,
        device_id_type=pl.DeviceIdType.MESH,
    )


def kernel(
    dims,
    mel,
    ids,
    lengths,
    shards,
    slots,
    mixing,
    gating,
    taps_in,
    gain_in,
    sub,
    cot,
    o_mix,
    o_gate,
    o_taps,
    o_gain,
    W,
    TAPS,
    GAIN,
    tg,
    gain8,
    MF,
    slabs,
    T1,
    T2,
    TF,
    EA,
    CP,
    MASK,
    X,
    NT,
    NS,
    GL,
    SP,
    V,
    SG,
    CV,
    GC,
    CT,
    PF,
    XH,
    GO,
    GS,
    MS,
    MR,
    MT,
    G,
    RA,
    RB,
    FS,
    FR,
    TT,
    TS,
    TY,
    TYR,
    TZR,
    TX,
    TXR,
    TO1,
    TO2,
    lw_s,
    xw_s,
    xw_r,
    tg_s,
    tg_r,
    tl_s,
    tl_r,
    p1_s,
    p1_r,
    p2_s,
    p2_r,
    ra_s,
    ra_r,
    rb_s,
    rb_r,
    sw_s,
    sw_r,
    st_s,
    st_r,
    xf_s,
    xf_r,
    xb_s,
    xb_r,
    xt_s,
    xt_r,
    sn_s,
    sn_r,
    sg_s,
    sg_r,
    fin_s,
    fin_r,
    tt_s,
    tt_r,
):
    NX, NY, NZ = dims["X"], dims["Y"], dims["Z"]
    D, R, FRM, TSUB, J, KT = (dims[k] for k in ("D", "R", "F", "TSUB", "J", "TAPS"))
    DX = D // NX
    ND = NY * NZ
    SECT = 2 * NX
    reach = KT // 2
    lanes_x = DX // 128

    dpi = lax.axis_index("dp")
    pipe = lax.axis_index("pipe")
    x, c = pipe // CORES, pipe % CORES
    y, z = dpi // NZ, dpi % NZ

    def dev(yy=None, zz=None, xx=None, cc=None):
        yy = y if yy is None else yy
        zz = z if zz is None else zz
        xx = x if xx is None else xx
        cc = c if cc is None else cc
        return {"dp": yy * NZ + zz, "pipe": xx * CORES + cc}

    sib = dev(cc=1 - c)
    xs_ = [(j, (x + j) % NX) for j in range(1, NX)]
    far_first = sorted(xs_, key=lambda item: -min(item[0], NX - item[0]))
    ys_ = [(j, (y + j) % NY) for j in range(1, NY)]
    zs_ = [(j, (z + j) % NZ) for j in range(1, NZ)]

    def half(h):
        return pl.ds(h * DX, DX)

    def cols(b):
        return pl.ds(pl.multiple_of(b * DX, 128), DX)

    barrier = pltpu.get_barrier_semaphore()
    peers = [sib]
    peers += [dev(xx=xx) for _, xx in xs_]
    peers += [dev(yy=yy) for _, yy in ys_]
    peers += [dev(zz=zz) for _, zz in zs_]
    for peer in peers:
        pl.semaphore_signal(barrier, inc=1, device_id=peer, device_id_type=pl.DeviceIdType.MESH)
    pl.semaphore_wait(barrier, len(peers))

    for j, xx in xs_:
        rcopy(mixing.at[0, :, cols(xx)], W.at[c, x, y, z, :, half(0)], xw_s.at[j], xw_r.at[x], dev(xx=xx)).start()
        rcopy(gating.at[0, :, cols(xx)], W.at[c, x, y, z, :, half(1)], xw_s.at[j], xw_r.at[x], dev(xx=xx)).start()
    own_copies = [
        pltpu.make_async_copy(cot.at[pl.ds(pl.multiple_of(c * FRM, 16), FRM), cols(x)], CT, lw_s.at[2]),
        pltpu.make_async_copy(mixing.at[0, :, cols(x)], W.at[c, x, y, z, :, half(0)], lw_s.at[0]),
        pltpu.make_async_copy(gating.at[0, :, cols(x)], W.at[c, x, y, z, :, half(1)], lw_s.at[1]),
    ]
    feats = sub.shape[0]
    for k in range(NX // 2):
        for b in range(NZ):
            count = max(0, min(feats - b * R, R))
            if count < R:
                G[0, k, b, count:] = jnp.zeros((R - count, 2 * DX), BF16)
            if count > 0:
                part = sub.at[b * R : b * R + count, k * 2 * DX : (k + 1) * 2 * DX]
                own_copies.append(pltpu.make_async_copy(part, G.at[0, k, b, 0:count], lw_s.at[3 + k * NZ + b]))
    for copy in own_copies:
        copy.start()

    MF[...] = mel[...].astype(F32)
    order = shards[...] == lax.broadcasted_iota(jnp.int32, (ND, ND), 0)
    order_bf = order.astype(F32).astype(BF16)
    TF[...] = jnp.zeros(TF.shape, F32)
    for f in range(TSUB):
        moved = jnp.dot(order_bf, MF[:, f, :].astype(BF16), preferred_element_type=F32)
        for j in range(J):
            wide = min(128, feats - j * 128)
            TF[:, f * J + j, :wide] = moved[:, j * 128 : j * 128 + wide]
    lane_of = lax.broadcasted_iota(jnp.int32, (ND, 128), 1)
    details = jnp.zeros((ND, 128), F32)
    for k, row in enumerate((slots, ids, lengths)):
        column = jnp.sum(jnp.where(order, row[...].astype(F32), 0.0), axis=1, keepdims=True)
        details = jnp.where(lane_of == k, column, details)
    TF[:, TSUB * J, :] = details
    slabs[...] = TF[...].astype(BF16)

    for j, yy in ys_:
        rcopy(slabs.at[pl.ds(yy * NZ, NZ)], T1.at[y], tl_s.at[0, j], tl_r.at[0, y], dev(yy=yy)).start()
    T1[y] = slabs[pl.ds(y * NZ, NZ)]

    tg[0:KT] = taps_in[0]
    tg[KT : KT + 1] = gain_in[...]
    gain8[...] = jnp.broadcast_to(gain_in[...], gain8.shape)
    for j, xx in xs_:
        rcopy(tg.at[:, cols(xx)], TAPS.at[c, x], tg_s.at[0, j], tg_r.at[0, x], dev(xx=xx)).start()
        rcopy(gain8, GAIN.at[c, x], tg_s.at[1, j], tg_r.at[1, x], dev(xx=xx)).start()
    TAPS[c, x] = tg[:, cols(x)]
    GAIN[c, x] = gain8[...]

    for j, yy in ys_:
        rcopy(slabs.at[pl.ds(yy * NZ, NZ)], T1.at[yy], tl_s.at[0, j], tl_r.at[0, yy], dev(yy=yy)).wait()
    for j, zz in zs_:
        rcopy(T1.at[:, zz], T2.at[z], tl_s.at[1, j], tl_r.at[1, z], dev(zz=zz)).start()
    T2[z] = T1[:, z]

    for copy in own_copies:
        copy.wait()
    for j, xx in xs_:
        rcopy(W.at[c, x, y, z], W.at[c, xx, y, z], xw_s.at[j], xw_r.at[xx], dev(xx=xx)).wait()

    dirs = ((0, 1), (1, -1))

    class Rings:
        def __init__(self, cc):
            self.cc = cc
            self.n1, self.n2 = (NY, NZ) if cc == 0 else (NZ, NY)
            self.me1, self.me2 = (y, z) if cc == 0 else (z, y)
            self.h1, self.h2 = self.n1 // 2, self.n2 // 2
            self.m = self.n1 // 2

        def to(self, ring, sgn):
            me, n = (self.me1, self.n1) if ring == 1 else (self.me2, self.n2)
            pos = (me + sgn + n) % n
            return dev(yy=pos) if (ring == 1) == (self.cc == 0) else dev(zz=pos)

        def near(self, u, d):
            return u == d

    def at(e):
        return 1 + e // 2, e % 2

    class Gather(Rings):
        def block1(self, i, b, u):
            return W.at[0, i, b, z, :, half(u)] if self.cc == 0 else W.at[1, i, y, b, :, half(u)]

        def block2(self, i, b, u):
            part = pl.ds(u * self.m, self.m)
            return W.at[0, i, part, b] if self.cc == 0 else W.at[1, i, b, part]

        def step(self, ring, t, u, i):
            n, me, last, block, send, recv = (
                (self.n1, self.me1, self.h1, self.block1, p1_s, p1_r)
                if ring == 1
                else (self.n2, self.me2, self.h2, self.block2, p2_s, p2_r)
            )
            for d, sgn in dirs:
                held = block(i, (me - sgn * t + 2 * n) % n, u)

                def copy(k):
                    return rcopy(held, held, send.at[i, d, u], recv.at[i, d, u, k], self.to(ring, sgn))

                def arrive():
                    copy(t - 1).wait_recv()
                    if ring == 2:
                        rcopy(held, held, sw_s.at[i], sw_r.at[i], sib).start()

                if isinstance(t, int) and t == 0:
                    if ring == 2 and d == 0:
                        rcopy(held, held, sw_s.at[i], sw_r.at[i], sib).start()
                    if last > 1 or self.near(u, d):
                        copy(0).start()
                    continue
                if self.near(u, d):
                    pl.when(t <= last)(arrive)
                    pl.when(t < last)(lambda: copy(t).start())
                else:
                    pl.when(t < last)(arrive)
                    pl.when(t < last - 1)(lambda: copy(t).start())

        def begin(self, ring, i):
            for u in range(2):
                self.step(ring, 0, u, i)

        def drain(self):
            def one(i, _):
                for u in range(2):
                    for d in range(2):
                        far = 0 if self.near(u, d) else 1
                        k1, k2 = self.h1 - far, self.h2 - far
                        part = pl.ds(0, self.m)
                        if k1 > 0:
                            sent = W.at[0, i, 0:k1, 0, :, half(u)] if self.cc == 0 else W.at[1, i, 0, 0:k1, :, half(u)]
                            rcopy(sent, sent, p1_s.at[i, d, u], p1_r.at[i, d, u, 0], sib).wait_send()
                        if k2 > 0:
                            sent = W.at[0, i, part, 0:k2] if self.cc == 0 else W.at[1, i, 0:k2, part]
                            rcopy(sent, sent, p2_s.at[i, d, u], p2_r.at[i, d, u, 0], sib).wait_send()
                return 0

            lax.fori_loop(0, NX, one, 0)

    gathers = [Gather(cc) for cc in range(CORES)]

    def each(rings, f):
        for cc in range(CORES):
            pl.when(c == cc)(functools.partial(f, rings[cc]))

    def begin(g):
        g.begin(1, 0)
        for e in range(2 * g.h1):
            g.step(1, *at(e), 0)
        g.begin(2, 0)
        for i in range(1, NX if g.cc == 0 else min(NX, 2)):
            g.begin(1, i)

    def go_on(low, high, g):
        for e in range(low, high):
            if e < 2 * g.h2:
                g.step(2, *at(e), 0)
            if e < 2 * g.h1:
                for i in range(1, NX if g.cc == 0 else min(NX, 2)):
                    g.step(1, *at(e), i)
            if e == 2 * g.h1 - 1 and NX > 1:
                g.begin(2, 1)
                if g.cc == 1 and NX > 2:
                    g.begin(1, 2)
            if g.cc == 0 and 0 <= e - 4 < 2 * g.h2 and NX > 1:
                g.step(2, *at(e - 4), 1)
        if g.cc == 0 and high == 8 and NX > 2:
            g.begin(2, 2)

    each(gathers, begin)

    for j, xx in xs_:
        rcopy(tg.at[:, cols(xx)], TAPS.at[c, xx], tg_s.at[0, j], tg_r.at[0, xx], dev(xx=xx)).wait()
        rcopy(gain8, GAIN.at[c, xx], tg_s.at[1, j], tg_r.at[1, xx], dev(xx=xx)).wait()
    taps_out = rcopy(TAPS.at[c], TAPS.at[c], st_s.at[0], st_r.at[0], sib)
    gain_out = rcopy(GAIN.at[c], GAIN.at[c], st_s.at[1], st_r.at[1], sib)
    taps_out.start()
    gain_out.start()

    for j, zz in zs_:
        rcopy(T1.at[:, zz], T2.at[zz], tl_s.at[1, j], tl_r.at[1, zz], dev(zz=zz)).wait()
    TF[...] = T2[...].astype(F32).reshape(TF.shape)
    for f in range(TSUB):
        for j in range(J):
            EA[f * ND : (f + 1) * ND, j * 128 : (j + 1) * 128] = TF[:, f * J + j, :]

    each(gathers, functools.partial(go_on, 0, 1))
    stacked = EA[...].astype(BF16)
    embedded = [
        jnp.dot(stacked, G[0, k].reshape(J * 128, 2 * DX), preferred_element_type=F32).astype(BF16)
        for k in range(NX // 2)
    ]
    embedded = jnp.concatenate(embedded, axis=1)
    detail = TF[:, TSUB * J, :]
    rows = TSUB * ND
    detail_rows = jnp.concatenate([detail] * TSUB, axis=0)
    slot, label, length = (detail_rows[:, k : k + 1] for k in range(3))
    frame_in_tile = (lax.broadcasted_iota(jnp.int32, (rows, 1), 0) // ND).astype(F32)
    time_lane = lax.broadcasted_iota(jnp.int32, (rows, FRM), 1)
    first_slot = (c * (FRM // TSUB)).astype(F32)
    pick = (slot - first_slot == (time_lane // TSUB).astype(F32)) & (
        frame_in_tile == (time_lane % TSUB).astype(F32)
    )
    pick = pick.astype(F32).astype(BF16)
    placed = lax.dot_general(pick, embedded, (((0,), (0,)), ((), ())), preferred_element_type=F32).astype(BF16)
    for b in range(NX):
        X[0, b] = placed[:, b * DX : (b + 1) * DX]
    each(gathers, functools.partial(go_on, 1, 3))

    code_rows = jnp.broadcast_to(jnp.where(frame_in_tile < length, label, -1.0), (rows, 128)).astype(BF16)
    code = lax.dot_general(pick, code_rows, (((0,), (0,)), ((), ())), preferred_element_type=F32)
    CP[...] = jnp.full(CP.shape, -2.0, F32)
    CP[16 : 16 + FRM] = code
    for k in range(KT):
        start = 16 - reach + k
        MASK[k] = jnp.where((CP[start : start + FRM] == code) & (code >= 0.0), 1.0, 0.0)
    edge = jnp.zeros((16, DX), F32)
    SP[0:16] = edge
    SP[16 + FRM :] = edge

    def clear(s, _):
        GL[s, 0:16] = edge
        GL[s, 16 + FRM :] = edge
        return 0

    lax.fori_loop(0, SECT, clear, 0)
    each(gathers, functools.partial(go_on, 3, 8))

    rcopy(TAPS.at[1 - c], TAPS.at[1 - c], st_s.at[0], st_r.at[0], sib).wait_recv()
    rcopy(GAIN.at[1 - c], GAIN.at[1 - c], st_s.at[1], st_r.at[1], sib).wait_recv()

    def pump(s, q):
        pair = s // 2 + 1
        u = q // 2

        def run(g, ring, t, u, i):
            pl.when((i < NX) & (t <= (g.h1 if ring == 1 else g.h2)))(lambda: g.step(ring, t, u, i))

        def first(g):
            if q % 2 == 0:
                run(g, 2, 3 + s % 2, u, pair)
            else:
                run(g, 2, 1 + s % 2, u, pair + 1)
            if q == 3:
                pl.when((s % 2 == 1) & (pair + 2 < NX))(lambda: g.begin(2, pair + 2))

        def second(g):
            if q % 2 == 0:
                run(g, 2, 1 + s % 2, u, pair)
            else:
                for part in range(2):
                    run(g, 1, 1 + (s % 2) * 2 + u, part, pair + 1)
            if q == 3:
                pl.when((s % 2 == 1) & (pair + 1 < NX))(lambda: g.begin(2, pair + 1))
                pl.when((s % 2 == 1) & (pair + 2 < NX))(lambda: g.begin(1, pair + 2))

        each(gathers, lambda g: first(g) if g.cc == 0 else second(g))

    def statistics(s):
        blocks = [X[s, b].astype(F32) for b in range(NX)]
        mean = sum(jnp.sum(v, axis=1, keepdims=True) for v in blocks) * (1.0 / D)
        shifted = [v - mean for v in blocks]
        spread = sum(jnp.sum(v * v, axis=1, keepdims=True) for v in shifted) * (1.0 / D)
        return mean, shifted, lax.rsqrt(spread + EPSILON)

    def weight(s):
        return W[s % 2, s // 2].reshape(D, 2 * DX)

    def forward(s, _):
        @pl.when(s % 2 != c)
        def _():
            there = W.at[1 - c, s // 2]
            rcopy(there, there, sw_s.at[s // 2], sw_r.at[s // 2], sib).wait_recv()

        @pl.when(s > 0)
        def _():
            for j, xx in xs_:
                rcopy(X.at[s, x], X.at[s, xx], xf_s.at[s, j], xf_r.at[s, xx], dev(xx=xx)).wait()

        _, shifted, inverse = statistics(s)
        for b in range(NX):
            gain = GAIN[s % 2, s // 2, 0:1, b * DX : (b + 1) * DX]
            NT[s, :, b * DX : (b + 1) * DX] = (shifted[b] * inverse * gain).astype(BF16)

        @pl.when(s % 2 != c)
        def _():
            rcopy(NT.at[s], NS.at[s // 2], sn_s.at[s // 2], sn_r.at[s // 2], sib).start()

        pump(s, 0)
        both = jnp.dot(NT[s], weight(s), preferred_element_type=F32)
        value, gate = both[:, :DX], both[:, DX:]
        sig = jax.nn.sigmoid(gate)
        V[s] = value
        SG[s] = sig
        GL[s, 16 : 16 + FRM] = value * sig
        pump(s, 1)
        for tile in range(lanes_x):
            if tile == lanes_x // 2:
                pump(s, 2)
            lane = slice(tile * 128, (tile + 1) * 128)
            conv = jnp.zeros((FRM, 128), F32)
            for k in range(KT):
                start = 16 - reach + k
                conv = conv + GL[s, start : start + FRM, lane] * MASK[k] * TAPS[s % 2, s // 2, k : k + 1, lane]
            CV[s, :, lane] = conv

            @pl.when(s < SECT - 1)
            def _():
                result = X[s, x, :, lane].astype(F32) + conv * jax.nn.sigmoid(conv)
                X[s + 1, x, :, lane] = result.astype(BF16)
                piece = X.at[s + 1, x, :, lane]
                for j, xx in far_first:
                    rcopy(piece, piece, xf_s.at[s + 1, j], xf_r.at[s + 1, x], dev(xx=xx)).start()

        pump(s, 3)
        return 0

    lax.fori_loop(0, SECT, forward, 0)

    GC[...] = CT[...].astype(F32)

    def weight_gradient(s):
        i = s // 2
        rcopy(NT.at[s], NS.at[i], sn_s.at[i], sn_r.at[i], sib).wait_recv()
        rcopy(GO.at[s], GS.at[i], sg_s.at[i], sg_r.at[i], sib).wait_recv()
        grads = jnp.concatenate([GO[s], GS[i]], axis=0)
        width = D // NY
        for part in range(NY):
            lane = slice(part * width, (part + 1) * width)
            normed = jnp.concatenate([NT[s, :, lane], NS[i, :, lane]], axis=0)
            product = lax.dot_general(normed, grads, (((0,), (0,)), ((), ())), preferred_element_type=F32)
            G[i, part] = product.astype(BF16).reshape(NZ, R, 2 * DX)

    class Scatter(Rings):
        def own2(self, i, b, u):
            part = pl.ds(u * self.m, self.m)
            return G.at[i, part, b] if self.cc == 0 else G.at[i, b, part]

        def own1(self, i, b, u):
            return RA.at[i, 0, (self.h2 - 1) * self.n1 + b, :, half(u)]

        def held2(self, i, d, t, u):
            return RA.at[i, d, pl.ds((t - 1) * self.n1 + u * self.m, self.m)]

        def held1(self, i, d, t, u):
            return RB.at[i, d, t - 1, :, half(u)]

        def step(self, ring, t, u, i):
            n, me, last, own, held, send, recv = (
                (self.n1, self.me1, self.h1, self.own1, self.held1, rb_s, rb_r)
                if ring == 1
                else (self.n2, self.me2, self.h2, self.own2, self.held2, ra_s, ra_r)
            )
            for d, sgn in dirs:
                mine = own(i, (me + sgn * (last - t) + 2 * n) % n, u)
                near = self.near(u, d)

                def onward(src):
                    return rcopy(src, held(i, d, t + 1, u), send.at[i, d, u], recv.at[i, d, u, t], self.to(ring, sgn))

                if isinstance(t, int) and t == 0:
                    if near:
                        onward(mine).start()
                    continue

                def arrive():
                    there = held(i, d, t, u)
                    rcopy(there, there, send.at[i, d, u], recv.at[i, d, u, t - 1], self.to(ring, sgn)).wait_recv()

                    @pl.when(t < last)
                    def _():
                        there[...] = (there[...].astype(F32) + mine[...].astype(F32)).astype(BF16)
                        onward(there).start()

                if near:
                    arrive()
                else:
                    pl.when((t == 1) & (t < last))(lambda: onward(mine).start())
                    pl.when(t > 1)(arrive)

            @pl.when(t == last)
            def _():
                total = own(i, me, u)[...].astype(F32)
                for d in range(2):
                    if last > 1 or self.near(u, d):
                        total = total + held(i, d, last, u)[...].astype(F32)
                if ring == 1:
                    FS[i, :, half(u)] = total.astype(BF16)
                else:
                    held(i, 0, last, u)[...] = total.astype(BF16)

        def begin(self, ring, i):
            for u in range(2):
                self.step(ring, 0, u, i)

        def drain(self):
            def one(i, _):
                for u in range(2):
                    for d in range(2):
                        far = 0 if self.near(u, d) else 1
                        k1, k2 = self.h1 - far, self.h2 - far
                        if k1 > 0:
                            sent = RB.at[i, d, 0:k1, :, half(u)]
                            rcopy(sent, sent, rb_s.at[i, d, u], rb_r.at[i, d, u, 0], sib).wait_send()
                        if k2 > 0:
                            sent = RA.at[i, d, 0 : k2 * self.m]
                            rcopy(sent, sent, ra_s.at[i, d, u], ra_r.at[i, d, u, 0], sib).wait_send()
                return 0

            lax.fori_loop(0, NX, one, 0)

    scatters = [Scatter(cc) for cc in range(CORES)]

    both_parts = (0, 1)
    plan = {
        (0, 0): {0: [(2, 3, (1,), 1)], 1: [(2, 4, (0,), 1)], 2: [(2, 4, (1,), 1)], 3: [(2, 1, (0,), 0), (1, 0, None, 1)]},
        (0, 1): {
            0: [(2, 1, (1,), 1), (1, 1, both_parts, 2)],
            1: [(2, 2, (0,), 1)],
            2: [(2, 2, (1,), 1), (1, 2, both_parts, 2)],
            3: [(2, 3, (0,), 1)],
        },
        (1, 0): {
            0: [(2, 1, (0,), 0)],
            1: [(1, 1, both_parts, 1)],
            2: [(2, 1, (1,), 0)],
            3: [(1, 2, both_parts, 1)],
        },
        (1, 1): {
            0: [(2, 2, (0,), 1)],
            1: [(1, 3, both_parts, 2)],
            2: [(2, 2, (1,), 1)],
            3: [(1, 4, both_parts, 2), (1, 0, None, 1)],
        },
    }

    def pump_back(s, q):
        def one(g):
            for parity in range(2):
                for ring, t, parts, ahead in plan[g.cc, parity][q]:
                    if t <= (g.h1 if ring == 1 else g.h2):
                        pair = s // 2 + ahead

                        @pl.when((s % 2 == parity) & (pair < NX))
                        def _():
                            if t == 0:
                                g.begin(ring, pair)
                            else:
                                for u in parts:
                                    g.step(ring, t, u, pair)

        each(scatters, one)

    def backward(step, _):
        s = SECT - 1 - step
        par, i = s % 2, s // 2
        conv = CV[s]
        sig_conv = jax.nn.sigmoid(conv)
        seed = GC[...]
        SP[16 : 16 + FRM] = seed * (sig_conv * (1.0 + conv * (1.0 - sig_conv)))
        for tile in range(lanes_x):
            lane = slice(tile * 128, (tile + 1) * 128)
            total = jnp.zeros((FRM, 128), F32)
            for k in range(KT):
                start = 16 - reach + k
                total = total + SP[start : start + FRM, lane] * MASK[k] * TAPS[par, i, KT - 1 - k : KT - k, lane]
            grad_value = total * SG[s, :, lane]
            grad_gate = grad_value * V[s, :, lane] * (1.0 - SG[s, :, lane])
            GO[s, :, lane] = grad_value.astype(BF16)
            GO[s, :, DX + tile * 128 : DX + (tile + 1) * 128] = grad_gate.astype(BF16)

        @pl.when(par != c)
        def _():
            rcopy(GO.at[s], GS.at[i], sg_s.at[i], sg_r.at[i], sib).start()

        pump_back(s, 0)
        mean, shifted, inverse = statistics(s)
        for b in range(NX):
            XH[b] = shifted[b] * inverse
        sum_a = jnp.zeros((FRM, 1), F32)
        sum_b = jnp.zeros((FRM, 1), F32)
        per = NY // NX
        for j, xx in far_first + [(0, x)]:
            rows_w = W[par, i, pl.ds(xx * per, per)].reshape(DX, 2 * DX)
            block = lax.dot_general(GO[s], rows_w, (((1,), (1,)), ((), ())), preferred_element_type=F32)
            if j == 0:
                PF[...] = block
            else:
                MS[xx] = block.astype(BF16)
                rcopy(MS.at[xx], MR.at[par, x], xb_s.at[s, j], xb_r.at[s, x], dev(xx=xx)).start()
            scaled = block * GAIN[par, i, 0:1, cols(xx)]
            sum_a = sum_a + jnp.sum(scaled, axis=1, keepdims=True)
            sum_b = sum_b + jnp.sum(scaled * XH[xx], axis=1, keepdims=True)
        lane_id = lax.broadcasted_iota(jnp.int32, (FRM, 128), 1)
        high_a, high_b = sum_a.astype(BF16).astype(F32), sum_b.astype(BF16).astype(F32)
        packed = jnp.where(lane_id == 0, high_a, 0.0)
        packed = jnp.where(lane_id == 1, sum_a - high_a, packed)
        packed = jnp.where(lane_id == 2, high_b, packed)
        MT[par, x] = jnp.where(lane_id == 3, sum_b - high_b, packed).astype(BF16)
        for j, xx in far_first:
            rcopy(MT.at[par, x], MT.at[par, x], xt_s.at[s, j], xt_r.at[s, x], dev(xx=xx)).start()

        pump_back(s, 1)
        for tile in range(lanes_x):
            lane = slice(tile * 128, (tile + 1) * 128)
            spread = SP[16 : 16 + FRM, lane]
            for k in range(KT):
                start = 16 - reach + k
                TT[s, k : k + 1, lane] = jnp.sum(
                    spread * GL[s, start : start + FRM, lane] * MASK[k], axis=0, keepdims=True
                )

        @pl.when(par == c)
        def _():
            weight_gradient(s)
            each(scatters, lambda g: g.begin(2, i))

        pump_back(s, 2)
        for j, xx in xs_:
            rcopy(MS.at[xx], MR.at[par, xx], xb_s.at[s, j], xb_r.at[s, xx], dev(xx=xx)).wait()
            rcopy(MT.at[par, xx], MT.at[par, xx], xt_s.at[s, j], xt_r.at[s, xx], dev(xx=xx)).wait()
        total = PF[...]
        for j, xx in xs_:
            total = total + MR[par, xx].astype(F32)
            packed = MT[par, xx].astype(F32)
            sum_a = sum_a + packed[:, 0:1] + packed[:, 1:2]
            sum_b = sum_b + packed[:, 2:3] + packed[:, 3:4]
        xhat = XH[x]
        TT[s, KT : KT + 1, :] = jnp.sum(total * xhat, axis=0, keepdims=True)
        gain = GAIN[par, i, 0:1, cols(x)]
        grad_in = inverse * (total * gain - sum_a * (1.0 / D) - xhat * (sum_b * (1.0 / D)))
        GC[...] = (GC[...] + grad_in).astype(BF16).astype(F32)
        pump_back(s, 3)
        return 0

    lax.fori_loop(0, SECT, backward, 0)

    for i in range(NX):
        rcopy(TT.at[2 * i + 1 - c], TS.at[i], tt_s.at[4, i], tt_r.at[4, i], sib).start()

    def tail(low, high, g):
        done = 1 if g.cc == 0 else 2
        for e in range(low, high):
            if done <= e < 2 * g.h2:
                g.step(2, *at(e), 0)
            if NX > 1 and e < 2 * g.h1 and (g.cc == 0 or e >= 4):
                g.step(1, *at(e), 1)
            if e == 2 * g.h2 - 1:
                g.begin(1, 0)
            if 0 <= e - 2 * g.h2 < 2 * g.h1:
                g.step(1, *at(e - 2 * g.h2), 0)

    each(scatters, functools.partial(tail, 0, 2))

    for i in range(NX):
        rcopy(TT.at[2 * i + 1 - c], TS.at[i], tt_s.at[4, i], tt_r.at[4, i], sib).wait()
    TY[...] = jnp.zeros(TY.shape, F32)
    for i in range(NX):
        summed = TT[2 * i + c] + TS[i]
        for r in range(KT + 1):
            TY[r // NZ, r % NZ, i : i + 1, :] = summed[r : r + 1]
    for j, yy in ys_:
        rcopy(TY.at[yy], TYR.at[y], tt_s.at[0, j], tt_r.at[0, y], dev(yy=yy)).start()
    TYR[y] = TY[y]
    each(scatters, functools.partial(tail, 2, 4))
    for j, yy in ys_:
        rcopy(TY.at[yy], TYR.at[yy], tt_s.at[0, j], tt_r.at[0, yy], dev(yy=yy)).wait()
    TY[y] = sum(TYR[k] for k in range(NY))
    for j, zz in zs_:
        rcopy(TY.at[y, zz], TZR.at[z], tt_s.at[1, j], tt_r.at[1, z], dev(zz=zz)).start()
    TZR[z] = TY[y, z]
    each(scatters, functools.partial(tail, 4, 6))
    for j, zz in zs_:
        rcopy(TY.at[y, zz], TZR.at[zz], tt_s.at[1, j], tt_r.at[1, zz], dev(zz=zz)).wait()
    TX[...] = sum(TZR[k] for k in range(NZ))
    for j, xx in xs_:
        rcopy(TX, TXR.at[x], tt_s.at[2, j], tt_r.at[2, x], dev(xx=xx)).start()
    TXR[x] = TX[...]
    each(scatters, functools.partial(tail, 6, 8))
    for j, xx in xs_:
        rcopy(TX, TXR.at[xx], tt_s.at[2, j], tt_r.at[2, xx], dev(xx=xx)).wait()
    TO1[z] = jnp.zeros(TO1.shape[1:], F32)
    mine = lax.broadcasted_iota(jnp.int32, (8, DX), 0) == x
    for b in range(NX):
        row = jnp.sum(jnp.where(mine, TXR[b], 0.0), axis=0, keepdims=True)
        for tile in range(lanes_x):
            k = b * lanes_x + tile
            TO1[z, k : k + 1, :] = row[:, tile * 128 : (tile + 1) * 128]
    for j, zz in zs_:
        rcopy(TO1.at[z], TO1.at[z], tt_s.at[3, j], tt_r.at[3, z], dev(zz=zz)).start()
    each(scatters, functools.partial(tail, 8, 10))
    for j, zz in zs_:
        rcopy(TO1.at[z], TO1.at[zz], tt_s.at[3, j], tt_r.at[3, zz], dev(zz=zz)).wait()
    for j, yy in ys_:
        rcopy(TO1, TO2.at[y], tt_s.at[5, j], tt_r.at[5, y], dev(yy=yy)).start()
    TO2[y] = TO1[...]
    each(scatters, functools.partial(tail, 10, 12))
    for j, xx in xs_:
        rcopy(FS.at[xx], FR.at[x], fin_s.at[j], fin_r.at[x], dev(xx=xx)).start()
    FR[x] = FS[x]
    for j, yy in ys_:
        rcopy(TO1, TO2.at[yy], tt_s.at[5, j], tt_r.at[5, yy], dev(yy=yy)).wait()
    for k in range(D // 128):
        lane = slice(k * 128, (k + 1) * 128)
        for yy in range(NY):
            low, count = yy * NZ, min(NZ, KT - yy * NZ)
            piece = TO2[yy, :, k, :]
            o_taps[0, low : low + count, lane] = piece[:count]
            if count < NZ:
                o_gain[:, lane] = piece[count : count + 1]

    for j, xx in xs_:
        rcopy(FS.at[xx], FR.at[xx], fin_s.at[j], fin_r.at[xx], dev(xx=xx)).wait()
    for b in range(NX):
        o_mix[0, :, b * DX : (b + 1) * DX] = FR[b, :, :DX].astype(F32)
        o_gate[0, :, b * DX : (b + 1) * DX] = FR[b, :, DX:].astype(F32)

    taps_out.wait_send()
    gain_out.wait_send()

    def drain(i, _):
        there = W.at[c, i]
        rcopy(there, there, sw_s.at[i], sw_r.at[i], sib).wait_send()
        rcopy(NT.at[0], NS.at[i], sn_s.at[i], sn_r.at[i], sib).wait_send()
        rcopy(GO.at[0], GS.at[i], sg_s.at[i], sg_r.at[i], sib).wait_send()
        return 0

    lax.fori_loop(0, NX, drain, 0)
    each(gathers, lambda g: g.drain())
    each(scatters, lambda g: g.drain())


def body(
    mel_tiles,
    utt_ids,
    tile_lengths,
    dest_shard,
    dest_slot,
    subsample_weight,
    mixing_weight,
    gate_weight,
    conv_taps,
    norm_gain,
    out_cot,
):
    ND = lax.axis_size("dp")
    SECT = lax.axis_size("pipe")
    NX = SECT // CORES
    NY, NZ = PHYS[ND]
    tiles, TSUB, feats = mel_tiles.shape
    D = subsample_weight.shape[1]
    KT = conv_taps.shape[1]
    R = mixing_weight.shape[1]
    FRM = tiles * TSUB // 2
    J = -(-feats // 128)
    DX = D // NX
    SR = -(-(TSUB * J + 1) // 16) * 16
    dims = dict(X=NX, Y=NY, Z=NZ, D=D, R=R, F=FRM, TSUB=TSUB, J=J, TAPS=KT)

    OR = -(-(D // 128) // 8) * 8
    NR = max(NY, NZ) // 2

    def vm(shape, kind=F32):
        return pltpu.VMEM(shape, kind)

    def sems(*shape):
        return pltpu.SemaphoreType.DMA(shape)

    scratch = [
        vm((2, NX, NY, NZ, R, 2 * DX), BF16),
        vm((2, NX, KT + 1, DX)),
        vm((2, NX, 8, D)),
        vm((KT + 1, D)),
        vm((8, D)),
        vm((tiles, TSUB, feats)),
        vm((ND, SR, 128), BF16),
        vm((NY, NZ, SR, 128), BF16),
        vm((NZ, NY, SR, 128), BF16),
        vm((ND, SR, 128)),
        vm((TSUB * ND, J * 128)),
        vm((FRM + 32, 128)),
        vm((KT, FRM, 128)),
        vm((SECT, NX, FRM, DX), BF16),
        vm((SECT, FRM, D), BF16),
        vm((NX, FRM, D), BF16),
        vm((SECT, FRM + 32, DX)),
        vm((FRM + 32, DX)),
        vm((SECT, FRM, DX)),
        vm((SECT, FRM, DX)),
        vm((SECT, FRM, DX)),
        vm((FRM, DX)),
        vm((FRM, DX), BF16),
        vm((FRM, DX)),
        vm((NX, FRM, DX)),
        vm((SECT, FRM, 2 * DX), BF16),
        vm((NX, FRM, 2 * DX), BF16),
        vm((NX, FRM, DX), BF16),
        vm((2, NX, FRM, DX), BF16),
        vm((2, NX, FRM, 128), BF16),
        vm((NX, NY, NZ, R, 2 * DX), BF16),
        vm((NX, 2, ND // 2, R, 2 * DX), BF16),
        vm((NX, 2, NR, R, 2 * DX), BF16),
        vm((NX, R, 2 * DX), BF16),
        vm((NX, R, 2 * DX), BF16),
        vm((SECT, KT + 1, DX)),
        vm((NX, KT + 1, DX)),
        vm((NY, NZ, 8, DX)),
        vm((NY, NZ, 8, DX)),
        vm((NZ, 8, DX)),
        vm((8, DX)),
        vm((NX, 8, DX)),
        vm((NZ, OR, 128)),
        vm((NY, NZ, OR, 128)),
        sems(3 + NX * NZ),
        sems(NX),
        sems(NX),
        sems(2, NX),
        sems(2, NX),
        sems(2, max(NY, NZ)),
        sems(2, max(NY, NZ)),
        sems(NX, 2, 2),
        sems(NX, 2, 2, NR),
        sems(NX, 2, 2),
        sems(NX, 2, 2, NR),
        sems(NX, 2, 2),
        sems(NX, 2, 2, NR),
        sems(NX, 2, 2),
        sems(NX, 2, 2, NR),
        sems(NX),
        sems(NX),
        sems(2),
        sems(2),
        sems(SECT, NX),
        sems(SECT, NX),
        sems(SECT, NX),
        sems(SECT, NX),
        sems(SECT, NX),
        sems(SECT, NX),
        sems(NX),
        sems(NX),
        sems(NX),
        sems(NX),
        sems(NX),
        sems(NX),
        sems(6, max(NX, NY, NZ)),
        sems(6, max(NX, NY, NZ)),
    ]
    in_vmem = pl.BlockSpec(memory_space=pltpu.VMEM)
    in_any = pl.BlockSpec(memory_space=pl.ANY)
    return pl.pallas_call(
        functools.partial(kernel, dims),
        out_shape=(
            jax.ShapeDtypeStruct((1, R, D), F32),
            jax.ShapeDtypeStruct((1, R, D), F32),
            jax.ShapeDtypeStruct((1, KT, D), F32),
            jax.ShapeDtypeStruct((1, D), F32),
        ),
        in_specs=[in_vmem] * 5 + [in_any] * 2 + [in_vmem] * 2 + [in_any] * 2,
        out_specs=(in_vmem,) * 4,
        scratch_shapes=scratch,
        compiler_params=pltpu.CompilerParams(
            collective_id=0, has_side_effects=True, vmem_limit_bytes=VMEM_LIMIT
        ),
    )(
        mel_tiles,
        utt_ids[None],
        tile_lengths[None],
        dest_shard[None],
        dest_slot[None],
        mixing_weight,
        gate_weight,
        conv_taps,
        norm_gain,
        subsample_weight,
        out_cot,
    )


def solution(mesh):
    in_specs = (
        P("dp", None, None),
        P("dp"),
        P("dp"),
        P("dp"),
        P("dp"),
        P(),
        P("pipe", "dp", None),
        P("pipe", "dp", None),
        P("pipe", None, None),
        P("pipe", None),
        P("dp", None),
    )
    out_specs = (
        P("pipe", "dp", None),
        P("pipe", "dp", None),
        P("pipe", None, None),
        P("pipe", None),
    )
    return jax.shard_map(body, mesh=mesh, in_specs=in_specs, out_specs=out_specs, check_vma=False)
```

```python
import functools

import jax
import jax.numpy as jnp
from jax import lax
from jax.experimental import pallas as pl
from jax.experimental.pallas import tpu as pltpu
from jax.sharding import PartitionSpec as P

PHYS = {32: (4, 8), 8: (2, 4), 4: (2, 2)}
CORES = 2
EPSILON = 1e-05
F32 = jnp.float32
BF16 = jnp.bfloat16
VMEM_LIMIT = 60 * 1024 * 1024


def rcopy(src, dst, send_sem, recv_sem, device):
    return pltpu.make_async_remote_copy(
        src_ref=src,
        dst_ref=dst,
        send_sem=send_sem,
        recv_sem=recv_sem,
        device_id=device,
        device_id_type=pl.DeviceIdType.MESH,
    )


def kernel(
    dims,
    mel,
    ids,
    lengths,
    shards,
    slots,
    mixing,
    gating,
    taps_in,
    gain_in,
    sub,
    cot,
    o_mix,
    o_gate,
    o_taps,
    o_gain,
    W,
    TAPS,
    GAIN,
    tg,
    gain8,
    MF,
    slabs,
    T1,
    T2,
    TF,
    EA,
    CP,
    MASK,
    X,
    NT,
    NS,
    GL,
    SP,
    V,
    SG,
    CV,
    GC,
    CT,
    PF,
    XH,
    GO,
    GS,
    MS,
    MR,
    MT,
    G,
    RA,
    RB,
    FS,
    FR,
    TT,
    TS,
    TY,
    TYR,
    TZR,
    TX,
    TXR,
    TO1,
    TO2,
    lw_s,
    xw_s,
    xw_r,
    tg_s,
    tg_r,
    tl_s,
    tl_r,
    p1_s,
    p1_r,
    p2_s,
    p2_r,
    ra_s,
    ra_r,
    rb_s,
    rb_r,
    sw_s,
    sw_r,
    st_s,
    st_r,
    xf_s,
    xf_r,
    xb_s,
    xb_r,
    xt_s,
    xt_r,
    sn_s,
    sn_r,
    sg_s,
    sg_r,
    fin_s,
    fin_r,
    tt_s,
    tt_r,
):
    NX, NY, NZ = dims["X"], dims["Y"], dims["Z"]
    D, R, FRM, TSUB, J, KT = (dims[k] for k in ("D", "R", "F", "TSUB", "J", "TAPS"))
    DX = D // NX
    ND = NY * NZ
    SECT = 2 * NX
    reach = KT // 2
    lanes_x = DX // 128

    dpi = lax.axis_index("dp")
    pipe = lax.axis_index("pipe")
    x, c = pipe // CORES, pipe % CORES
    y, z = dpi // NZ, dpi % NZ

    def dev(yy=None, zz=None, xx=None, cc=None):
        yy = y if yy is None else yy
        zz = z if zz is None else zz
        xx = x if xx is None else xx
        cc = c if cc is None else cc
        return {"dp": yy * NZ + zz, "pipe": xx * CORES + cc}

    sib = dev(cc=1 - c)
    xs_ = [(j, (x + j) % NX) for j in range(1, NX)]
    far_first = sorted(xs_, key=lambda item: -min(item[0], NX - item[0]))
    ys_ = [(j, (y + j) % NY) for j in range(1, NY)]
    zs_ = [(j, (z + j) % NZ) for j in range(1, NZ)]

    def half(h):
        return pl.ds(h * DX, DX)

    def cols(b):
        return pl.ds(pl.multiple_of(b * DX, 128), DX)

    barrier = pltpu.get_barrier_semaphore()
    peers = [sib]
    peers += [dev(xx=xx) for _, xx in xs_]
    peers += [dev(yy=yy) for _, yy in ys_]
    peers += [dev(zz=zz) for _, zz in zs_]
    for peer in peers:
        pl.semaphore_signal(barrier, inc=1, device_id=peer, device_id_type=pl.DeviceIdType.MESH)
    pl.semaphore_wait(barrier, len(peers))

    for j, xx in xs_:
        rcopy(mixing.at[0, :, cols(xx)], W.at[c, x, y, z, :, half(0)], xw_s.at[j], xw_r.at[x], dev(xx=xx)).start()
        rcopy(gating.at[0, :, cols(xx)], W.at[c, x, y, z, :, half(1)], xw_s.at[j], xw_r.at[x], dev(xx=xx)).start()
    own_copies = [
        pltpu.make_async_copy(cot.at[pl.ds(pl.multiple_of(c * FRM, 16), FRM), cols(x)], CT, lw_s.at[2]),
        pltpu.make_async_copy(mixing.at[0, :, cols(x)], W.at[c, x, y, z, :, half(0)], lw_s.at[0]),
        pltpu.make_async_copy(gating.at[0, :, cols(x)], W.at[c, x, y, z, :, half(1)], lw_s.at[1]),
    ]
    feats = sub.shape[0]
    for k in range(NX // 2):
        for b in range(NZ):
            count = max(0, min(feats - b * R, R))
            if count < R:
                G[0, k, b, count:] = jnp.zeros((R - count, 2 * DX), BF16)
            if count > 0:
                part = sub.at[b * R : b * R + count, k * 2 * DX : (k + 1) * 2 * DX]
                own_copies.append(pltpu.make_async_copy(part, G.at[0, k, b, 0:count], lw_s.at[3 + k * NZ + b]))
    for copy in own_copies:
        copy.start()

    MF[...] = mel[...].astype(F32)
    order = shards[...] == lax.broadcasted_iota(jnp.int32, (ND, ND), 0)
    order_bf = order.astype(F32).astype(BF16)
    TF[...] = jnp.zeros(TF.shape, F32)
    for f in range(TSUB):
        moved = jnp.dot(order_bf, MF[:, f, :].astype(BF16), preferred_element_type=F32)
        for j in range(J):
            wide = min(128, feats - j * 128)
            TF[:, f * J + j, :wide] = moved[:, j * 128 : j * 128 + wide]
    lane_of = lax.broadcasted_iota(jnp.int32, (ND, 128), 1)
    details = jnp.zeros((ND, 128), F32)
    for k, row in enumerate((slots, ids, lengths)):
        column = jnp.sum(jnp.where(order, row[...].astype(F32), 0.0), axis=1, keepdims=True)
        details = jnp.where(lane_of == k, column, details)
    TF[:, TSUB * J, :] = details
    slabs[...] = TF[...].astype(BF16)

    for j, yy in ys_:
        rcopy(slabs.at[pl.ds(yy * NZ, NZ)], T1.at[y], tl_s.at[0, j], tl_r.at[0, y], dev(yy=yy)).start()
    T1[y] = slabs[pl.ds(y * NZ, NZ)]

    tg[0:KT] = taps_in[0]
    tg[KT : KT + 1] = gain_in[...]
    gain8[...] = jnp.broadcast_to(gain_in[...], gain8.shape)
    for j, xx in xs_:
        rcopy(tg.at[:, cols(xx)], TAPS.at[c, x], tg_s.at[0, j], tg_r.at[0, x], dev(xx=xx)).start()
        rcopy(gain8, GAIN.at[c, x], tg_s.at[1, j], tg_r.at[1, x], dev(xx=xx)).start()
    TAPS[c, x] = tg[:, cols(x)]
    GAIN[c, x] = gain8[...]

    for j, yy in ys_:
        rcopy(slabs.at[pl.ds(yy * NZ, NZ)], T1.at[yy], tl_s.at[0, j], tl_r.at[0, yy], dev(yy=yy)).wait()
    for j, zz in zs_:
        rcopy(T1.at[:, zz], T2.at[z], tl_s.at[1, j], tl_r.at[1, z], dev(zz=zz)).start()
    T2[z] = T1[:, z]

    for copy in own_copies:
        copy.wait()
    for j, xx in xs_:
        rcopy(W.at[c, x, y, z], W.at[c, xx, y, z], xw_s.at[j], xw_r.at[xx], dev(xx=xx)).wait()

    dirs = ((0, 1), (1, -1))

    class Rings:
        def __init__(self, cc):
            self.cc = cc
            self.n1, self.n2 = (NY, NZ) if cc == 0 else (NZ, NY)
            self.me1, self.me2 = (y, z) if cc == 0 else (z, y)
            self.h1, self.h2 = self.n1 // 2, self.n2 // 2
            self.m = self.n1 // 2

        def to(self, ring, sgn):
            me, n = (self.me1, self.n1) if ring == 1 else (self.me2, self.n2)
            pos = (me + sgn + n) % n
            return dev(yy=pos) if (ring == 1) == (self.cc == 0) else dev(zz=pos)

        def near(self, u, d):
            return u == d

    def at(e):
        return 1 + e // 2, e % 2

    class Gather(Rings):
        def block1(self, i, b, u):
            return W.at[0, i, b, z, :, half(u)] if self.cc == 0 else W.at[1, i, y, b, :, half(u)]

        def block2(self, i, b, u):
            part = pl.ds(u * self.m, self.m)
            return W.at[0, i, part, b] if self.cc == 0 else W.at[1, i, b, part]

        def step(self, ring, t, u, i):
            n, me, last, block, send, recv = (
                (self.n1, self.me1, self.h1, self.block1, p1_s, p1_r)
                if ring == 1
                else (self.n2, self.me2, self.h2, self.block2, p2_s, p2_r)
            )
            for d, sgn in dirs:
                held = block(i, (me - sgn * t + 2 * n) % n, u)

                def copy(k):
                    return rcopy(held, held, send.at[i, d, u], recv.at[i, d, u, k], self.to(ring, sgn))

                def arrive():
                    copy(t - 1).wait_recv()
                    if ring == 2:
                        rcopy(held, held, sw_s.at[i], sw_r.at[i], sib).start()

                if isinstance(t, int) and t == 0:
                    if ring == 2 and d == 0:
                        rcopy(held, held, sw_s.at[i], sw_r.at[i], sib).start()
                    if last > 1 or self.near(u, d):
                        copy(0).start()
                    continue
                if self.near(u, d):
                    pl.when(t <= last)(arrive)
                    pl.when(t < last)(lambda: copy(t).start())
                else:
                    pl.when(t < last)(arrive)
                    pl.when(t < last - 1)(lambda: copy(t).start())

        def begin(self, ring, i):
            for u in range(2):
                self.step(ring, 0, u, i)

        def drain(self):
            def one(i, _):
                for u in range(2):
                    for d in range(2):
                        far = 0 if self.near(u, d) else 1
                        k1, k2 = self.h1 - far, self.h2 - far
                        part = pl.ds(0, self.m)
                        if k1 > 0:
                            sent = W.at[0, i, 0:k1, 0, :, half(u)] if self.cc == 0 else W.at[1, i, 0, 0:k1, :, half(u)]
                            rcopy(sent, sent, p1_s.at[i, d, u], p1_r.at[i, d, u, 0], sib).wait_send()
                        if k2 > 0:
                            sent = W.at[0, i, part, 0:k2] if self.cc == 0 else W.at[1, i, 0:k2, part]
                            rcopy(sent, sent, p2_s.at[i, d, u], p2_r.at[i, d, u, 0], sib).wait_send()
                return 0

            lax.fori_loop(0, NX, one, 0)

    gathers = [Gather(cc) for cc in range(CORES)]

    def each(rings, f):
        for cc in range(CORES):
            pl.when(c == cc)(functools.partial(f, rings[cc]))

    def begin(g):
        if g.cc == 1:
            for i in range(NX):
                g.begin(1, i)
            for e in range(2 * g.h1):
                for i in range(NX):
                    g.step(1, *at(e), i)
                    if e == 2 * g.h1 - 1 and i == 0:
                        g.begin(2, 0)
            return
        g.begin(1, 0)
        for e in range(2 * g.h1):
            g.step(1, *at(e), 0)
        g.begin(2, 0)
        for i in range(1, NX):
            g.begin(1, i)

    def go_on(low, high, g):
        for e in range(low, high):
            if e < 2 * g.h2:
                g.step(2, *at(e), 0)
            if g.cc == 1:
                if e == 1 and NX > 1:
                    g.begin(2, 1)
                continue
            if e < 2 * g.h1:
                for i in range(1, NX):
                    g.step(1, *at(e), i)
            if e == 2 * g.h1 - 1 and NX > 1:
                g.begin(2, 1)
            if 0 <= e - 4 < 2 * g.h2 and NX > 1:
                g.step(2, *at(e - 4), 1)
        if g.cc == 0 and high == 8 and NX > 2:
            g.begin(2, 2)

    each(gathers, begin)

    for j, xx in xs_:
        rcopy(tg.at[:, cols(xx)], TAPS.at[c, xx], tg_s.at[0, j], tg_r.at[0, xx], dev(xx=xx)).wait()
        rcopy(gain8, GAIN.at[c, xx], tg_s.at[1, j], tg_r.at[1, xx], dev(xx=xx)).wait()
    taps_out = rcopy(TAPS.at[c], TAPS.at[c], st_s.at[0], st_r.at[0], sib)
    gain_out = rcopy(GAIN.at[c], GAIN.at[c], st_s.at[1], st_r.at[1], sib)
    taps_out.start()
    gain_out.start()

    for j, zz in zs_:
        rcopy(T1.at[:, zz], T2.at[zz], tl_s.at[1, j], tl_r.at[1, zz], dev(zz=zz)).wait()
    TF[...] = T2[...].astype(F32).reshape(TF.shape)
    for f in range(TSUB):
        for j in range(J):
            EA[f * ND : (f + 1) * ND, j * 128 : (j + 1) * 128] = TF[:, f * J + j, :]

    each(gathers, functools.partial(go_on, 0, 1))
    stacked = EA[...].astype(BF16)
    embedded = [
        jnp.dot(stacked, G[0, k].reshape(J * 128, 2 * DX), preferred_element_type=F32).astype(BF16)
        for k in range(NX // 2)
    ]
    embedded = jnp.concatenate(embedded, axis=1)
    detail = TF[:, TSUB * J, :]
    rows = TSUB * ND
    detail_rows = jnp.concatenate([detail] * TSUB, axis=0)
    slot, label, length = (detail_rows[:, k : k + 1] for k in range(3))
    frame_in_tile = (lax.broadcasted_iota(jnp.int32, (rows, 1), 0) // ND).astype(F32)
    time_lane = lax.broadcasted_iota(jnp.int32, (rows, FRM), 1)
    first_slot = (c * (FRM // TSUB)).astype(F32)
    pick = (slot - first_slot == (time_lane // TSUB).astype(F32)) & (
        frame_in_tile == (time_lane % TSUB).astype(F32)
    )
    pick = pick.astype(F32).astype(BF16)
    placed = lax.dot_general(pick, embedded, (((0,), (0,)), ((), ())), preferred_element_type=F32).astype(BF16)
    for b in range(NX):
        X[0, b] = placed[:, b * DX : (b + 1) * DX]
    each(gathers, functools.partial(go_on, 1, 3))

    code_rows = jnp.broadcast_to(jnp.where(frame_in_tile < length, label, -1.0), (rows, 128)).astype(BF16)
    code = lax.dot_general(pick, code_rows, (((0,), (0,)), ((), ())), preferred_element_type=F32)
    CP[...] = jnp.full(CP.shape, -2.0, F32)
    CP[16 : 16 + FRM] = code
    for k in range(KT):
        start = 16 - reach + k
        MASK[k] = jnp.where((CP[start : start + FRM] == code) & (code >= 0.0), 1.0, 0.0)
    edge = jnp.zeros((16, DX), F32)
    SP[0:16] = edge
    SP[16 + FRM :] = edge

    def clear(s, _):
        GL[s, 0:16] = edge
        GL[s, 16 + FRM :] = edge
        return 0

    lax.fori_loop(0, SECT, clear, 0)
    each(gathers, functools.partial(go_on, 3, 8))

    rcopy(TAPS.at[1 - c], TAPS.at[1 - c], st_s.at[0], st_r.at[0], sib).wait_recv()
    rcopy(GAIN.at[1 - c], GAIN.at[1 - c], st_s.at[1], st_r.at[1], sib).wait_recv()

    def pump(s, q):
        pair = s // 2 + 1
        u = q // 2

        def run(g, t, u, i):
            pl.when((i < NX) & (t <= g.h2))(lambda: g.step(2, t, u, i))

        def first(g):
            if q % 2 == 0:
                run(g, 3 + s % 2, u, pair)
            else:
                run(g, 1 + s % 2, u, pair + 1)
            if q == 3:
                pl.when((s % 2 == 1) & (pair + 2 < NX))(lambda: g.begin(2, pair + 2))

        def second(g):
            if q % 2 == 0:
                run(g, 1 + s % 2, u, pair)
            if q == 3:
                pl.when((s % 2 == 0) & (pair + 1 < NX))(lambda: g.begin(2, pair + 1))

        each(gathers, lambda g: first(g) if g.cc == 0 else second(g))

    def statistics(s):
        blocks = [X[s, b].astype(F32) for b in range(NX)]
        mean = sum(jnp.sum(v, axis=1, keepdims=True) for v in blocks) * (1.0 / D)
        shifted = [v - mean for v in blocks]
        spread = sum(jnp.sum(v * v, axis=1, keepdims=True) for v in shifted) * (1.0 / D)
        return mean, shifted, lax.rsqrt(spread + EPSILON)

    def weight(s):
        return W[s % 2, s // 2].reshape(D, 2 * DX)

    def forward(s, _):
        @pl.when(s % 2 != c)
        def _():
            there = W.at[1 - c, s // 2]
            rcopy(there, there, sw_s.at[s // 2], sw_r.at[s // 2], sib).wait_recv()

        @pl.when(s > 0)
        def _():
            for j, xx in xs_:
                rcopy(X.at[s, x], X.at[s, xx], xf_s.at[s, j], xf_r.at[s, xx], dev(xx=xx)).wait()

        _, shifted, inverse = statistics(s)
        for b in range(NX):
            gain = GAIN[s % 2, s // 2, 0:1, b * DX : (b + 1) * DX]
            NT[s, :, b * DX : (b + 1) * DX] = (shifted[b] * inverse * gain).astype(BF16)

        @pl.when(s % 2 != c)
        def _():
            rcopy(NT.at[s], NS.at[s // 2], sn_s.at[s // 2], sn_r.at[s // 2], sib).start()

        pump(s, 0)
        both = jnp.dot(NT[s], weight(s), preferred_element_type=F32)
        value, gate = both[:, :DX], both[:, DX:]
        sig = jax.nn.sigmoid(gate)
        V[s] = value
        SG[s] = sig
        GL[s, 16 : 16 + FRM] = value * sig
        pump(s, 1)
        for tile in range(lanes_x):
            if tile == lanes_x // 2:
                pump(s, 2)
            lane = slice(tile * 128, (tile + 1) * 128)
            conv = jnp.zeros((FRM, 128), F32)
            for k in range(KT):
                start = 16 - reach + k
                conv = conv + GL[s, start : start + FRM, lane] * MASK[k] * TAPS[s % 2, s // 2, k : k + 1, lane]
            CV[s, :, lane] = conv

            @pl.when(s < SECT - 1)
            def _():
                result = X[s, x, :, lane].astype(F32) + conv * jax.nn.sigmoid(conv)
                X[s + 1, x, :, lane] = result.astype(BF16)
                piece = X.at[s + 1, x, :, lane]
                for j, xx in far_first:
                    rcopy(piece, piece, xf_s.at[s + 1, j], xf_r.at[s + 1, x], dev(xx=xx)).start()

        pump(s, 3)
        return 0

    lax.fori_loop(0, SECT, forward, 0)

    GC[...] = CT[...].astype(F32)

    def weight_gradient(s):
        i = s // 2
        rcopy(NT.at[s], NS.at[i], sn_s.at[i], sn_r.at[i], sib).wait_recv()
        rcopy(GO.at[s], GS.at[i], sg_s.at[i], sg_r.at[i], sib).wait_recv()
        grads = jnp.concatenate([GO[s], GS[i]], axis=0)
        width = D // NY
        for part in range(NY):
            lane = slice(part * width, (part + 1) * width)
            normed = jnp.concatenate([NT[s, :, lane], NS[i, :, lane]], axis=0)
            product = lax.dot_general(normed, grads, (((0,), (0,)), ((), ())), preferred_element_type=F32)
            G[i, part] = product.astype(BF16).reshape(NZ, R, 2 * DX)

    class Scatter(Rings):
        def own2(self, i, b, u):
            part = pl.ds(u * self.m, self.m)
            return G.at[i, part, b] if self.cc == 0 else G.at[i, b, part]

        def own1(self, i, b, u):
            return RA.at[i, 0, (self.h2 - 1) * self.n1 + b, :, half(u)]

        def held2(self, i, d, t, u):
            return RA.at[i, d, pl.ds((t - 1) * self.n1 + u * self.m, self.m)]

        def held1(self, i, d, t, u):
            return RB.at[i, d, t - 1, :, half(u)]

        def step(self, ring, t, u, i):
            n, me, last, own, held, send, recv = (
                (self.n1, self.me1, self.h1, self.own1, self.held1, rb_s, rb_r)
                if ring == 1
                else (self.n2, self.me2, self.h2, self.own2, self.held2, ra_s, ra_r)
            )
            for d, sgn in dirs:
                mine = own(i, (me + sgn * (last - t) + 2 * n) % n, u)
                near = self.near(u, d)

                def onward(src):
                    return rcopy(src, held(i, d, t + 1, u), send.at[i, d, u], recv.at[i, d, u, t], self.to(ring, sgn))

                if isinstance(t, int) and t == 0:
                    if near:
                        onward(mine).start()
                    continue

                def arrive():
                    there = held(i, d, t, u)
                    rcopy(there, there, send.at[i, d, u], recv.at[i, d, u, t - 1], self.to(ring, sgn)).wait_recv()

                    @pl.when(t < last)
                    def _():
                        there[...] = (there[...].astype(F32) + mine[...].astype(F32)).astype(BF16)
                        onward(there).start()

                if near:
                    arrive()
                else:
                    pl.when((t == 1) & (t < last))(lambda: onward(mine).start())
                    pl.when(t > 1)(arrive)

            @pl.when(t == last)
            def _():
                total = own(i, me, u)[...].astype(F32)
                for d in range(2):
                    if last > 1 or self.near(u, d):
                        total = total + held(i, d, last, u)[...].astype(F32)
                if ring == 1:
                    FS[i, :, half(u)] = total.astype(BF16)
                else:
                    held(i, 0, last, u)[...] = total.astype(BF16)

        def begin(self, ring, i):
            for u in range(2):
                self.step(ring, 0, u, i)

        def drain(self):
            def one(i, _):
                for u in range(2):
                    for d in range(2):
                        far = 0 if self.near(u, d) else 1
                        k1, k2 = self.h1 - far, self.h2 - far
                        if k1 > 0:
                            sent = RB.at[i, d, 0:k1, :, half(u)]
                            rcopy(sent, sent, rb_s.at[i, d, u], rb_r.at[i, d, u, 0], sib).wait_send()
                        if k2 > 0:
                            sent = RA.at[i, d, 0 : k2 * self.m]
                            rcopy(sent, sent, ra_s.at[i, d, u], ra_r.at[i, d, u, 0], sib).wait_send()
                return 0

            lax.fori_loop(0, NX, one, 0)

    scatters = [Scatter(cc) for cc in range(CORES)]

    both_parts = (0, 1)
    plan = {
        (0, 0): {
            0: [(2, 4, (1,), 2), (1, 0, None, 2)],
            1: [(2, 2, (1,), 1)],
            2: [(2, 3, (0,), 1)],
            3: [(2, 1, (0,), 0)],
        },
        (0, 1): {
            0: [(2, 3, (1,), 2), (1, 1, both_parts, 3)],
            1: [(2, 1, (1,), 1)],
            2: [(2, 4, (0,), 2), (1, 2, both_parts, 3)],
            3: [(2, 2, (0,), 1)],
        },
        (1, 0): {
            0: [(2, 1, (0,), 0)],
            1: [(1, 1, both_parts, 1)],
            2: [(2, 1, (1,), 0)],
            3: [(1, 2, both_parts, 1)],
        },
        (1, 1): {
            0: [(2, 2, (0,), 1)],
            1: [(1, 3, both_parts, 2)],
            2: [(2, 2, (1,), 1)],
            3: [(1, 4, both_parts, 2), (1, 0, None, 1)],
        },
    }

    def pump_back(s, q):
        def one(g):
            for parity in range(2):
                for ring, t, parts, ahead in plan[g.cc, parity][q]:
                    if t <= (g.h1 if ring == 1 else g.h2):
                        pair = s // 2 + ahead

                        @pl.when((s % 2 == parity) & (pair < NX))
                        def _():
                            if t == 0:
                                g.begin(ring, pair)
                            else:
                                for u in parts:
                                    g.step(ring, t, u, pair)

        each(scatters, one)

    def backward(step, _):
        s = SECT - 1 - step
        par, i = s % 2, s // 2
        conv = CV[s]
        sig_conv = jax.nn.sigmoid(conv)
        seed = GC[...]
        SP[16 : 16 + FRM] = seed * (sig_conv * (1.0 + conv * (1.0 - sig_conv)))
        for tile in range(lanes_x):
            lane = slice(tile * 128, (tile + 1) * 128)
            total = jnp.zeros((FRM, 128), F32)
            for k in range(KT):
                start = 16 - reach + k
                total = total + SP[start : start + FRM, lane] * MASK[k] * TAPS[par, i, KT - 1 - k : KT - k, lane]
            grad_value = total * SG[s, :, lane]
            grad_gate = grad_value * V[s, :, lane] * (1.0 - SG[s, :, lane])
            GO[s, :, lane] = grad_value.astype(BF16)
            GO[s, :, DX + tile * 128 : DX + (tile + 1) * 128] = grad_gate.astype(BF16)

        @pl.when(par != c)
        def _():
            rcopy(GO.at[s], GS.at[i], sg_s.at[i], sg_r.at[i], sib).start()

        pump_back(s, 0)
        mean, shifted, inverse = statistics(s)
        for b in range(NX):
            XH[b] = shifted[b] * inverse
        sum_a = jnp.zeros((FRM, 1), F32)
        sum_b = jnp.zeros((FRM, 1), F32)
        per = NY // NX
        for j, xx in far_first + [(0, x)]:
            rows_w = W[par, i, pl.ds(xx * per, per)].reshape(DX, 2 * DX)
            block = lax.dot_general(GO[s], rows_w, (((1,), (1,)), ((), ())), preferred_element_type=F32)
            if j == 0:
                PF[...] = block
            else:
                MS[xx] = block.astype(BF16)
                rcopy(MS.at[xx], MR.at[par, x], xb_s.at[s, j], xb_r.at[s, x], dev(xx=xx)).start()
            scaled = block * GAIN[par, i, 0:1, cols(xx)]
            sum_a = sum_a + jnp.sum(scaled, axis=1, keepdims=True)
            sum_b = sum_b + jnp.sum(scaled * XH[xx], axis=1, keepdims=True)
        lane_id = lax.broadcasted_iota(jnp.int32, (FRM, 128), 1)
        high_a, high_b = sum_a.astype(BF16).astype(F32), sum_b.astype(BF16).astype(F32)
        packed = jnp.where(lane_id == 0, high_a, 0.0)
        packed = jnp.where(lane_id == 1, sum_a - high_a, packed)
        packed = jnp.where(lane_id == 2, high_b, packed)
        MT[par, x] = jnp.where(lane_id == 3, sum_b - high_b, packed).astype(BF16)
        for j, xx in far_first:
            rcopy(MT.at[par, x], MT.at[par, x], xt_s.at[s, j], xt_r.at[s, x], dev(xx=xx)).start()

        pump_back(s, 1)
        @pl.when(par == c)
        def _():
            weight_gradient(s)
            each(scatters, lambda g: g.begin(2, i))

        for tile in range(lanes_x):
            lane = slice(tile * 128, (tile + 1) * 128)
            spread = SP[16 : 16 + FRM, lane]
            for k in range(KT):
                start = 16 - reach + k
                TT[s, k : k + 1, lane] = jnp.sum(
                    spread * GL[s, start : start + FRM, lane] * MASK[k], axis=0, keepdims=True
                )

        pump_back(s, 2)
        for j, xx in xs_:
            rcopy(MS.at[xx], MR.at[par, xx], xb_s.at[s, j], xb_r.at[s, xx], dev(xx=xx)).wait()
            rcopy(MT.at[par, xx], MT.at[par, xx], xt_s.at[s, j], xt_r.at[s, xx], dev(xx=xx)).wait()
        total = PF[...]
        for j, xx in xs_:
            total = total + MR[par, xx].astype(F32)
            packed = MT[par, xx].astype(F32)
            sum_a = sum_a + packed[:, 0:1] + packed[:, 1:2]
            sum_b = sum_b + packed[:, 2:3] + packed[:, 3:4]
        xhat = XH[x]
        TT[s, KT : KT + 1, :] = jnp.sum(total * xhat, axis=0, keepdims=True)
        gain = GAIN[par, i, 0:1, cols(x)]
        grad_in = inverse * (total * gain - sum_a * (1.0 / D) - xhat * (sum_b * (1.0 / D)))
        GC[...] = (GC[...] + grad_in).astype(BF16).astype(F32)
        pump_back(s, 3)
        return 0

    lax.fori_loop(0, SECT, backward, 0)

    for i in range(NX):
        rcopy(TT.at[2 * i + 1 - c], TS.at[i], tt_s.at[4, i], tt_r.at[4, i], sib).start()

    def tail(low, high, g):
        done = 1 if g.cc == 0 else 2
        late = {0: 5, 2: 6, 3: 7} if g.cc == 0 and NX > 1 else {}
        for e in range(low, high):
            if late.get(e, 8) < 2 * g.h2:
                g.step(2, *at(late[e]), 1)
            if done <= e < 2 * g.h2:
                g.step(2, *at(e), 0)
            if g.cc == 0:
                if NX > 2 and e < 2 * g.h1:
                    g.step(1, *at(e), 2)
                if NX > 1 and e == 3:
                    g.begin(1, 1)
                if NX > 1 and 0 <= e - 4 < 2 * g.h1:
                    g.step(1, *at(e - 4), 1)
            elif NX > 1 and 4 <= e < 2 * g.h1:
                g.step(1, *at(e), 1)
            if e == 2 * g.h2 - 1:
                g.begin(1, 0)
            if 0 <= e - 2 * g.h2 < 2 * g.h1:
                g.step(1, *at(e - 2 * g.h2), 0)

    each(scatters, functools.partial(tail, 0, 2))

    for i in range(NX):
        rcopy(TT.at[2 * i + 1 - c], TS.at[i], tt_s.at[4, i], tt_r.at[4, i], sib).wait()
    TY[...] = jnp.zeros(TY.shape, F32)
    for i in range(NX):
        summed = TT[2 * i + c] + TS[i]
        for r in range(KT + 1):
            TY[r // NZ, r % NZ, i : i + 1, :] = summed[r : r + 1]
    for j, yy in ys_:
        rcopy(TY.at[yy], TYR.at[y], tt_s.at[0, j], tt_r.at[0, y], dev(yy=yy)).start()
    TYR[y] = TY[y]
    each(scatters, functools.partial(tail, 2, 4))
    for j, yy in ys_:
        rcopy(TY.at[yy], TYR.at[yy], tt_s.at[0, j], tt_r.at[0, yy], dev(yy=yy)).wait()
    TY[y] = sum(TYR[k] for k in range(NY))
    for j, zz in zs_:
        rcopy(TY.at[y, zz], TZR.at[z], tt_s.at[1, j], tt_r.at[1, z], dev(zz=zz)).start()
    TZR[z] = TY[y, z]
    each(scatters, functools.partial(tail, 4, 6))
    for j, zz in zs_:
        rcopy(TY.at[y, zz], TZR.at[zz], tt_s.at[1, j], tt_r.at[1, zz], dev(zz=zz)).wait()
    TX[...] = sum(TZR[k] for k in range(NZ))
    for j, xx in xs_:
        rcopy(TX, TXR.at[x], tt_s.at[2, j], tt_r.at[2, x], dev(xx=xx)).start()
    TXR[x] = TX[...]
    each(scatters, functools.partial(tail, 6, 8))
    for j, xx in xs_:
        rcopy(TX, TXR.at[xx], tt_s.at[2, j], tt_r.at[2, xx], dev(xx=xx)).wait()
    TO1[z] = jnp.zeros(TO1.shape[1:], F32)
    mine = lax.broadcasted_iota(jnp.int32, (8, DX), 0) == x
    for b in range(NX):
        row = jnp.sum(jnp.where(mine, TXR[b], 0.0), axis=0, keepdims=True)
        for tile in range(lanes_x):
            k = b * lanes_x + tile
            TO1[z, k : k + 1, :] = row[:, tile * 128 : (tile + 1) * 128]
    for j, zz in zs_:
        rcopy(TO1.at[z], TO1.at[z], tt_s.at[3, j], tt_r.at[3, z], dev(zz=zz)).start()
    each(scatters, functools.partial(tail, 8, 10))
    for j, zz in zs_:
        rcopy(TO1.at[z], TO1.at[zz], tt_s.at[3, j], tt_r.at[3, zz], dev(zz=zz)).wait()
    for j, yy in ys_:
        rcopy(TO1, TO2.at[y], tt_s.at[5, j], tt_r.at[5, y], dev(yy=yy)).start()
    TO2[y] = TO1[...]
    each(scatters, functools.partial(tail, 10, 12))
    for j, xx in xs_:
        rcopy(FS.at[xx], FR.at[x], fin_s.at[j], fin_r.at[x], dev(xx=xx)).start()
    FR[x] = FS[x]
    for j, yy in ys_:
        rcopy(TO1, TO2.at[yy], tt_s.at[5, j], tt_r.at[5, yy], dev(yy=yy)).wait()
    for k in range(D // 128):
        lane = slice(k * 128, (k + 1) * 128)
        for yy in range(NY):
            low, count = yy * NZ, min(NZ, KT - yy * NZ)
            piece = TO2[yy, :, k, :]
            o_taps[0, low : low + count, lane] = piece[:count]
            if count < NZ:
                o_gain[:, lane] = piece[count : count + 1]

    for j, xx in xs_:
        rcopy(FS.at[xx], FR.at[xx], fin_s.at[j], fin_r.at[xx], dev(xx=xx)).wait()
    for b in range(NX):
        o_mix[0, :, b * DX : (b + 1) * DX] = FR[b, :, :DX].astype(F32)
        o_gate[0, :, b * DX : (b + 1) * DX] = FR[b, :, DX:].astype(F32)

    taps_out.wait_send()
    gain_out.wait_send()

    def drain(i, _):
        there = W.at[c, i]
        rcopy(there, there, sw_s.at[i], sw_r.at[i], sib).wait_send()
        rcopy(NT.at[0], NS.at[i], sn_s.at[i], sn_r.at[i], sib).wait_send()
        rcopy(GO.at[0], GS.at[i], sg_s.at[i], sg_r.at[i], sib).wait_send()
        return 0

    lax.fori_loop(0, NX, drain, 0)
    each(gathers, lambda g: g.drain())
    each(scatters, lambda g: g.drain())


def body(
    mel_tiles,
    utt_ids,
    tile_lengths,
    dest_shard,
    dest_slot,
    subsample_weight,
    mixing_weight,
    gate_weight,
    conv_taps,
    norm_gain,
    out_cot,
):
    ND = lax.axis_size("dp")
    SECT = lax.axis_size("pipe")
    NX = SECT // CORES
    NY, NZ = PHYS[ND]
    tiles, TSUB, feats = mel_tiles.shape
    D = subsample_weight.shape[1]
    KT = conv_taps.shape[1]
    R = mixing_weight.shape[1]
    FRM = tiles * TSUB // 2
    J = -(-feats // 128)
    DX = D // NX
    SR = -(-(TSUB * J + 1) // 16) * 16
    dims = dict(X=NX, Y=NY, Z=NZ, D=D, R=R, F=FRM, TSUB=TSUB, J=J, TAPS=KT)

    OR = -(-(D // 128) // 8) * 8
    NR = max(NY, NZ) // 2

    def vm(shape, kind=F32):
        return pltpu.VMEM(shape, kind)

    def sems(*shape):
        return pltpu.SemaphoreType.DMA(shape)

    scratch = [
        vm((2, NX, NY, NZ, R, 2 * DX), BF16),
        vm((2, NX, KT + 1, DX)),
        vm((2, NX, 8, D)),
        vm((KT + 1, D)),
        vm((8, D)),
        vm((tiles, TSUB, feats)),
        vm((ND, SR, 128), BF16),
        vm((NY, NZ, SR, 128), BF16),
        vm((NZ, NY, SR, 128), BF16),
        vm((ND, SR, 128)),
        vm((TSUB * ND, J * 128)),
        vm((FRM + 32, 128)),
        vm((KT, FRM, 128)),
        vm((SECT, NX, FRM, DX), BF16),
        vm((SECT, FRM, D), BF16),
        vm((NX, FRM, D), BF16),
        vm((SECT, FRM + 32, DX)),
        vm((FRM + 32, DX)),
        vm((SECT, FRM, DX)),
        vm((SECT, FRM, DX)),
        vm((SECT, FRM, DX)),
        vm((FRM, DX)),
        vm((FRM, DX), BF16),
        vm((FRM, DX)),
        vm((NX, FRM, DX)),
        vm((SECT, FRM, 2 * DX), BF16),
        vm((NX, FRM, 2 * DX), BF16),
        vm((NX, FRM, DX), BF16),
        vm((2, NX, FRM, DX), BF16),
        vm((2, NX, FRM, 128), BF16),
        vm((NX, NY, NZ, R, 2 * DX), BF16),
        vm((NX, 2, ND // 2, R, 2 * DX), BF16),
        vm((NX, 2, NR, R, 2 * DX), BF16),
        vm((NX, R, 2 * DX), BF16),
        vm((NX, R, 2 * DX), BF16),
        vm((SECT, KT + 1, DX)),
        vm((NX, KT + 1, DX)),
        vm((NY, NZ, 8, DX)),
        vm((NY, NZ, 8, DX)),
        vm((NZ, 8, DX)),
        vm((8, DX)),
        vm((NX, 8, DX)),
        vm((NZ, OR, 128)),
        vm((NY, NZ, OR, 128)),
        sems(3 + NX * NZ),
        sems(NX),
        sems(NX),
        sems(2, NX),
        sems(2, NX),
        sems(2, max(NY, NZ)),
        sems(2, max(NY, NZ)),
        sems(NX, 2, 2),
        sems(NX, 2, 2, NR),
        sems(NX, 2, 2),
        sems(NX, 2, 2, NR),
        sems(NX, 2, 2),
        sems(NX, 2, 2, NR),
        sems(NX, 2, 2),
        sems(NX, 2, 2, NR),
        sems(NX),
        sems(NX),
        sems(2),
        sems(2),
        sems(SECT, NX),
        sems(SECT, NX),
        sems(SECT, NX),
        sems(SECT, NX),
        sems(SECT, NX),
        sems(SECT, NX),
        sems(NX),
        sems(NX),
        sems(NX),
        sems(NX),
        sems(NX),
        sems(NX),
        sems(6, max(NX, NY, NZ)),
        sems(6, max(NX, NY, NZ)),
    ]
    in_vmem = pl.BlockSpec(memory_space=pltpu.VMEM)
    in_any = pl.BlockSpec(memory_space=pl.ANY)
    return pl.pallas_call(
        functools.partial(kernel, dims),
        out_shape=(
            jax.ShapeDtypeStruct((1, R, D), F32),
            jax.ShapeDtypeStruct((1, R, D), F32),
            jax.ShapeDtypeStruct((1, KT, D), F32),
            jax.ShapeDtypeStruct((1, D), F32),
        ),
        in_specs=[in_vmem] * 5 + [in_any] * 2 + [in_vmem] * 2 + [in_any] * 2,
        out_specs=(in_vmem,) * 4,
        scratch_shapes=scratch,
        compiler_params=pltpu.CompilerParams(
            collective_id=0, has_side_effects=True, vmem_limit_bytes=VMEM_LIMIT
        ),
    )(
        mel_tiles,
        utt_ids[None],
        tile_lengths[None],
        dest_shard[None],
        dest_slot[None],
        mixing_weight,
        gate_weight,
        conv_taps,
        norm_gain,
        subsample_weight,
        out_cot,
    )


def solution(mesh):
    in_specs = (
        P("dp", None, None),
        P("dp"),
        P("dp"),
        P("dp"),
        P("dp"),
        P(),
        P("pipe", "dp", None),
        P("pipe", "dp", None),
        P("pipe", None, None),
        P("pipe", None),
        P("dp", None),
    )
    out_specs = (
        P("pipe", "dp", None),
        P("pipe", "dp", None),
        P("pipe", None, None),
        P("pipe", None),
    )
    return jax.shard_map(body, mesh=mesh, in_specs=in_specs, out_specs=out_specs, check_vma=False)
```

```python
import functools

import jax
import jax.numpy as jnp
from jax import lax
from jax.experimental import pallas as pl
from jax.experimental.pallas import tpu as pltpu
from jax.sharding import PartitionSpec as P

PHYS = {32: (4, 8), 8: (2, 4), 4: (2, 2)}
CORES = 2
EPSILON = 1e-05
F32 = jnp.float32
BF16 = jnp.bfloat16
VMEM_LIMIT = 60 * 1024 * 1024


def rcopy(src, dst, send_sem, recv_sem, device):
    return pltpu.make_async_remote_copy(
        src_ref=src,
        dst_ref=dst,
        send_sem=send_sem,
        recv_sem=recv_sem,
        device_id=device,
        device_id_type=pl.DeviceIdType.MESH,
    )


def kernel(
    dims,
    mel,
    ids,
    lengths,
    shards,
    slots,
    mixing,
    gating,
    taps_in,
    gain_in,
    sub,
    cot,
    o_mix,
    o_gate,
    o_taps,
    o_gain,
    W,
    TAPS,
    GAIN,
    tg,
    gain8,
    MF,
    slabs,
    T1,
    T2,
    TF,
    EA,
    CP,
    MASK,
    X,
    NT,
    NS,
    GL,
    SP,
    V,
    SG,
    CV,
    GC,
    CT,
    PF,
    XH,
    GO,
    GS,
    MS,
    MR,
    MT,
    G,
    RA,
    RB,
    FS,
    FR,
    TT,
    TS,
    TY,
    TYR,
    TZR,
    TX,
    TXR,
    TO1,
    TO2,
    lw_s,
    xw_s,
    xw_r,
    tg_s,
    tg_r,
    tl_s,
    tl_r,
    p1_s,
    p1_r,
    p2_s,
    p2_r,
    ra_s,
    ra_r,
    rb_s,
    rb_r,
    sw_s,
    sw_r,
    st_s,
    st_r,
    xf_s,
    xf_r,
    xb_s,
    xb_r,
    xt_s,
    xt_r,
    sn_s,
    sn_r,
    sg_s,
    sg_r,
    fin_s,
    fin_r,
    tt_s,
    tt_r,
):
    NX, NY, NZ = dims["X"], dims["Y"], dims["Z"]
    D, R, FRM, TSUB, J, KT = (dims[k] for k in ("D", "R", "F", "TSUB", "J", "TAPS"))
    DX = D // NX
    ND = NY * NZ
    SECT = 2 * NX
    reach = KT // 2
    lanes_x = DX // 128

    dpi = lax.axis_index("dp")
    pipe = lax.axis_index("pipe")
    x, c = pipe // CORES, pipe % CORES
    y, z = dpi // NZ, dpi % NZ

    def dev(yy=None, zz=None, xx=None, cc=None):
        yy = y if yy is None else yy
        zz = z if zz is None else zz
        xx = x if xx is None else xx
        cc = c if cc is None else cc
        return {"dp": yy * NZ + zz, "pipe": xx * CORES + cc}

    sib = dev(cc=1 - c)
    xs_ = [(j, (x + j) % NX) for j in range(1, NX)]
    far_first = sorted(xs_, key=lambda item: -min(item[0], NX - item[0]))
    ys_ = [(j, (y + j) % NY) for j in range(1, NY)]
    zs_ = [(j, (z + j) % NZ) for j in range(1, NZ)]

    def half(h):
        return pl.ds(h * DX, DX)

    def cols(b):
        return pl.ds(pl.multiple_of(b * DX, 128), DX)

    barrier = pltpu.get_barrier_semaphore()
    peers = [sib]
    peers += [dev(xx=xx) for _, xx in xs_]
    peers += [dev(yy=yy) for _, yy in ys_]
    peers += [dev(zz=zz) for _, zz in zs_]
    for peer in peers:
        pl.semaphore_signal(barrier, inc=1, device_id=peer, device_id_type=pl.DeviceIdType.MESH)
    pl.semaphore_wait(barrier, len(peers))

    for j, xx in xs_:
        rcopy(mixing.at[0, :, cols(xx)], W.at[c, x, y, z, :, half(0)], xw_s.at[j], xw_r.at[x], dev(xx=xx)).start()
        rcopy(gating.at[0, :, cols(xx)], W.at[c, x, y, z, :, half(1)], xw_s.at[j], xw_r.at[x], dev(xx=xx)).start()
    own_copies = [
        pltpu.make_async_copy(cot.at[pl.ds(pl.multiple_of(c * FRM, 16), FRM), cols(x)], CT, lw_s.at[2]),
        pltpu.make_async_copy(mixing.at[0, :, cols(x)], W.at[c, x, y, z, :, half(0)], lw_s.at[0]),
        pltpu.make_async_copy(gating.at[0, :, cols(x)], W.at[c, x, y, z, :, half(1)], lw_s.at[1]),
    ]
    feats = sub.shape[0]
    for k in range(NX // 2):
        for b in range(NZ):
            count = max(0, min(feats - b * R, R))
            if count < R:
                G[0, k, b, count:] = jnp.zeros((R - count, 2 * DX), BF16)
            if count > 0:
                part = sub.at[b * R : b * R + count, k * 2 * DX : (k + 1) * 2 * DX]
                own_copies.append(pltpu.make_async_copy(part, G.at[0, k, b, 0:count], lw_s.at[3 + k * NZ + b]))
    for copy in own_copies:
        copy.start()

    MF[...] = mel[...].astype(F32)
    order = shards[...] == lax.broadcasted_iota(jnp.int32, (ND, ND), 0)
    order_bf = order.astype(F32).astype(BF16)
    TF[...] = jnp.zeros(TF.shape, F32)
    for f in range(TSUB):
        moved = jnp.dot(order_bf, MF[:, f, :].astype(BF16), preferred_element_type=F32)
        for j in range(J):
            wide = min(128, feats - j * 128)
            TF[:, f * J + j, :wide] = moved[:, j * 128 : j * 128 + wide]
    lane_of = lax.broadcasted_iota(jnp.int32, (ND, 128), 1)
    details = jnp.zeros((ND, 128), F32)
    for k, row in enumerate((slots, ids, lengths)):
        column = jnp.sum(jnp.where(order, row[...].astype(F32), 0.0), axis=1, keepdims=True)
        details = jnp.where(lane_of == k, column, details)
    TF[:, TSUB * J, :] = details
    slabs[...] = TF[...].astype(BF16)

    for j, yy in ys_:
        rcopy(slabs.at[pl.ds(yy * NZ, NZ)], T1.at[y], tl_s.at[0, j], tl_r.at[0, y], dev(yy=yy)).start()
    T1[y] = slabs[pl.ds(y * NZ, NZ)]

    tg[0:KT] = taps_in[0]
    tg[KT : KT + 1] = gain_in[...]
    gain8[...] = jnp.broadcast_to(gain_in[...], gain8.shape)
    for j, xx in xs_:
        rcopy(tg.at[:, cols(xx)], TAPS.at[c, x], tg_s.at[0, j], tg_r.at[0, x], dev(xx=xx)).start()
        rcopy(gain8, GAIN.at[c, x], tg_s.at[1, j], tg_r.at[1, x], dev(xx=xx)).start()
    TAPS[c, x] = tg[:, cols(x)]
    GAIN[c, x] = gain8[...]

    for j, yy in ys_:
        rcopy(slabs.at[pl.ds(yy * NZ, NZ)], T1.at[yy], tl_s.at[0, j], tl_r.at[0, yy], dev(yy=yy)).wait()
    for j, zz in zs_:
        rcopy(T1.at[:, zz], T2.at[z], tl_s.at[1, j], tl_r.at[1, z], dev(zz=zz)).start()
    T2[z] = T1[:, z]

    for copy in own_copies:
        copy.wait()
    for j, xx in xs_:
        rcopy(W.at[c, x, y, z], W.at[c, xx, y, z], xw_s.at[j], xw_r.at[xx], dev(xx=xx)).wait()

    dirs = ((0, 1), (1, -1))

    class Rings:
        def __init__(self, cc):
            self.cc = cc
            self.n1, self.n2 = (NY, NZ) if cc == 0 else (NZ, NY)
            self.me1, self.me2 = (y, z) if cc == 0 else (z, y)
            self.h1, self.h2 = self.n1 // 2, self.n2 // 2
            self.m = self.n1 // 2

        def to(self, ring, sgn):
            me, n = (self.me1, self.n1) if ring == 1 else (self.me2, self.n2)
            pos = (me + sgn + n) % n
            return dev(yy=pos) if (ring == 1) == (self.cc == 0) else dev(zz=pos)

        def near(self, u, d):
            return u == d

    def at(e):
        return 1 + e // 2, e % 2

    class Gather(Rings):
        def block1(self, i, b, u):
            return W.at[0, i, b, z, :, half(u)] if self.cc == 0 else W.at[1, i, y, b, :, half(u)]

        def block2(self, i, b, u):
            part = pl.ds(u * self.m, self.m)
            return W.at[0, i, part, b] if self.cc == 0 else W.at[1, i, b, part]

        def step(self, ring, t, u, i):
            n, me, last, block, send, recv = (
                (self.n1, self.me1, self.h1, self.block1, p1_s, p1_r)
                if ring == 1
                else (self.n2, self.me2, self.h2, self.block2, p2_s, p2_r)
            )
            for d, sgn in dirs:
                held = block(i, (me - sgn * t + 2 * n) % n, u)

                def copy(k):
                    return rcopy(held, held, send.at[i, d, u], recv.at[i, d, u, k], self.to(ring, sgn))

                def arrive():
                    copy(t - 1).wait_recv()
                    if ring == 2:
                        rcopy(held, held, sw_s.at[i], sw_r.at[i], sib).start()

                if isinstance(t, int) and t == 0:
                    if ring == 2 and d == 0:
                        rcopy(held, held, sw_s.at[i], sw_r.at[i], sib).start()
                    if last > 1 or self.near(u, d):
                        copy(0).start()
                    continue
                if self.near(u, d):
                    pl.when(t <= last)(arrive)
                    pl.when(t < last)(lambda: copy(t).start())
                else:
                    pl.when(t < last)(arrive)
                    pl.when(t < last - 1)(lambda: copy(t).start())

        def begin(self, ring, i):
            for u in range(2):
                self.step(ring, 0, u, i)

        def drain(self):
            def one(i, _):
                for u in range(2):
                    for d in range(2):
                        far = 0 if self.near(u, d) else 1
                        k1, k2 = self.h1 - far, self.h2 - far
                        part = pl.ds(0, self.m)
                        if k1 > 0:
                            sent = W.at[0, i, 0:k1, 0, :, half(u)] if self.cc == 0 else W.at[1, i, 0, 0:k1, :, half(u)]
                            rcopy(sent, sent, p1_s.at[i, d, u], p1_r.at[i, d, u, 0], sib).wait_send()
                        if k2 > 0:
                            sent = W.at[0, i, part, 0:k2] if self.cc == 0 else W.at[1, i, 0:k2, part]
                            rcopy(sent, sent, p2_s.at[i, d, u], p2_r.at[i, d, u, 0], sib).wait_send()
                return 0

            lax.fori_loop(0, NX, one, 0)

    gathers = [Gather(cc) for cc in range(CORES)]

    def each(rings, f):
        for cc in range(CORES):
            pl.when(c == cc)(functools.partial(f, rings[cc]))

    def begin(g):
        if g.cc == 1:
            for i in range(NX):
                g.begin(1, i)
            for e in range(2 * g.h1):
                for i in range(NX):
                    g.step(1, *at(e), i)
                    if e == 2 * g.h1 - 1 and i == 0:
                        g.begin(2, 0)
            return
        g.begin(1, 0)
        for e in range(2 * g.h1):
            g.step(1, *at(e), 0)
        g.begin(2, 0)
        for i in range(1, NX):
            g.begin(1, i)

    def go_on(low, high, g):
        for e in range(low, high):
            if e < 2 * g.h2:
                g.step(2, *at(e), 0)
            if g.cc == 1:
                if e == 1 and NX > 1:
                    g.begin(2, 1)
                continue
            if e < 2 * g.h1:
                for i in range(1, NX):
                    g.step(1, *at(e), i)
            if e == 2 * g.h1 - 1 and NX > 1:
                g.begin(2, 1)
            if 0 <= e - 4 < 2 * g.h2 and NX > 1:
                g.step(2, *at(e - 4), 1)
        if g.cc == 0 and high == 8 and NX > 2:
            g.begin(2, 2)

    each(gathers, begin)

    for j, xx in xs_:
        rcopy(tg.at[:, cols(xx)], TAPS.at[c, xx], tg_s.at[0, j], tg_r.at[0, xx], dev(xx=xx)).wait()
        rcopy(gain8, GAIN.at[c, xx], tg_s.at[1, j], tg_r.at[1, xx], dev(xx=xx)).wait()
    taps_out = rcopy(TAPS.at[c], TAPS.at[c], st_s.at[0], st_r.at[0], sib)
    gain_out = rcopy(GAIN.at[c], GAIN.at[c], st_s.at[1], st_r.at[1], sib)
    taps_out.start()
    gain_out.start()

    for j, zz in zs_:
        rcopy(T1.at[:, zz], T2.at[zz], tl_s.at[1, j], tl_r.at[1, zz], dev(zz=zz)).wait()
    TF[...] = T2[...].astype(F32).reshape(TF.shape)
    for f in range(TSUB):
        for j in range(J):
            EA[f * ND : (f + 1) * ND, j * 128 : (j + 1) * 128] = TF[:, f * J + j, :]

    each(gathers, functools.partial(go_on, 0, 1))
    stacked = EA[...].astype(BF16)
    embedded = [
        jnp.dot(stacked, G[0, k].reshape(J * 128, 2 * DX), preferred_element_type=F32).astype(BF16)
        for k in range(NX // 2)
    ]
    embedded = jnp.concatenate(embedded, axis=1)
    detail = TF[:, TSUB * J, :]
    rows = TSUB * ND
    detail_rows = jnp.concatenate([detail] * TSUB, axis=0)
    slot, label, length = (detail_rows[:, k : k + 1] for k in range(3))
    frame_in_tile = (lax.broadcasted_iota(jnp.int32, (rows, 1), 0) // ND).astype(F32)
    time_lane = lax.broadcasted_iota(jnp.int32, (rows, FRM), 1)
    first_slot = (c * (FRM // TSUB)).astype(F32)
    pick = (slot - first_slot == (time_lane // TSUB).astype(F32)) & (
        frame_in_tile == (time_lane % TSUB).astype(F32)
    )
    pick = pick.astype(F32).astype(BF16)
    placed = lax.dot_general(pick, embedded, (((0,), (0,)), ((), ())), preferred_element_type=F32).astype(BF16)
    for b in range(NX):
        X[0, b] = placed[:, b * DX : (b + 1) * DX]
    each(gathers, functools.partial(go_on, 1, 3))

    code_rows = jnp.broadcast_to(jnp.where(frame_in_tile < length, label, -1.0), (rows, 128)).astype(BF16)
    code = lax.dot_general(pick, code_rows, (((0,), (0,)), ((), ())), preferred_element_type=F32)
    CP[...] = jnp.full(CP.shape, -2.0, F32)
    CP[16 : 16 + FRM] = code
    for k in range(KT):
        start = 16 - reach + k
        MASK[k] = jnp.where((CP[start : start + FRM] == code) & (code >= 0.0), 1.0, 0.0)
    edge = jnp.zeros((16, DX), F32)
    SP[0:16] = edge
    SP[16 + FRM :] = edge

    def clear(s, _):
        GL[s, 0:16] = edge
        GL[s, 16 + FRM :] = edge
        return 0

    lax.fori_loop(0, SECT, clear, 0)
    each(gathers, functools.partial(go_on, 3, 8))

    rcopy(TAPS.at[1 - c], TAPS.at[1 - c], st_s.at[0], st_r.at[0], sib).wait_recv()
    rcopy(GAIN.at[1 - c], GAIN.at[1 - c], st_s.at[1], st_r.at[1], sib).wait_recv()

    def pump(s, q):
        pair = s // 2 + 1
        u = q // 2

        def run(g, t, u, i):
            pl.when((i < NX) & (t <= g.h2))(lambda: g.step(2, t, u, i))

        def first(g):
            if q % 2 == 0:
                run(g, 3 + s % 2, u, pair)
            else:
                run(g, 1 + s % 2, u, pair + 1)
            if q == 3:
                pl.when((s % 2 == 1) & (pair + 2 < NX))(lambda: g.begin(2, pair + 2))

        def second(g):
            if q % 2 == 0:
                run(g, 1 + s % 2, u, pair)
            if q == 3:
                pl.when((s % 2 == 0) & (pair + 1 < NX))(lambda: g.begin(2, pair + 1))

        each(gathers, lambda g: first(g) if g.cc == 0 else second(g))

    def statistics(s):
        blocks = [X[s, b].astype(F32) for b in range(NX)]
        mean = sum(jnp.sum(v, axis=1, keepdims=True) for v in blocks) * (1.0 / D)
        shifted = [v - mean for v in blocks]
        spread = sum(jnp.sum(v * v, axis=1, keepdims=True) for v in shifted) * (1.0 / D)
        return mean, shifted, lax.rsqrt(spread + EPSILON)

    def weight(s):
        return W[s % 2, s // 2].reshape(D, 2 * DX)

    def forward(s, _):
        @pl.when(s % 2 != c)
        def _():
            there = W.at[1 - c, s // 2]
            rcopy(there, there, sw_s.at[s // 2], sw_r.at[s // 2], sib).wait_recv()

        @pl.when(s > 0)
        def _():
            for j, xx in xs_:
                rcopy(X.at[s, x], X.at[s, xx], xf_s.at[s, j], xf_r.at[s, xx], dev(xx=xx)).wait()

        _, shifted, inverse = statistics(s)
        for b in range(NX):
            gain = GAIN[s % 2, s // 2, 0:1, b * DX : (b + 1) * DX]
            NT[s, :, b * DX : (b + 1) * DX] = (shifted[b] * inverse * gain).astype(BF16)

        @pl.when(s % 2 != c)
        def _():
            rcopy(NT.at[s], NS.at[s // 2], sn_s.at[s // 2], sn_r.at[s // 2], sib).start()

        pump(s, 0)
        both = jnp.dot(NT[s], weight(s), preferred_element_type=F32)
        value, gate = both[:, :DX], both[:, DX:]
        sig = jax.nn.sigmoid(gate)
        V[s] = value
        SG[s] = sig
        GL[s, 16 : 16 + FRM] = value * sig
        pump(s, 1)
        for tile in range(lanes_x):
            if tile == lanes_x // 2:
                pump(s, 2)
            lane = slice(tile * 128, (tile + 1) * 128)
            conv = jnp.zeros((FRM, 128), F32)
            for k in range(KT):
                start = 16 - reach + k
                conv = conv + GL[s, start : start + FRM, lane] * MASK[k] * TAPS[s % 2, s // 2, k : k + 1, lane]
            CV[s, :, lane] = conv

            @pl.when(s < SECT - 1)
            def _():
                result = X[s, x, :, lane].astype(F32) + conv * jax.nn.sigmoid(conv)
                X[s + 1, x, :, lane] = result.astype(BF16)
                piece = X.at[s + 1, x, :, lane]
                for j, xx in far_first:
                    rcopy(piece, piece, xf_s.at[s + 1, j], xf_r.at[s + 1, x], dev(xx=xx)).start()

        pump(s, 3)
        return 0

    lax.fori_loop(0, SECT, forward, 0)

    GC[...] = CT[...].astype(F32)

    def weight_gradient(s):
        i = s // 2
        rcopy(NT.at[s], NS.at[i], sn_s.at[i], sn_r.at[i], sib).wait_recv()
        rcopy(GO.at[s], GS.at[i], sg_s.at[i], sg_r.at[i], sib).wait_recv()
        grads = jnp.concatenate([GO[s], GS[i]], axis=0)
        width = D // NY
        for part in range(NY):
            lane = slice(part * width, (part + 1) * width)
            normed = jnp.concatenate([NT[s, :, lane], NS[i, :, lane]], axis=0)
            product = lax.dot_general(normed, grads, (((0,), (0,)), ((), ())), preferred_element_type=F32)
            G[i, part] = product.astype(BF16).reshape(NZ, R, 2 * DX)

    class Scatter(Rings):
        def own2(self, i, b, u):
            part = pl.ds(u * self.m, self.m)
            return G.at[i, part, b] if self.cc == 0 else G.at[i, b, part]

        def own1(self, i, b, u):
            return RA.at[i, 0, (self.h2 - 1) * self.n1 + b, :, half(u)]

        def held2(self, i, d, t, u):
            return RA.at[i, d, pl.ds((t - 1) * self.n1 + u * self.m, self.m)]

        def held1(self, i, d, t, u):
            return RB.at[i, d, t - 1, :, half(u)]

        def step(self, ring, t, u, i):
            n, me, last, own, held, send, recv = (
                (self.n1, self.me1, self.h1, self.own1, self.held1, rb_s, rb_r)
                if ring == 1
                else (self.n2, self.me2, self.h2, self.own2, self.held2, ra_s, ra_r)
            )
            for d, sgn in dirs:
                mine = own(i, (me + sgn * (last - t) + 2 * n) % n, u)
                near = self.near(u, d)

                def onward(src):
                    return rcopy(src, held(i, d, t + 1, u), send.at[i, d, u], recv.at[i, d, u, t], self.to(ring, sgn))

                if isinstance(t, int) and t == 0:
                    if near:
                        onward(mine).start()
                    continue

                def arrive():
                    there = held(i, d, t, u)
                    rcopy(there, there, send.at[i, d, u], recv.at[i, d, u, t - 1], self.to(ring, sgn)).wait_recv()

                    @pl.when(t < last)
                    def _():
                        there[...] = (there[...].astype(F32) + mine[...].astype(F32)).astype(BF16)
                        onward(there).start()

                if near:
                    arrive()
                else:
                    pl.when((t == 1) & (t < last))(lambda: onward(mine).start())
                    pl.when(t > 1)(arrive)

            @pl.when(t == last)
            def _():
                total = own(i, me, u)[...].astype(F32)
                for d in range(2):
                    if last > 1 or self.near(u, d):
                        total = total + held(i, d, last, u)[...].astype(F32)
                if ring == 1:
                    FS[i, :, half(u)] = total.astype(BF16)
                else:
                    held(i, 0, last, u)[...] = total.astype(BF16)

        def begin(self, ring, i):
            for u in range(2):
                self.step(ring, 0, u, i)

        def drain(self):
            def one(i, _):
                for u in range(2):
                    for d in range(2):
                        far = 0 if self.near(u, d) else 1
                        k1, k2 = self.h1 - far, self.h2 - far
                        if k1 > 0:
                            sent = RB.at[i, d, 0:k1, :, half(u)]
                            rcopy(sent, sent, rb_s.at[i, d, u], rb_r.at[i, d, u, 0], sib).wait_send()
                        if k2 > 0:
                            sent = RA.at[i, d, 0 : k2 * self.m]
                            rcopy(sent, sent, ra_s.at[i, d, u], ra_r.at[i, d, u, 0], sib).wait_send()
                return 0

            lax.fori_loop(0, NX, one, 0)

    scatters = [Scatter(cc) for cc in range(CORES)]

    both_parts = (0, 1)
    plan = {
        (0, 0): {
            0: [(2, 2, (0,), 1)],
            1: [(2, 4, (1,), 2), (1, 0, None, 2)],
            2: [(2, 2, (1,), 1)],
            3: [(2, 3, (0,), 1)],
        },
        (0, 1): {
            0: [(2, 1, (0,), 1)],
            1: [(2, 3, (1,), 2), (1, 1, both_parts, 3)],
            2: [(2, 1, (1,), 1)],
            3: [(2, 4, (0,), 2), (1, 2, both_parts, 3)],
        },
        (1, 0): {
            0: [],
            1: [(2, 1, (0,), 0), (1, 1, both_parts, 1)],
            2: [],
            3: [(2, 1, (1,), 0), (1, 2, both_parts, 1)],
        },
        (1, 1): {
            0: [],
            1: [(2, 2, (0,), 1), (1, 3, both_parts, 2)],
            2: [],
            3: [(2, 2, (1,), 1), (1, 4, both_parts, 2), (1, 0, None, 1)],
        },
    }

    def pump_back(s, q):
        def one(g):
            for parity in range(2):
                for ring, t, parts, ahead in plan[g.cc, parity][q]:
                    if t <= (g.h1 if ring == 1 else g.h2):
                        pair = s // 2 + ahead

                        @pl.when((s % 2 == parity) & (pair < NX))
                        def _():
                            if t == 0:
                                g.begin(ring, pair)
                            else:
                                for u in parts:
                                    g.step(ring, t, u, pair)

        each(scatters, one)

    def backward(step, _):
        s = SECT - 1 - step
        par, i = s % 2, s // 2
        conv = CV[s]
        sig_conv = jax.nn.sigmoid(conv)
        seed = GC[...]
        SP[16 : 16 + FRM] = seed * (sig_conv * (1.0 + conv * (1.0 - sig_conv)))
        for tile in range(lanes_x):
            lane = slice(tile * 128, (tile + 1) * 128)
            total = jnp.zeros((FRM, 128), F32)
            for k in range(KT):
                start = 16 - reach + k
                total = total + SP[start : start + FRM, lane] * MASK[k] * TAPS[par, i, KT - 1 - k : KT - k, lane]
            grad_value = total * SG[s, :, lane]
            grad_gate = grad_value * V[s, :, lane] * (1.0 - SG[s, :, lane])
            GO[s, :, lane] = grad_value.astype(BF16)
            GO[s, :, DX + tile * 128 : DX + (tile + 1) * 128] = grad_gate.astype(BF16)

        @pl.when(par != c)
        def _():
            rcopy(GO.at[s], GS.at[i], sg_s.at[i], sg_r.at[i], sib).start()

        pump_back(s, 0)
        mean, shifted, inverse = statistics(s)
        for b in range(NX):
            XH[b] = shifted[b] * inverse
        sum_a = jnp.zeros((FRM, 1), F32)
        sum_b = jnp.zeros((FRM, 1), F32)
        per = NY // NX
        for j, xx in far_first + [(0, x)]:
            rows_w = W[par, i, pl.ds(xx * per, per)].reshape(DX, 2 * DX)
            block = lax.dot_general(GO[s], rows_w, (((1,), (1,)), ((), ())), preferred_element_type=F32)
            if j == 0:
                PF[...] = block
            else:
                MS[xx] = block.astype(BF16)
                rcopy(MS.at[xx], MR.at[par, x], xb_s.at[s, j], xb_r.at[s, x], dev(xx=xx)).start()
            scaled = block * GAIN[par, i, 0:1, cols(xx)]
            sum_a = sum_a + jnp.sum(scaled, axis=1, keepdims=True)
            sum_b = sum_b + jnp.sum(scaled * XH[xx], axis=1, keepdims=True)
        lane_id = lax.broadcasted_iota(jnp.int32, (FRM, 128), 1)
        high_a, high_b = sum_a.astype(BF16).astype(F32), sum_b.astype(BF16).astype(F32)
        packed = jnp.where(lane_id == 0, high_a, 0.0)
        packed = jnp.where(lane_id == 1, sum_a - high_a, packed)
        packed = jnp.where(lane_id == 2, high_b, packed)
        MT[par, x] = jnp.where(lane_id == 3, sum_b - high_b, packed).astype(BF16)
        for j, xx in far_first:
            rcopy(MT.at[par, x], MT.at[par, x], xt_s.at[s, j], xt_r.at[s, x], dev(xx=xx)).start()

        pump_back(s, 1)
        @pl.when(par == c)
        def _():
            weight_gradient(s)
            each(scatters, lambda g: g.begin(2, i))

        for tile in range(lanes_x):
            lane = slice(tile * 128, (tile + 1) * 128)
            spread = SP[16 : 16 + FRM, lane]
            for k in range(KT):
                start = 16 - reach + k
                TT[s, k : k + 1, lane] = jnp.sum(
                    spread * GL[s, start : start + FRM, lane] * MASK[k], axis=0, keepdims=True
                )

        pump_back(s, 2)
        for j, xx in xs_:
            rcopy(MS.at[xx], MR.at[par, xx], xb_s.at[s, j], xb_r.at[s, xx], dev(xx=xx)).wait()
            rcopy(MT.at[par, xx], MT.at[par, xx], xt_s.at[s, j], xt_r.at[s, xx], dev(xx=xx)).wait()
        total = PF[...]
        for j, xx in xs_:
            total = total + MR[par, xx].astype(F32)
            packed = MT[par, xx].astype(F32)
            sum_a = sum_a + packed[:, 0:1] + packed[:, 1:2]
            sum_b = sum_b + packed[:, 2:3] + packed[:, 3:4]
        xhat = XH[x]
        TT[s, KT : KT + 1, :] = jnp.sum(total * xhat, axis=0, keepdims=True)
        gain = GAIN[par, i, 0:1, cols(x)]
        grad_in = inverse * (total * gain - sum_a * (1.0 / D) - xhat * (sum_b * (1.0 / D)))
        GC[...] = (GC[...] + grad_in).astype(BF16).astype(F32)
        pump_back(s, 3)
        return 0

    lax.fori_loop(0, SECT, backward, 0)

    for i in range(NX):
        rcopy(TT.at[2 * i + 1 - c], TS.at[i], tt_s.at[4, i], tt_r.at[4, i], sib).start()

    def tail(low, high, g):
        done = 0 if g.cc == 0 else 2
        late = {0: 5, 2: 6, 3: 7} if g.cc == 0 and NX > 1 else {}
        for e in range(low, high):
            if late.get(e, 8) < 2 * g.h2:
                g.step(2, *at(late[e]), 1)
            if done <= e < 2 * g.h2:
                g.step(2, *at(e), 0)
            if g.cc == 0:
                if NX > 2 and e < 2 * g.h1:
                    g.step(1, *at(e), 2)
                if NX > 1 and e == 3:
                    g.begin(1, 1)
                if NX > 1 and 0 <= e - 4 < 2 * g.h1:
                    g.step(1, *at(e - 4), 1)
            elif NX > 1 and 4 <= e < 2 * g.h1:
                g.step(1, *at(e), 1)
            if e == 2 * g.h2 - 1:
                g.begin(1, 0)
            if 0 <= e - 2 * g.h2 < 2 * g.h1:
                g.step(1, *at(e - 2 * g.h2), 0)

    each(scatters, functools.partial(tail, 0, 2))

    for i in range(NX):
        rcopy(TT.at[2 * i + 1 - c], TS.at[i], tt_s.at[4, i], tt_r.at[4, i], sib).wait()
    TY[...] = jnp.zeros(TY.shape, F32)
    for i in range(NX):
        summed = TT[2 * i + c] + TS[i]
        for r in range(KT + 1):
            TY[r // NZ, r % NZ, i : i + 1, :] = summed[r : r + 1]
    for j, yy in ys_:
        rcopy(TY.at[yy], TYR.at[y], tt_s.at[0, j], tt_r.at[0, y], dev(yy=yy)).start()
    TYR[y] = TY[y]
    each(scatters, functools.partial(tail, 2, 4))
    for j, yy in ys_:
        rcopy(TY.at[yy], TYR.at[yy], tt_s.at[0, j], tt_r.at[0, yy], dev(yy=yy)).wait()
    TY[y] = sum(TYR[k] for k in range(NY))
    for j, zz in zs_:
        rcopy(TY.at[y, zz], TZR.at[z], tt_s.at[1, j], tt_r.at[1, z], dev(zz=zz)).start()
    TZR[z] = TY[y, z]
    each(scatters, functools.partial(tail, 4, 6))
    for j, zz in zs_:
        rcopy(TY.at[y, zz], TZR.at[zz], tt_s.at[1, j], tt_r.at[1, zz], dev(zz=zz)).wait()
    TX[...] = sum(TZR[k] for k in range(NZ))
    for j, xx in xs_:
        rcopy(TX, TXR.at[x], tt_s.at[2, j], tt_r.at[2, x], dev(xx=xx)).start()
    TXR[x] = TX[...]
    each(scatters, functools.partial(tail, 6, 8))
    for j, xx in xs_:
        rcopy(TX, TXR.at[xx], tt_s.at[2, j], tt_r.at[2, xx], dev(xx=xx)).wait()
    TO1[z] = jnp.zeros(TO1.shape[1:], F32)
    mine = lax.broadcasted_iota(jnp.int32, (8, DX), 0) == x
    for b in range(NX):
        row = jnp.sum(jnp.where(mine, TXR[b], 0.0), axis=0, keepdims=True)
        for tile in range(lanes_x):
            k = b * lanes_x + tile
            TO1[z, k : k + 1, :] = row[:, tile * 128 : (tile + 1) * 128]
    for j, zz in zs_:
        rcopy(TO1.at[z], TO1.at[z], tt_s.at[3, j], tt_r.at[3, z], dev(zz=zz)).start()
    each(scatters, functools.partial(tail, 8, 10))
    for j, zz in zs_:
        rcopy(TO1.at[z], TO1.at[zz], tt_s.at[3, j], tt_r.at[3, zz], dev(zz=zz)).wait()
    for j, yy in ys_:
        rcopy(TO1, TO2.at[y], tt_s.at[5, j], tt_r.at[5, y], dev(yy=yy)).start()
    TO2[y] = TO1[...]
    each(scatters, functools.partial(tail, 10, 12))
    for j, xx in xs_:
        rcopy(FS.at[xx], FR.at[x], fin_s.at[j], fin_r.at[x], dev(xx=xx)).start()
    FR[x] = FS[x]
    for j, yy in ys_:
        rcopy(TO1, TO2.at[yy], tt_s.at[5, j], tt_r.at[5, yy], dev(yy=yy)).wait()
    for k in range(D // 128):
        lane = slice(k * 128, (k + 1) * 128)
        for yy in range(NY):
            low, count = yy * NZ, min(NZ, KT - yy * NZ)
            piece = TO2[yy, :, k, :]
            o_taps[0, low : low + count, lane] = piece[:count]
            if count < NZ:
                o_gain[:, lane] = piece[count : count + 1]

    for j, xx in xs_:
        rcopy(FS.at[xx], FR.at[xx], fin_s.at[j], fin_r.at[xx], dev(xx=xx)).wait()
    for b in range(NX):
        o_mix[0, :, b * DX : (b + 1) * DX] = FR[b, :, :DX].astype(F32)
        o_gate[0, :, b * DX : (b + 1) * DX] = FR[b, :, DX:].astype(F32)

    taps_out.wait_send()
    gain_out.wait_send()

    def drain(i, _):
        there = W.at[c, i]
        rcopy(there, there, sw_s.at[i], sw_r.at[i], sib).wait_send()
        rcopy(NT.at[0], NS.at[i], sn_s.at[i], sn_r.at[i], sib).wait_send()
        rcopy(GO.at[0], GS.at[i], sg_s.at[i], sg_r.at[i], sib).wait_send()
        return 0

    lax.fori_loop(0, NX, drain, 0)
    each(gathers, lambda g: g.drain())
    each(scatters, lambda g: g.drain())


def body(
    mel_tiles,
    utt_ids,
    tile_lengths,
    dest_shard,
    dest_slot,
    subsample_weight,
    mixing_weight,
    gate_weight,
    conv_taps,
    norm_gain,
    out_cot,
):
    ND = lax.axis_size("dp")
    SECT = lax.axis_size("pipe")
    NX = SECT // CORES
    NY, NZ = PHYS[ND]
    tiles, TSUB, feats = mel_tiles.shape
    D = subsample_weight.shape[1]
    KT = conv_taps.shape[1]
    R = mixing_weight.shape[1]
    FRM = tiles * TSUB // 2
    J = -(-feats // 128)
    DX = D // NX
    SR = -(-(TSUB * J + 1) // 16) * 16
    dims = dict(X=NX, Y=NY, Z=NZ, D=D, R=R, F=FRM, TSUB=TSUB, J=J, TAPS=KT)

    OR = -(-(D // 128) // 8) * 8
    NR = max(NY, NZ) // 2

    def vm(shape, kind=F32):
        return pltpu.VMEM(shape, kind)

    def sems(*shape):
        return pltpu.SemaphoreType.DMA(shape)

    scratch = [
        vm((2, NX, NY, NZ, R, 2 * DX), BF16),
        vm((2, NX, KT + 1, DX)),
        vm((2, NX, 8, D)),
        vm((KT + 1, D)),
        vm((8, D)),
        vm((tiles, TSUB, feats)),
        vm((ND, SR, 128), BF16),
        vm((NY, NZ, SR, 128), BF16),
        vm((NZ, NY, SR, 128), BF16),
        vm((ND, SR, 128)),
        vm((TSUB * ND, J * 128)),
        vm((FRM + 32, 128)),
        vm((KT, FRM, 128)),
        vm((SECT, NX, FRM, DX), BF16),
        vm((SECT, FRM, D), BF16),
        vm((NX, FRM, D), BF16),
        vm((SECT, FRM + 32, DX)),
        vm((FRM + 32, DX)),
        vm((SECT, FRM, DX)),
        vm((SECT, FRM, DX)),
        vm((SECT, FRM, DX)),
        vm((FRM, DX)),
        vm((FRM, DX), BF16),
        vm((FRM, DX)),
        vm((NX, FRM, DX)),
        vm((SECT, FRM, 2 * DX), BF16),
        vm((NX, FRM, 2 * DX), BF16),
        vm((NX, FRM, DX), BF16),
        vm((2, NX, FRM, DX), BF16),
        vm((2, NX, FRM, 128), BF16),
        vm((NX, NY, NZ, R, 2 * DX), BF16),
        vm((NX, 2, ND // 2, R, 2 * DX), BF16),
        vm((NX, 2, NR, R, 2 * DX), BF16),
        vm((NX, R, 2 * DX), BF16),
        vm((NX, R, 2 * DX), BF16),
        vm((SECT, KT + 1, DX)),
        vm((NX, KT + 1, DX)),
        vm((NY, NZ, 8, DX)),
        vm((NY, NZ, 8, DX)),
        vm((NZ, 8, DX)),
        vm((8, DX)),
        vm((NX, 8, DX)),
        vm((NZ, OR, 128)),
        vm((NY, NZ, OR, 128)),
        sems(3 + NX * NZ),
        sems(NX),
        sems(NX),
        sems(2, NX),
        sems(2, NX),
        sems(2, max(NY, NZ)),
        sems(2, max(NY, NZ)),
        sems(NX, 2, 2),
        sems(NX, 2, 2, NR),
        sems(NX, 2, 2),
        sems(NX, 2, 2, NR),
        sems(NX, 2, 2),
        sems(NX, 2, 2, NR),
        sems(NX, 2, 2),
        sems(NX, 2, 2, NR),
        sems(NX),
        sems(NX),
        sems(2),
        sems(2),
        sems(SECT, NX),
        sems(SECT, NX),
        sems(SECT, NX),
        sems(SECT, NX),
        sems(SECT, NX),
        sems(SECT, NX),
        sems(NX),
        sems(NX),
        sems(NX),
        sems(NX),
        sems(NX),
        sems(NX),
        sems(6, max(NX, NY, NZ)),
        sems(6, max(NX, NY, NZ)),
    ]
    in_vmem = pl.BlockSpec(memory_space=pltpu.VMEM)
    in_any = pl.BlockSpec(memory_space=pl.ANY)
    return pl.pallas_call(
        functools.partial(kernel, dims),
        out_shape=(
            jax.ShapeDtypeStruct((1, R, D), F32),
            jax.ShapeDtypeStruct((1, R, D), F32),
            jax.ShapeDtypeStruct((1, KT, D), F32),
            jax.ShapeDtypeStruct((1, D), F32),
        ),
        in_specs=[in_vmem] * 5 + [in_any] * 2 + [in_vmem] * 2 + [in_any] * 2,
        out_specs=(in_vmem,) * 4,
        scratch_shapes=scratch,
        compiler_params=pltpu.CompilerParams(
            collective_id=0, has_side_effects=True, vmem_limit_bytes=VMEM_LIMIT
        ),
    )(
        mel_tiles,
        utt_ids[None],
        tile_lengths[None],
        dest_shard[None],
        dest_slot[None],
        mixing_weight,
        gate_weight,
        conv_taps,
        norm_gain,
        subsample_weight,
        out_cot,
    )


def solution(mesh):
    in_specs = (
        P("dp", None, None),
        P("dp"),
        P("dp"),
        P("dp"),
        P("dp"),
        P(),
        P("pipe", "dp", None),
        P("pipe", "dp", None),
        P("pipe", None, None),
        P("pipe", None),
        P("dp", None),
    )
    out_specs = (
        P("pipe", "dp", None),
        P("pipe", "dp", None),
        P("pipe", None, None),
        P("pipe", None),
    )
    return jax.shard_map(body, mesh=mesh, in_specs=in_specs, out_specs=out_specs, check_vma=False)
```

```python
import functools

import jax
import jax.numpy as jnp
from jax import lax
from jax.experimental import pallas as pl
from jax.experimental.pallas import tpu as pltpu
from jax.sharding import PartitionSpec as P

PHYS = {32: (4, 8), 8: (2, 4), 4: (2, 2)}
CORES = 2
EPSILON = 1e-05
F32 = jnp.float32
BF16 = jnp.bfloat16
VMEM_LIMIT = 60 * 1024 * 1024


def rcopy(src, dst, send_sem, recv_sem, device):
    return pltpu.make_async_remote_copy(
        src_ref=src,
        dst_ref=dst,
        send_sem=send_sem,
        recv_sem=recv_sem,
        device_id=device,
        device_id_type=pl.DeviceIdType.MESH,
    )


def kernel(
    dims,
    mel,
    ids,
    lengths,
    shards,
    slots,
    mixing,
    gating,
    taps_in,
    gain_in,
    sub,
    cot,
    o_mix,
    o_gate,
    o_taps,
    o_gain,
    W,
    TAPS,
    GAIN,
    tg,
    gain8,
    MF,
    slabs,
    T1,
    T2,
    TF,
    EA,
    CP,
    MASK,
    X,
    NT,
    NS,
    GL,
    SP,
    V,
    SG,
    CV,
    GC,
    CT,
    PF,
    XH,
    ST,
    GO,
    GS,
    MS,
    MR,
    MT,
    G,
    RA,
    RB,
    FS,
    FR,
    TT,
    TS,
    TY,
    TYR,
    TZR,
    TX,
    TXR,
    TO1,
    TO2,
    lw_s,
    xw_s,
    xw_r,
    tg_s,
    tg_r,
    tl_s,
    tl_r,
    p1_s,
    p1_r,
    p2_s,
    p2_r,
    ra_s,
    ra_r,
    rb_s,
    rb_r,
    sw_s,
    sw_r,
    st_s,
    st_r,
    xf_s,
    xf_r,
    xb_s,
    xb_r,
    xt_s,
    xt_r,
    sn_s,
    sn_r,
    sg_s,
    sg_r,
    fin_s,
    fin_r,
    tt_s,
    tt_r,
):
    NX, NY, NZ = dims["X"], dims["Y"], dims["Z"]
    D, R, FRM, TSUB, J, KT = (dims[k] for k in ("D", "R", "F", "TSUB", "J", "TAPS"))
    DX = D // NX
    ND = NY * NZ
    SECT = 2 * NX
    reach = KT // 2
    lanes_x = DX // 128

    dpi = lax.axis_index("dp")
    pipe = lax.axis_index("pipe")
    x, c = pipe // CORES, pipe % CORES
    y, z = dpi // NZ, dpi % NZ

    def dev(yy=None, zz=None, xx=None, cc=None):
        yy = y if yy is None else yy
        zz = z if zz is None else zz
        xx = x if xx is None else xx
        cc = c if cc is None else cc
        return {"dp": yy * NZ + zz, "pipe": xx * CORES + cc}

    sib = dev(cc=1 - c)
    xs_ = [(j, (x + j) % NX) for j in range(1, NX)]
    far_first = sorted(xs_, key=lambda item: -min(item[0], NX - item[0]))
    ys_ = [(j, (y + j) % NY) for j in range(1, NY)]
    zs_ = [(j, (z + j) % NZ) for j in range(1, NZ)]

    def half(h):
        return pl.ds(h * DX, DX)

    def cols(b):
        return pl.ds(pl.multiple_of(b * DX, 128), DX)

    barrier = pltpu.get_barrier_semaphore()
    peers = [sib]
    peers += [dev(xx=xx) for _, xx in xs_]
    peers += [dev(yy=yy) for _, yy in ys_]
    peers += [dev(zz=zz) for _, zz in zs_]
    for peer in peers:
        pl.semaphore_signal(barrier, inc=1, device_id=peer, device_id_type=pl.DeviceIdType.MESH)
    pl.semaphore_wait(barrier, len(peers))

    for j, xx in xs_:
        rcopy(mixing.at[0, :, cols(xx)], W.at[c, x, y, z, :, half(0)], xw_s.at[j], xw_r.at[x], dev(xx=xx)).start()
        rcopy(gating.at[0, :, cols(xx)], W.at[c, x, y, z, :, half(1)], xw_s.at[j], xw_r.at[x], dev(xx=xx)).start()
    own_copies = [
        pltpu.make_async_copy(cot.at[pl.ds(pl.multiple_of(c * FRM, 16), FRM), cols(x)], CT, lw_s.at[2]),
        pltpu.make_async_copy(mixing.at[0, :, cols(x)], W.at[c, x, y, z, :, half(0)], lw_s.at[0]),
        pltpu.make_async_copy(gating.at[0, :, cols(x)], W.at[c, x, y, z, :, half(1)], lw_s.at[1]),
    ]
    feats = sub.shape[0]
    for k in range(NX // 2):
        for b in range(NZ):
            count = max(0, min(feats - b * R, R))
            if count < R:
                G[0, k, b, count:] = jnp.zeros((R - count, 2 * DX), BF16)
            if count > 0:
                part = sub.at[b * R : b * R + count, k * 2 * DX : (k + 1) * 2 * DX]
                own_copies.append(pltpu.make_async_copy(part, G.at[0, k, b, 0:count], lw_s.at[3 + k * NZ + b]))
    for copy in own_copies:
        copy.start()

    MF[...] = mel[...].astype(F32)
    order = shards[...] == lax.broadcasted_iota(jnp.int32, (ND, ND), 0)
    order_bf = order.astype(F32).astype(BF16)
    TF[...] = jnp.zeros(TF.shape, F32)
    for f in range(TSUB):
        moved = jnp.dot(order_bf, MF[:, f, :].astype(BF16), preferred_element_type=F32)
        for j in range(J):
            wide = min(128, feats - j * 128)
            TF[:, f * J + j, :wide] = moved[:, j * 128 : j * 128 + wide]
    lane_of = lax.broadcasted_iota(jnp.int32, (ND, 128), 1)
    details = jnp.zeros((ND, 128), F32)
    for k, row in enumerate((slots, ids, lengths)):
        column = jnp.sum(jnp.where(order, row[...].astype(F32), 0.0), axis=1, keepdims=True)
        details = jnp.where(lane_of == k, column, details)
    TF[:, TSUB * J, :] = details
    slabs[...] = TF[...].astype(BF16)

    for j, yy in ys_:
        rcopy(slabs.at[pl.ds(yy * NZ, NZ)], T1.at[y], tl_s.at[0, j], tl_r.at[0, y], dev(yy=yy)).start()
    T1[y] = slabs[pl.ds(y * NZ, NZ)]

    tg[0:KT] = taps_in[0]
    tg[KT : KT + 1] = gain_in[...]
    gain8[...] = jnp.broadcast_to(gain_in[...], gain8.shape)
    for j, xx in xs_:
        rcopy(tg.at[:, cols(xx)], TAPS.at[c, x], tg_s.at[0, j], tg_r.at[0, x], dev(xx=xx)).start()
        rcopy(gain8, GAIN.at[c, x], tg_s.at[1, j], tg_r.at[1, x], dev(xx=xx)).start()
    TAPS[c, x] = tg[:, cols(x)]
    GAIN[c, x] = gain8[...]

    for j, yy in ys_:
        rcopy(slabs.at[pl.ds(yy * NZ, NZ)], T1.at[yy], tl_s.at[0, j], tl_r.at[0, yy], dev(yy=yy)).wait()
    for j, zz in zs_:
        rcopy(T1.at[:, zz], T2.at[z], tl_s.at[1, j], tl_r.at[1, z], dev(zz=zz)).start()
    T2[z] = T1[:, z]

    for copy in own_copies:
        copy.wait()
    for j, xx in xs_:
        rcopy(W.at[c, x, y, z], W.at[c, xx, y, z], xw_s.at[j], xw_r.at[xx], dev(xx=xx)).wait()

    dirs = ((0, 1), (1, -1))

    class Rings:
        def __init__(self, cc):
            self.cc = cc
            self.n1, self.n2 = (NY, NZ) if cc == 0 else (NZ, NY)
            self.me1, self.me2 = (y, z) if cc == 0 else (z, y)
            self.h1, self.h2 = self.n1 // 2, self.n2 // 2
            self.m = self.n1 // 2

        def to(self, ring, sgn):
            me, n = (self.me1, self.n1) if ring == 1 else (self.me2, self.n2)
            pos = (me + sgn + n) % n
            return dev(yy=pos) if (ring == 1) == (self.cc == 0) else dev(zz=pos)

        def near(self, u, d):
            return u == d

    def at(e):
        return 1 + e // 2, e % 2

    class Gather(Rings):
        def block1(self, i, b, u):
            return W.at[0, i, b, z, :, half(u)] if self.cc == 0 else W.at[1, i, y, b, :, half(u)]

        def block2(self, i, b, u):
            part = pl.ds(u * self.m, self.m)
            return W.at[0, i, part, b] if self.cc == 0 else W.at[1, i, b, part]

        def step(self, ring, t, u, i):
            n, me, last, block, send, recv = (
                (self.n1, self.me1, self.h1, self.block1, p1_s, p1_r)
                if ring == 1
                else (self.n2, self.me2, self.h2, self.block2, p2_s, p2_r)
            )
            for d, sgn in dirs:
                held = block(i, (me - sgn * t + 2 * n) % n, u)

                def copy(k):
                    return rcopy(held, held, send.at[i, d, u], recv.at[i, d, u, k], self.to(ring, sgn))

                def arrive():
                    copy(t - 1).wait_recv()
                    if ring == 2:
                        rcopy(held, held, sw_s.at[i], sw_r.at[i], sib).start()

                if isinstance(t, int) and t == 0:
                    if ring == 2 and d == 0:
                        rcopy(held, held, sw_s.at[i], sw_r.at[i], sib).start()
                    if last > 1 or self.near(u, d):
                        copy(0).start()
                    continue
                if self.near(u, d):
                    pl.when(t <= last)(arrive)
                    pl.when(t < last)(lambda: copy(t).start())
                else:
                    pl.when(t < last)(arrive)
                    pl.when(t < last - 1)(lambda: copy(t).start())

        def begin(self, ring, i):
            for u in range(2):
                self.step(ring, 0, u, i)

        def drain(self):
            def one(i, _):
                for u in range(2):
                    for d in range(2):
                        far = 0 if self.near(u, d) else 1
                        k1, k2 = self.h1 - far, self.h2 - far
                        part = pl.ds(0, self.m)
                        if k1 > 0:
                            sent = W.at[0, i, 0:k1, 0, :, half(u)] if self.cc == 0 else W.at[1, i, 0, 0:k1, :, half(u)]
                            rcopy(sent, sent, p1_s.at[i, d, u], p1_r.at[i, d, u, 0], sib).wait_send()
                        if k2 > 0:
                            sent = W.at[0, i, part, 0:k2] if self.cc == 0 else W.at[1, i, 0:k2, part]
                            rcopy(sent, sent, p2_s.at[i, d, u], p2_r.at[i, d, u, 0], sib).wait_send()
                return 0

            lax.fori_loop(0, NX, one, 0)

    gathers = [Gather(cc) for cc in range(CORES)]

    def each(rings, f):
        for cc in range(CORES):
            pl.when(c == cc)(functools.partial(f, rings[cc]))

    def begin(g):
        if g.cc == 1:
            for i in range(NX):
                g.begin(1, i)
            for e in range(2 * g.h1):
                for i in range(NX):
                    g.step(1, *at(e), i)
                    if e == 2 * g.h1 - 1 and i == 0:
                        g.begin(2, 0)
            return
        g.begin(1, 0)
        for e in range(2 * g.h1):
            g.step(1, *at(e), 0)
        g.begin(2, 0)
        for i in range(1, NX):
            g.begin(1, i)

    def go_on(low, high, g):
        for e in range(low, high):
            if e < 2 * g.h2:
                g.step(2, *at(e), 0)
            if g.cc == 1:
                if e == 1 and NX > 1:
                    g.begin(2, 1)
                continue
            if e < 2 * g.h1:
                for i in range(1, NX):
                    g.step(1, *at(e), i)
            if e == 2 * g.h1 - 1 and NX > 1:
                g.begin(2, 1)
            if 0 <= e - 4 < 2 * g.h2 and NX > 1:
                g.step(2, *at(e - 4), 1)
        if g.cc == 0 and high == 8 and NX > 2:
            g.begin(2, 2)

    each(gathers, begin)

    for j, xx in xs_:
        rcopy(tg.at[:, cols(xx)], TAPS.at[c, xx], tg_s.at[0, j], tg_r.at[0, xx], dev(xx=xx)).wait()
        rcopy(gain8, GAIN.at[c, xx], tg_s.at[1, j], tg_r.at[1, xx], dev(xx=xx)).wait()
    taps_out = rcopy(TAPS.at[c], TAPS.at[c], st_s.at[0], st_r.at[0], sib)
    gain_out = rcopy(GAIN.at[c], GAIN.at[c], st_s.at[1], st_r.at[1], sib)
    taps_out.start()
    gain_out.start()

    for j, zz in zs_:
        rcopy(T1.at[:, zz], T2.at[zz], tl_s.at[1, j], tl_r.at[1, zz], dev(zz=zz)).wait()
    TF[...] = T2[...].astype(F32).reshape(TF.shape)
    for f in range(TSUB):
        for j in range(J):
            EA[f * ND : (f + 1) * ND, j * 128 : (j + 1) * 128] = TF[:, f * J + j, :]

    each(gathers, functools.partial(go_on, 0, 1))
    stacked = EA[...].astype(BF16)
    embedded = [
        jnp.dot(stacked, G[0, k].reshape(J * 128, 2 * DX), preferred_element_type=F32).astype(BF16)
        for k in range(NX // 2)
    ]
    embedded = jnp.concatenate(embedded, axis=1)
    detail = TF[:, TSUB * J, :]
    rows = TSUB * ND
    detail_rows = jnp.concatenate([detail] * TSUB, axis=0)
    slot, label, length = (detail_rows[:, k : k + 1] for k in range(3))
    frame_in_tile = (lax.broadcasted_iota(jnp.int32, (rows, 1), 0) // ND).astype(F32)
    time_lane = lax.broadcasted_iota(jnp.int32, (rows, FRM), 1)
    first_slot = (c * (FRM // TSUB)).astype(F32)
    pick = (slot - first_slot == (time_lane // TSUB).astype(F32)) & (
        frame_in_tile == (time_lane % TSUB).astype(F32)
    )
    pick = pick.astype(F32).astype(BF16)
    placed = lax.dot_general(pick, embedded, (((0,), (0,)), ((), ())), preferred_element_type=F32).astype(BF16)
    for b in range(NX):
        X[0, b] = placed[:, b * DX : (b + 1) * DX]
    each(gathers, functools.partial(go_on, 1, 3))

    code_rows = jnp.broadcast_to(jnp.where(frame_in_tile < length, label, -1.0), (rows, 128)).astype(BF16)
    code = lax.dot_general(pick, code_rows, (((0,), (0,)), ((), ())), preferred_element_type=F32)
    CP[...] = jnp.full(CP.shape, -2.0, F32)
    CP[16 : 16 + FRM] = code
    for k in range(KT):
        start = 16 - reach + k
        MASK[k] = jnp.where((CP[start : start + FRM] == code) & (code >= 0.0), 1.0, 0.0)
    edge = jnp.zeros((16, DX), F32)
    SP[0:16] = edge
    SP[16 + FRM :] = edge

    def clear(s, _):
        GL[s, 0:16] = edge
        GL[s, 16 + FRM :] = edge
        return 0

    lax.fori_loop(0, SECT, clear, 0)
    each(gathers, functools.partial(go_on, 3, 8))

    rcopy(TAPS.at[1 - c], TAPS.at[1 - c], st_s.at[0], st_r.at[0], sib).wait_recv()
    rcopy(GAIN.at[1 - c], GAIN.at[1 - c], st_s.at[1], st_r.at[1], sib).wait_recv()

    def pump(s, q):
        pair = s // 2 + 1
        u = q // 2

        def run(g, t, u, i):
            pl.when((i < NX) & (t <= g.h2))(lambda: g.step(2, t, u, i))

        def first(g):
            if q % 2 == 0:
                run(g, 3 + s % 2, u, pair)
            else:
                run(g, 1 + s % 2, u, pair + 1)
            if q == 3:
                pl.when((s % 2 == 1) & (pair + 2 < NX))(lambda: g.begin(2, pair + 2))

        def second(g):
            if q % 2 == 0:
                run(g, 1 + s % 2, u, pair)
            if q == 3:
                pl.when((s % 2 == 0) & (pair + 1 < NX))(lambda: g.begin(2, pair + 1))

        each(gathers, lambda g: first(g) if g.cc == 0 else second(g))

    def statistics(s):
        blocks = [X[s, b].astype(F32) for b in range(NX)]
        mean = sum(jnp.sum(v, axis=1, keepdims=True) for v in blocks) * (1.0 / D)
        shifted = [v - mean for v in blocks]
        spread = sum(jnp.sum(v * v, axis=1, keepdims=True) for v in shifted) * (1.0 / D)
        return mean, shifted, lax.rsqrt(spread + EPSILON)

    def weight(s):
        return W[s % 2, s // 2].reshape(D, 2 * DX)

    def forward(s, _):
        @pl.when(s % 2 != c)
        def _():
            there = W.at[1 - c, s // 2]
            rcopy(there, there, sw_s.at[s // 2], sw_r.at[s // 2], sib).wait_recv()

        @pl.when(s > 0)
        def _():
            for j, xx in xs_:
                rcopy(X.at[s, x], X.at[s, xx], xf_s.at[s, j], xf_r.at[s, xx], dev(xx=xx)).wait()

        mean, shifted, inverse = statistics(s)
        ST[s, 0] = jnp.broadcast_to(mean, (FRM, 128))
        ST[s, 1] = jnp.broadcast_to(inverse, (FRM, 128))
        for b in range(NX):
            gain = GAIN[s % 2, s // 2, 0:1, b * DX : (b + 1) * DX]
            NT[s, :, b * DX : (b + 1) * DX] = (shifted[b] * inverse * gain).astype(BF16)

        @pl.when(s % 2 != c)
        def _():
            rcopy(NT.at[s], NS.at[s // 2], sn_s.at[s // 2], sn_r.at[s // 2], sib).start()

        pump(s, 0)
        both = jnp.dot(NT[s], weight(s), preferred_element_type=F32)
        value, gate = both[:, :DX], both[:, DX:]
        sig = jax.nn.sigmoid(gate)
        V[s] = value
        SG[s] = sig
        GL[s, 16 : 16 + FRM] = value * sig
        pump(s, 1)
        for tile in range(lanes_x):
            if tile == lanes_x // 2:
                pump(s, 2)
            lane = slice(tile * 128, (tile + 1) * 128)
            conv = jnp.zeros((FRM, 128), F32)
            for k in range(KT):
                start = 16 - reach + k
                conv = conv + GL[s, start : start + FRM, lane] * MASK[k] * TAPS[s % 2, s // 2, k : k + 1, lane]
            CV[s, :, lane] = conv

            @pl.when(s < SECT - 1)
            def _():
                result = X[s, x, :, lane].astype(F32) + conv * jax.nn.sigmoid(conv)
                X[s + 1, x, :, lane] = result.astype(BF16)
                piece = X.at[s + 1, x, :, lane]
                for j, xx in far_first:
                    rcopy(piece, piece, xf_s.at[s + 1, j], xf_r.at[s + 1, x], dev(xx=xx)).start()

        pump(s, 3)
        return 0

    lax.fori_loop(0, SECT, forward, 0)

    GC[...] = CT[...].astype(F32)

    def weight_gradient(s):
        i = s // 2
        rcopy(NT.at[s], NS.at[i], sn_s.at[i], sn_r.at[i], sib).wait_recv()
        rcopy(GO.at[s], GS.at[i], sg_s.at[i], sg_r.at[i], sib).wait_recv()
        grads = jnp.concatenate([GO[s], GS[i]], axis=0)
        width = D // NY
        for part in range(NY):
            lane = slice(part * width, (part + 1) * width)
            normed = jnp.concatenate([NT[s, :, lane], NS[i, :, lane]], axis=0)
            product = lax.dot_general(normed, grads, (((0,), (0,)), ((), ())), preferred_element_type=F32)
            G[i, part] = product.astype(BF16).reshape(NZ, R, 2 * DX)

    class Scatter(Rings):
        def own2(self, i, b, u):
            part = pl.ds(u * self.m, self.m)
            return G.at[i, part, b] if self.cc == 0 else G.at[i, b, part]

        def own1(self, i, b, u):
            return RA.at[i, 0, (self.h2 - 1) * self.n1 + b, :, half(u)]

        def held2(self, i, d, t, u):
            return RA.at[i, d, pl.ds((t - 1) * self.n1 + u * self.m, self.m)]

        def held1(self, i, d, t, u):
            return RB.at[i, d, t - 1, :, half(u)]

        def step(self, ring, t, u, i):
            n, me, last, own, held, send, recv = (
                (self.n1, self.me1, self.h1, self.own1, self.held1, rb_s, rb_r)
                if ring == 1
                else (self.n2, self.me2, self.h2, self.own2, self.held2, ra_s, ra_r)
            )
            for d, sgn in dirs:
                mine = own(i, (me + sgn * (last - t) + 2 * n) % n, u)
                near = self.near(u, d)

                def onward(src):
                    return rcopy(src, held(i, d, t + 1, u), send.at[i, d, u], recv.at[i, d, u, t], self.to(ring, sgn))

                if isinstance(t, int) and t == 0:
                    if near:
                        onward(mine).start()
                    continue

                def arrive():
                    there = held(i, d, t, u)
                    rcopy(there, there, send.at[i, d, u], recv.at[i, d, u, t - 1], self.to(ring, sgn)).wait_recv()

                    @pl.when(t < last)
                    def _():
                        there[...] = (there[...].astype(F32) + mine[...].astype(F32)).astype(BF16)
                        onward(there).start()

                if near:
                    arrive()
                else:
                    pl.when((t == 1) & (t < last))(lambda: onward(mine).start())
                    pl.when(t > 1)(arrive)

            @pl.when(t == last)
            def _():
                total = own(i, me, u)[...].astype(F32)
                for d in range(2):
                    if last > 1 or self.near(u, d):
                        total = total + held(i, d, last, u)[...].astype(F32)
                if ring == 1:
                    FS[i, :, half(u)] = total.astype(BF16)
                else:
                    held(i, 0, last, u)[...] = total.astype(BF16)

        def begin(self, ring, i):
            for u in range(2):
                self.step(ring, 0, u, i)

        def drain(self):
            def one(i, _):
                for u in range(2):
                    for d in range(2):
                        far = 0 if self.near(u, d) else 1
                        k1, k2 = self.h1 - far, self.h2 - far
                        if k1 > 0:
                            sent = RB.at[i, d, 0:k1, :, half(u)]
                            rcopy(sent, sent, rb_s.at[i, d, u], rb_r.at[i, d, u, 0], sib).wait_send()
                        if k2 > 0:
                            sent = RA.at[i, d, 0 : k2 * self.m]
                            rcopy(sent, sent, ra_s.at[i, d, u], ra_r.at[i, d, u, 0], sib).wait_send()
                return 0

            lax.fori_loop(0, NX, one, 0)

    scatters = [Scatter(cc) for cc in range(CORES)]

    both_parts = (0, 1)
    plan = {
        (0, 0): {
            0: [(2, 2, (0,), 1)],
            1: [(2, 4, (1,), 2), (1, 0, None, 2)],
            2: [(2, 2, (1,), 1)],
            3: [(2, 3, (0,), 1)],
        },
        (0, 1): {
            0: [(2, 1, (0,), 1)],
            1: [(2, 3, (1,), 2), (1, 1, both_parts, 3)],
            2: [(2, 1, (1,), 1)],
            3: [(2, 4, (0,), 2), (1, 2, both_parts, 3)],
        },
        (1, 0): {
            0: [],
            1: [(2, 1, (0,), 0), (1, 1, both_parts, 1)],
            2: [],
            3: [(2, 1, (1,), 0), (1, 2, both_parts, 1)],
        },
        (1, 1): {
            0: [],
            1: [(2, 2, (0,), 1), (1, 3, both_parts, 2)],
            2: [],
            3: [(2, 2, (1,), 1), (1, 4, both_parts, 2), (1, 0, None, 1)],
        },
    }

    def pump_back(s, q):
        def one(g):
            for parity in range(2):
                for ring, t, parts, ahead in plan[g.cc, parity][q]:
                    if t <= (g.h1 if ring == 1 else g.h2):
                        pair = s // 2 + ahead

                        @pl.when((s % 2 == parity) & (pair < NX))
                        def _():
                            if t == 0:
                                g.begin(ring, pair)
                            else:
                                for u in parts:
                                    g.step(ring, t, u, pair)

        each(scatters, one)

    def backward(step, _):
        s = SECT - 1 - step
        par, i = s % 2, s // 2
        conv = CV[s]
        sig_conv = jax.nn.sigmoid(conv)
        seed = GC[...]
        SP[16 : 16 + FRM] = seed * (sig_conv * (1.0 + conv * (1.0 - sig_conv)))
        for tile in range(lanes_x):
            lane = slice(tile * 128, (tile + 1) * 128)
            total = jnp.zeros((FRM, 128), F32)
            for k in range(KT):
                start = 16 - reach + k
                total = total + SP[start : start + FRM, lane] * MASK[k] * TAPS[par, i, KT - 1 - k : KT - k, lane]
            grad_value = total * SG[s, :, lane]
            grad_gate = grad_value * V[s, :, lane] * (1.0 - SG[s, :, lane])
            GO[s, :, lane] = grad_value.astype(BF16)
            GO[s, :, DX + tile * 128 : DX + (tile + 1) * 128] = grad_gate.astype(BF16)

        @pl.when(par != c)
        def _():
            rcopy(GO.at[s], GS.at[i], sg_s.at[i], sg_r.at[i], sib).start()

        pump_back(s, 0)
        mean = jnp.concatenate([ST[s, 0]] * lanes_x, axis=1)
        inverse = jnp.concatenate([ST[s, 1]] * lanes_x, axis=1)
        for b in range(NX):
            XH[b] = (X[s, b].astype(F32) - mean) * inverse
        sum_a = jnp.zeros((FRM, 1), F32)
        sum_b = jnp.zeros((FRM, 1), F32)
        per = NY // NX
        for j, xx in far_first + [(0, x)]:
            rows_w = W[par, i, pl.ds(xx * per, per)].reshape(DX, 2 * DX)
            block = lax.dot_general(GO[s], rows_w, (((1,), (1,)), ((), ())), preferred_element_type=F32)
            if j == 0:
                PF[...] = block
            else:
                MS[xx] = block.astype(BF16)
                rcopy(MS.at[xx], MR.at[par, x], xb_s.at[s, j], xb_r.at[s, x], dev(xx=xx)).start()
            scaled = block * GAIN[par, i, 0:1, cols(xx)]
            sum_a = sum_a + jnp.sum(scaled, axis=1, keepdims=True)
            sum_b = sum_b + jnp.sum(scaled * XH[xx], axis=1, keepdims=True)
        lane_id = lax.broadcasted_iota(jnp.int32, (FRM, 128), 1)
        high_a, high_b = sum_a.astype(BF16).astype(F32), sum_b.astype(BF16).astype(F32)
        packed = jnp.where(lane_id == 0, high_a, 0.0)
        packed = jnp.where(lane_id == 1, sum_a - high_a, packed)
        packed = jnp.where(lane_id == 2, high_b, packed)
        MT[par, x] = jnp.where(lane_id == 3, sum_b - high_b, packed).astype(BF16)
        for j, xx in far_first:
            rcopy(MT.at[par, x], MT.at[par, x], xt_s.at[s, j], xt_r.at[s, x], dev(xx=xx)).start()

        pump_back(s, 1)
        @pl.when(par == c)
        def _():
            weight_gradient(s)
            each(scatters, lambda g: g.begin(2, i))

        for tile in range(lanes_x):
            lane = slice(tile * 128, (tile + 1) * 128)
            spread = SP[16 : 16 + FRM, lane]
            for k in range(KT):
                start = 16 - reach + k
                TT[s, k : k + 1, lane] = jnp.sum(
                    spread * GL[s, start : start + FRM, lane] * MASK[k], axis=0, keepdims=True
                )

        pump_back(s, 2)
        for j, xx in xs_:
            rcopy(MS.at[xx], MR.at[par, xx], xb_s.at[s, j], xb_r.at[s, xx], dev(xx=xx)).wait()
            rcopy(MT.at[par, xx], MT.at[par, xx], xt_s.at[s, j], xt_r.at[s, xx], dev(xx=xx)).wait()
        total = PF[...]
        for j, xx in xs_:
            total = total + MR[par, xx].astype(F32)
            packed = MT[par, xx].astype(F32)
            sum_a = sum_a + packed[:, 0:1] + packed[:, 1:2]
            sum_b = sum_b + packed[:, 2:3] + packed[:, 3:4]
        xhat = XH[x]
        TT[s, KT : KT + 1, :] = jnp.sum(total * xhat, axis=0, keepdims=True)
        gain = GAIN[par, i, 0:1, cols(x)]
        grad_in = inverse * (total * gain - sum_a * (1.0 / D) - xhat * (sum_b * (1.0 / D)))
        GC[...] = (GC[...] + grad_in).astype(BF16).astype(F32)
        pump_back(s, 3)
        return 0

    lax.fori_loop(0, SECT, backward, 0)

    for i in range(NX):
        rcopy(TT.at[2 * i + 1 - c], TS.at[i], tt_s.at[4, i], tt_r.at[4, i], sib).start()

    def tail(low, high, g):
        done = 0 if g.cc == 0 else 2
        late = {0: 5, 2: 6, 3: 7} if g.cc == 0 and NX > 1 else {}
        for e in range(low, high):
            if late.get(e, 8) < 2 * g.h2:
                g.step(2, *at(late[e]), 1)
            if done <= e < 2 * g.h2:
                g.step(2, *at(e), 0)
            if g.cc == 0:
                if NX > 2 and e < 2 * g.h1:
                    g.step(1, *at(e), 2)
                if NX > 1 and e == 3:
                    g.begin(1, 1)
                if NX > 1 and 0 <= e - 4 < 2 * g.h1:
                    g.step(1, *at(e - 4), 1)
            elif NX > 1 and 4 <= e < 2 * g.h1:
                g.step(1, *at(e), 1)
            if e == 2 * g.h2 - 1:
                g.begin(1, 0)
            if 0 <= e - 2 * g.h2 < 2 * g.h1:
                g.step(1, *at(e - 2 * g.h2), 0)

    each(scatters, functools.partial(tail, 0, 2))

    for i in range(NX):
        rcopy(TT.at[2 * i + 1 - c], TS.at[i], tt_s.at[4, i], tt_r.at[4, i], sib).wait()
    TY[...] = jnp.zeros(TY.shape, F32)
    for i in range(NX):
        summed = TT[2 * i + c] + TS[i]
        for r in range(KT + 1):
            TY[r // NZ, r % NZ, i : i + 1, :] = summed[r : r + 1]
    for j, yy in ys_:
        rcopy(TY.at[yy], TYR.at[y], tt_s.at[0, j], tt_r.at[0, y], dev(yy=yy)).start()
    TYR[y] = TY[y]
    each(scatters, functools.partial(tail, 2, 4))
    for j, yy in ys_:
        rcopy(TY.at[yy], TYR.at[yy], tt_s.at[0, j], tt_r.at[0, yy], dev(yy=yy)).wait()
    TY[y] = sum(TYR[k] for k in range(NY))
    for j, zz in zs_:
        rcopy(TY.at[y, zz], TZR.at[z], tt_s.at[1, j], tt_r.at[1, z], dev(zz=zz)).start()
    TZR[z] = TY[y, z]
    each(scatters, functools.partial(tail, 4, 6))
    for j, zz in zs_:
        rcopy(TY.at[y, zz], TZR.at[zz], tt_s.at[1, j], tt_r.at[1, zz], dev(zz=zz)).wait()
    TX[...] = sum(TZR[k] for k in range(NZ))
    for j, xx in xs_:
        rcopy(TX, TXR.at[x], tt_s.at[2, j], tt_r.at[2, x], dev(xx=xx)).start()
    TXR[x] = TX[...]
    each(scatters, functools.partial(tail, 6, 8))
    for j, xx in xs_:
        rcopy(TX, TXR.at[xx], tt_s.at[2, j], tt_r.at[2, xx], dev(xx=xx)).wait()
    TO1[z] = jnp.zeros(TO1.shape[1:], F32)
    mine = lax.broadcasted_iota(jnp.int32, (8, DX), 0) == x
    for b in range(NX):
        row = jnp.sum(jnp.where(mine, TXR[b], 0.0), axis=0, keepdims=True)
        for tile in range(lanes_x):
            k = b * lanes_x + tile
            TO1[z, k : k + 1, :] = row[:, tile * 128 : (tile + 1) * 128]
    for j, zz in zs_:
        rcopy(TO1.at[z], TO1.at[z], tt_s.at[3, j], tt_r.at[3, z], dev(zz=zz)).start()
    each(scatters, functools.partial(tail, 8, 10))
    for j, zz in zs_:
        rcopy(TO1.at[z], TO1.at[zz], tt_s.at[3, j], tt_r.at[3, zz], dev(zz=zz)).wait()
    for j, yy in ys_:
        rcopy(TO1, TO2.at[y], tt_s.at[5, j], tt_r.at[5, y], dev(yy=yy)).start()
    TO2[y] = TO1[...]
    each(scatters, functools.partial(tail, 10, 12))
    for j, xx in xs_:
        rcopy(FS.at[xx], FR.at[x], fin_s.at[j], fin_r.at[x], dev(xx=xx)).start()
    FR[x] = FS[x]
    for j, yy in ys_:
        rcopy(TO1, TO2.at[yy], tt_s.at[5, j], tt_r.at[5, yy], dev(yy=yy)).wait()
    for k in range(D // 128):
        lane = slice(k * 128, (k + 1) * 128)
        for yy in range(NY):
            low, count = yy * NZ, min(NZ, KT - yy * NZ)
            piece = TO2[yy, :, k, :]
            o_taps[0, low : low + count, lane] = piece[:count]
            if count < NZ:
                o_gain[:, lane] = piece[count : count + 1]

    for j, xx in xs_:
        rcopy(FS.at[xx], FR.at[xx], fin_s.at[j], fin_r.at[xx], dev(xx=xx)).wait()
    for b in range(NX):
        o_mix[0, :, b * DX : (b + 1) * DX] = FR[b, :, :DX].astype(F32)
        o_gate[0, :, b * DX : (b + 1) * DX] = FR[b, :, DX:].astype(F32)

    taps_out.wait_send()
    gain_out.wait_send()

    def drain(i, _):
        there = W.at[c, i]
        rcopy(there, there, sw_s.at[i], sw_r.at[i], sib).wait_send()
        rcopy(NT.at[0], NS.at[i], sn_s.at[i], sn_r.at[i], sib).wait_send()
        rcopy(GO.at[0], GS.at[i], sg_s.at[i], sg_r.at[i], sib).wait_send()
        return 0

    lax.fori_loop(0, NX, drain, 0)
    each(gathers, lambda g: g.drain())
    each(scatters, lambda g: g.drain())


def body(
    mel_tiles,
    utt_ids,
    tile_lengths,
    dest_shard,
    dest_slot,
    subsample_weight,
    mixing_weight,
    gate_weight,
    conv_taps,
    norm_gain,
    out_cot,
):
    ND = lax.axis_size("dp")
    SECT = lax.axis_size("pipe")
    NX = SECT // CORES
    NY, NZ = PHYS[ND]
    tiles, TSUB, feats = mel_tiles.shape
    D = subsample_weight.shape[1]
    KT = conv_taps.shape[1]
    R = mixing_weight.shape[1]
    FRM = tiles * TSUB // 2
    J = -(-feats // 128)
    DX = D // NX
    SR = -(-(TSUB * J + 1) // 16) * 16
    dims = dict(X=NX, Y=NY, Z=NZ, D=D, R=R, F=FRM, TSUB=TSUB, J=J, TAPS=KT)

    OR = -(-(D // 128) // 8) * 8
    NR = max(NY, NZ) // 2

    def vm(shape, kind=F32):
        return pltpu.VMEM(shape, kind)

    def sems(*shape):
        return pltpu.SemaphoreType.DMA(shape)

    scratch = [
        vm((2, NX, NY, NZ, R, 2 * DX), BF16),
        vm((2, NX, KT + 1, DX)),
        vm((2, NX, 8, D)),
        vm((KT + 1, D)),
        vm((8, D)),
        vm((tiles, TSUB, feats)),
        vm((ND, SR, 128), BF16),
        vm((NY, NZ, SR, 128), BF16),
        vm((NZ, NY, SR, 128), BF16),
        vm((ND, SR, 128)),
        vm((TSUB * ND, J * 128)),
        vm((FRM + 32, 128)),
        vm((KT, FRM, 128)),
        vm((SECT, NX, FRM, DX), BF16),
        vm((SECT, FRM, D), BF16),
        vm((NX, FRM, D), BF16),
        vm((SECT, FRM + 32, DX)),
        vm((FRM + 32, DX)),
        vm((SECT, FRM, DX)),
        vm((SECT, FRM, DX)),
        vm((SECT, FRM, DX)),
        vm((FRM, DX)),
        vm((FRM, DX), BF16),
        vm((FRM, DX)),
        vm((NX, FRM, DX)),
        vm((SECT, 2, FRM, 128)),
        vm((SECT, FRM, 2 * DX), BF16),
        vm((NX, FRM, 2 * DX), BF16),
        vm((NX, FRM, DX), BF16),
        vm((2, NX, FRM, DX), BF16),
        vm((2, NX, FRM, 128), BF16),
        vm((NX, NY, NZ, R, 2 * DX), BF16),
        vm((NX, 2, ND // 2, R, 2 * DX), BF16),
        vm((NX, 2, NR, R, 2 * DX), BF16),
        vm((NX, R, 2 * DX), BF16),
        vm((NX, R, 2 * DX), BF16),
        vm((SECT, KT + 1, DX)),
        vm((NX, KT + 1, DX)),
        vm((NY, NZ, 8, DX)),
        vm((NY, NZ, 8, DX)),
        vm((NZ, 8, DX)),
        vm((8, DX)),
        vm((NX, 8, DX)),
        vm((NZ, OR, 128)),
        vm((NY, NZ, OR, 128)),
        sems(3 + NX * NZ),
        sems(NX),
        sems(NX),
        sems(2, NX),
        sems(2, NX),
        sems(2, max(NY, NZ)),
        sems(2, max(NY, NZ)),
        sems(NX, 2, 2),
        sems(NX, 2, 2, NR),
        sems(NX, 2, 2),
        sems(NX, 2, 2, NR),
        sems(NX, 2, 2),
        sems(NX, 2, 2, NR),
        sems(NX, 2, 2),
        sems(NX, 2, 2, NR),
        sems(NX),
        sems(NX),
        sems(2),
        sems(2),
        sems(SECT, NX),
        sems(SECT, NX),
        sems(SECT, NX),
        sems(SECT, NX),
        sems(SECT, NX),
        sems(SECT, NX),
        sems(NX),
        sems(NX),
        sems(NX),
        sems(NX),
        sems(NX),
        sems(NX),
        sems(6, max(NX, NY, NZ)),
        sems(6, max(NX, NY, NZ)),
    ]
    in_vmem = pl.BlockSpec(memory_space=pltpu.VMEM)
    in_any = pl.BlockSpec(memory_space=pl.ANY)
    return pl.pallas_call(
        functools.partial(kernel, dims),
        out_shape=(
            jax.ShapeDtypeStruct((1, R, D), F32),
            jax.ShapeDtypeStruct((1, R, D), F32),
            jax.ShapeDtypeStruct((1, KT, D), F32),
            jax.ShapeDtypeStruct((1, D), F32),
        ),
        in_specs=[in_vmem] * 5 + [in_any] * 2 + [in_vmem] * 2 + [in_any] * 2,
        out_specs=(in_vmem,) * 4,
        scratch_shapes=scratch,
        compiler_params=pltpu.CompilerParams(
            collective_id=0, has_side_effects=True, vmem_limit_bytes=VMEM_LIMIT
        ),
    )(
        mel_tiles,
        utt_ids[None],
        tile_lengths[None],
        dest_shard[None],
        dest_slot[None],
        mixing_weight,
        gate_weight,
        conv_taps,
        norm_gain,
        subsample_weight,
        out_cot,
    )


def solution(mesh):
    in_specs = (
        P("dp", None, None),
        P("dp"),
        P("dp"),
        P("dp"),
        P("dp"),
        P(),
        P("pipe", "dp", None),
        P("pipe", "dp", None),
        P("pipe", None, None),
        P("pipe", None),
        P("dp", None),
    )
    out_specs = (
        P("pipe", "dp", None),
        P("pipe", "dp", None),
        P("pipe", None, None),
        P("pipe", None),
    )
    return jax.shard_map(body, mesh=mesh, in_specs=in_specs, out_specs=out_specs, check_vma=False)
```
